32 devices in a mesh: shard: 4 (over y, x), dp: 8 (over z, core).
Axes of the slice: x: 2, y: 2, z: 4, core: 2. Of those that a mesh axis runs over, the one named last changes fastest.
Arguments:
- tokens: bfloat16 [8192, 1024], P(('shard', 'dp')), may hold values from -6 to 6
- cotangent: bfloat16 [8192, 1024], P(('shard', 'dp')), may hold values from -6 to 6
- lengths: int32 [32, 4], P(('shard', 'dp')), may hold values from 0 to 256, as said below
- w_qkv: float32 [1024, 3072], P('shard'), may hold values from -0.1875 to 0.1875
- w_out: float32 [1024, 1024], P('shard'), may hold values from -0.75 to 0.75
- w_up: float32 [1024, 4096], P('shard'), may hold values from -0.1875 to 0.1875
- w_down: float32 [4096, 1024], P('shard'), may hold values from -0.09375 to 0.09375
- vectors: float32 [13, 1024], P(None, 'shard')
- m_qkv: float32 [1024, 3072], P('shard'), may hold values from -0.75 to 0.75
- m_out: float32 [1024, 1024], P('shard'), may hold values from -0.75 to 0.75
- m_up: float32 [1024, 4096], P('shard'), may hold values from -0.75 to 0.75
- m_down: float32 [4096, 1024], P('shard'), may hold values from -0.75 to 0.75
- m_vectors: float32 [13, 1024], P(None, 'shard'), may hold values from -0.75 to 0.75
- v_qkv: float32 [1024, 3072], P('shard'), may hold values from 0.002 to 0.02
- v_out: float32 [1024, 1024], P('shard'), may hold values from 0.002 to 0.02
- v_up: float32 [1024, 4096], P('shard'), may hold values from 0.002 to 0.02
- v_down: float32 [4096, 1024], P('shard'), may hold values from 0.002 to 0.02
- v_vectors: float32 [13, 1024], P(None, 'shard'), may hold values from 0.002 to 0.02
Outputs:
- output: bfloat16 [8192, 1024], P(('shard', 'dp'))
- input_grad: bfloat16 [8192, 1024], P(('shard', 'dp'))
- grad_qkv: float32 [1024, 3072], P('shard')
- grad_out: float32 [1024, 1024], P('shard')
- grad_up: float32 [1024, 4096], P('shard')
- grad_down: float32 [4096, 1024], P('shard')
- grad_vectors: float32 [13, 1024], P(None, 'shard')
- new_qkv: float32 [1024, 3072], P('shard')
- new_out: float32 [1024, 1024], P('shard')
- new_up: float32 [1024, 4096], P('shard')
- new_down: float32 [4096, 1024], P('shard')
- new_vectors: float32 [13, 1024], P(None, 'shard')
- first_qkv: float32 [1024, 3072], P('shard')
- first_out: float32 [1024, 1024], P('shard')
- first_up: float32 [1024, 4096], P('shard')
- first_down: float32 [4096, 1024], P('shard')
- first_vectors: float32 [13, 1024], P(None, 'shard')
- second_qkv: float32 [1024, 3072], P('shard')
- second_out: float32 [1024, 1024], P('shard')
- second_up: float32 [1024, 4096], P('shard')
- second_down: float32 [4096, 1024], P('shard')
- second_vectors: float32 [13, 1024], P(None, 'shard')
The draws below stay inside these ranges and needn't reach their ends.
Inputs may be any that keep to these rules, and one draw needn't show every extreme that they name: Row b lists the lengths of the sequences packed from the first slot of token block b in order, 0 for an unused slot; a row sums to at most 256, and some row holds one sequence of exactly 256 tokens.
All inputs are finite; a program needn't handle non-finite values.
Results may differ from the reference program's by a relative error of at most 0.012.
The reference program's roundings to bfloat16 on the way count: a program that leaves them out, or rounds other values in their place, can miss the bound.
Values may be sent and summed in bfloat16 or wider, within the bound.
No kernel may reach another device: no remote copies, remote signals or barrier semaphores. Data moves between devices by JAX's collectives and lax.ppermute only.
A program may use at most 320 MiB of HBM per device.

```python
import math
import jax
import jax.numpy as jnp
from jax import lax

D = 1024
H = 16
HD = 64
FF = 4096
ROT = 16
TOK_DEV = 256
SLOTS = 4
ADAM_STEP = 4
NDEV = 32
TOKENS = 8192
VROWS = 13


def draw_lengths(key, part):
    key_total = jax.random.fold_in(key, 11)
    key_cut = jax.random.fold_in(key, 12)
    key_full = jax.random.fold_in(key, 13)
    totals = jax.random.randint(key_total, (NDEV, 1), TOK_DEV // 4, TOK_DEV + 1)
    cuts = jax.random.randint(key_cut, (NDEV, SLOTS - 1), 0, totals + 1)
    cuts = jnp.sort(cuts, axis=1)
    edges = jnp.concatenate([jnp.zeros((NDEV, 1), jnp.int32), cuts.astype(jnp.int32), totals.astype(jnp.int32)], axis=1)
    counts = edges[:, 1:] - edges[:, :-1]
    full_row = jax.random.randint(key_full, (), 0, NDEV)
    single = jnp.zeros((SLOTS,), jnp.int32).at[0].set(TOK_DEV)
    rows = jnp.arange(NDEV)[:, None]
    return jnp.where(rows == full_row, single[None, :], counts).astype(jnp.int32)


def draw_vectors(key, part):
    noise = jax.random.normal(key, (VROWS, D), jnp.float32)
    rows = jnp.arange(VROWS)[:, None]
    gains = (rows == 0) | (rows == 2)
    return jnp.where(gains, 1.0 + 0.15 * noise, 0.2 * noise).astype(jnp.float32)


def block_levels(key, extent, split, least, largest):
    def one(dim, shards_of):
        steps = jax.random.uniform(jax.random.fold_in(jax.random.fold_in(key, 6), dim), (shards_of,), jnp.float32, least / len(split), largest / len(split))
        return jnp.repeat(jnp.exp(steps), extent[dim] // shards_of).reshape((-1,) + (1,) * (len(extent) - dim - 1))

    factor_of = one(*split[0])
    for cut in split[1:]:
        factor_of = factor_of * one(*cut)
    return factor_of


def gaussian(stream_key, dims, scale, limit, shards=(), kind=jnp.bfloat16):
    result = jax.random.normal(stream_key, dims, jnp.float32) * scale
    if len(shards) > 0:
        result = block_levels(stream_key, dims, shards, -0.22, 0.18) * result
    return jnp.clip(result, min=-limit, max=limit).astype(kind)


def setup_inputs(seed: int = 0) -> dict:
    key_list = jax.random.split(jax.random.key(seed), 19)
    return {
        "tokens": gaussian(key_list[0], (TOKENS, D), 1.0, 6.0, ((0, 32),)),
        "cotangent": gaussian(key_list[1], (TOKENS, D), 1.0, 6.0, ((0, 32),)),
        "lengths": draw_lengths(jax.random.fold_in(key_list[18], 71), 0),
        "w_qkv": gaussian(key_list[3], (D, 3 * D), D ** -0.5, 0.1875, ((0, 4),), jnp.float32),
        "w_out": gaussian(key_list[4], (D, D), HD ** -0.5, 0.75, ((0, 4),), jnp.float32),
        "w_up": gaussian(key_list[5], (D, FF), D ** -0.5, 0.1875, ((0, 4),), jnp.float32),
        "w_down": gaussian(key_list[6], (FF, D), FF ** -0.5, 0.09375, ((0, 4),), jnp.float32),
        "vectors": draw_vectors(jax.random.fold_in(key_list[18], 71), 0),
        "m_qkv": gaussian(key_list[8], (D, 3 * D), 0.05, 0.75, ((0, 4),), jnp.float32),
        "m_out": gaussian(key_list[9], (D, D), 0.05, 0.75, ((0, 4),), jnp.float32),
        "m_up": gaussian(key_list[10], (D, FF), 0.05, 0.75, ((0, 4),), jnp.float32),
        "m_down": gaussian(key_list[11], (FF, D), 0.05, 0.75, ((0, 4),), jnp.float32),
        "m_vectors": gaussian(key_list[12], (VROWS, D), 0.05, 0.75, ((1, 4),), jnp.float32),
        "v_qkv": jnp.clip(jnp.exp(math.log(0.02) - 2.30258502 * jax.random.uniform(key_list[13], (D, 3 * D), jnp.float32) ** block_levels(key_list[13], (D, 3 * D), ((0, 4),), -0.2, 0.2)), 0.002, 0.02),
        "v_out": jnp.clip(jnp.exp(math.log(0.02) - 2.30258502 * jax.random.uniform(key_list[14], (D, D), jnp.float32) ** block_levels(key_list[14], (D, D), ((0, 4),), -0.2, 0.2)), 0.002, 0.02),
        "v_up": jnp.clip(jnp.exp(math.log(0.02) - 2.30258502 * jax.random.uniform(key_list[15], (D, FF), jnp.float32) ** block_levels(key_list[15], (D, FF), ((0, 4),), -0.2, 0.2)), 0.002, 0.02),
        "v_down": jnp.clip(jnp.exp(math.log(0.02) - 2.30258502 * jax.random.uniform(key_list[16], (FF, D), jnp.float32) ** block_levels(key_list[16], (FF, D), ((0, 4),), -0.2, 0.2)), 0.002, 0.02),
        "v_vectors": jnp.clip(jnp.exp(math.log(0.02) - 2.30258502 * jax.random.uniform(key_list[17], (VROWS, D), jnp.float32) ** block_levels(key_list[17], (VROWS, D), ((1, 4),), -0.2, 0.2)), 0.002, 0.02),
    }


EPS_NORM = 1e-05
BETA_ONE = 0.9
BETA_TWO = 0.95
ADAM_EPS = 1e-08
LEARN_RATE = 0.01
VECTOR_RATE = 0.1
DECAY_RATE = 0.1
SQRT_HALF = 0.7071067811865476
INV_ROOT_TWO_PI = 0.3989422804014327

def matmul(left, right):
    return jnp.dot(left, right, preferred_element_type=jnp.float32)

def left_t(left, right):
    return lax.dot_general(left, right, (((0,), (0,)), ((), ())), preferred_element_type=jnp.float32)

def right_t(left, right):
    return lax.dot_general(left, right, (((1,), (1,)), ((), ())), preferred_element_type=jnp.float32)

def heads_mix(form, left, right):
    return jnp.einsum(form, left.astype(jnp.float32), right.astype(jnp.float32))

def normalize(values):
    centred = values - lax.optimization_barrier(jnp.mean(values, axis=-1, keepdims=True))
    inv_std = lax.rsqrt(lax.optimization_barrier(jnp.mean(centred * centred, axis=-1, keepdims=True)) + EPS_NORM)
    return (centred * inv_std, inv_std)

def rotary_tables(position):
    half_dims = ROT // 2
    freq = jnp.exp(-jnp.arange(half_dims, dtype=jnp.float32) * (2.0 * math.log(10000.0) / ROT))
    angles = position.astype(jnp.float32)[:, None] * freq[None, :]
    return (jnp.cos(angles)[:, None, :], jnp.sin(angles)[:, None, :])

def rotate(values, cosine, sine):
    half_dims = ROT // 2
    first = values[..., :half_dims]
    second = values[..., half_dims:ROT]
    return jnp.concatenate([first * cosine - second * sine, second * cosine + first * sine, values[..., ROT:]], axis=-1)

def unrotate(values, cosine, sine):
    half_dims = ROT // 2
    first = values[..., :half_dims]
    second = values[..., half_dims:ROT]
    return jnp.concatenate([first * cosine + second * sine, second * cosine - first * sine, values[..., ROT:]], axis=-1)

def gelu_value(values):
    return 0.5 * values * (1.0 + lax.erf(values * SQRT_HALF))

def gelu_slope(values):
    return 0.5 * (1.0 + lax.erf(values * SQRT_HALF)) + values * jnp.exp(-0.5 * values * values) * INV_ROOT_TWO_PI

def layer_pass(tokens, cotangent, counts, params):
    w_qkv, w_out, w_up, w_down, vectors = params
    rows = tokens.shape[0]
    width = tokens.shape[1]
    scale = HD ** (-0.5)
    vector_rows = vectors.astype(jnp.float32)
    index_rows = jnp.arange(rows, dtype=jnp.int32)
    ends = jnp.cumsum(counts).astype(jnp.int32)
    passed = ends[None, :] <= index_rows[:, None]
    segment = lax.optimization_barrier(jnp.sum(passed.astype(jnp.int32), axis=1)).astype(jnp.int32)
    starts = lax.optimization_barrier(jnp.sum(jnp.where(passed, counts[None, :], 0), axis=1)).astype(jnp.int32)
    position = index_rows - starts
    valid = (index_rows < ends[-1]).astype(jnp.float32)[:, None]
    allowed = (segment[:, None] == segment[None, :]) & (index_rows[None, :] <= index_rows[:, None])
    x_float = tokens.astype(jnp.float32)
    normed, inv_std = normalize(x_float)
    in_attn = (normed * vector_rows[0] + vector_rows[1]).astype(jnp.bfloat16)
    in_mlp = (normed * vector_rows[2] + vector_rows[3]).astype(jnp.bfloat16)
    qkv_bias = vector_rows[6:9].reshape(-1)
    up_bias = vector_rows[9:].reshape(-1)
    projected = matmul(in_attn, w_qkv) + qkv_bias
    cosine, sine = rotary_tables(position)
    query_b = rotate(projected[:, :width].reshape(rows, H, HD), cosine, sine).astype(jnp.bfloat16)
    key_b = rotate(projected[:, width:2 * width].reshape(rows, H, HD), cosine, sine).astype(jnp.bfloat16)
    value_b = projected[:, 2 * width:].reshape(rows, H, HD).astype(jnp.bfloat16)
    scores = heads_mix('qhd,khd->hqk', query_b, key_b) * scale
    scores = jnp.where(allowed[None], scores, -1e+30)
    top_score = lax.optimization_barrier(jnp.max(scores, axis=-1, keepdims=True))
    log_total = top_score + jnp.log(lax.optimization_barrier(jnp.sum(jnp.exp(scores - top_score), axis=-1, keepdims=True)))
    probs = jnp.exp(scores - log_total)
    probs_b = probs.astype(jnp.bfloat16)
    heads_b = heads_mix('hqk,khd->qhd', probs_b, value_b).astype(jnp.bfloat16).reshape(rows, width)
    attn = matmul(heads_b, w_out) + vector_rows[4]
    up_pre = matmul(in_mlp, w_up) + up_bias
    act_b = gelu_value(up_pre).astype(jnp.bfloat16)
    mlp = matmul(act_b, w_down) + vector_rows[5]
    output = (x_float + valid * (attn + mlp)).astype(jnp.bfloat16)
    cot_float = cotangent.astype(jnp.float32)
    branch_grad = cot_float * valid
    branch_b = branch_grad.astype(jnp.bfloat16)
    grad_out = left_t(heads_b, branch_b)
    grad_down = left_t(act_b, branch_b)
    bias_out = lax.optimization_barrier(jnp.sum(branch_grad, axis=0))
    d_heads = right_t(branch_b, w_out).astype(jnp.bfloat16).reshape(rows, H, HD)
    d_up = right_t(branch_b, w_down) * gelu_slope(up_pre)
    d_up_b = d_up.astype(jnp.bfloat16)
    grad_up = left_t(in_mlp, d_up_b)
    bias_up = lax.optimization_barrier(jnp.sum(d_up, axis=0))
    d_mlp_in = right_t(d_up_b, w_up)
    d_probs = heads_mix('qhd,khd->hqk', d_heads, value_b)
    delta = lax.optimization_barrier(jnp.sum(probs * d_probs, axis=-1, keepdims=True))
    d_scores = (probs * (d_probs - delta)).astype(jnp.bfloat16)
    d_query = heads_mix('hqk,khd->qhd', d_scores, key_b) * scale
    d_key = heads_mix('hqk,qhd->khd', d_scores, query_b) * scale
    d_value = heads_mix('hqk,qhd->khd', probs_b, d_heads)
    d_proj = jnp.concatenate([unrotate(d_query, cosine, sine).reshape(rows, width), unrotate(d_key, cosine, sine).reshape(rows, width), d_value.reshape(rows, width)], axis=1)
    bias_qkv = lax.optimization_barrier(jnp.sum(d_proj, axis=0))
    d_proj_b = d_proj.astype(jnp.bfloat16)
    grad_qkv = left_t(in_attn, d_proj_b)
    d_attn_in = right_t(d_proj_b, w_qkv)
    scaled = d_attn_in * vector_rows[0] + d_mlp_in * vector_rows[2]
    d_tokens = inv_std * (scaled - lax.optimization_barrier(jnp.mean(scaled, axis=-1, keepdims=True)) - normed * lax.optimization_barrier(jnp.mean(scaled * normed, axis=-1, keepdims=True)))
    input_grad = (cot_float + d_tokens).astype(jnp.bfloat16)
    grad_vectors = jnp.concatenate([lax.optimization_barrier(jnp.sum(d_attn_in * normed, axis=0))[None], lax.optimization_barrier(jnp.sum(d_attn_in, axis=0))[None], lax.optimization_barrier(jnp.sum(d_mlp_in * normed, axis=0))[None], lax.optimization_barrier(jnp.sum(d_mlp_in, axis=0))[None], bias_out[None], bias_out[None], bias_qkv.reshape(3, width), bias_up.reshape(-1, width)], axis=0)
    return (output, input_grad, (grad_qkv, grad_out, grad_up, grad_down, grad_vectors))

def adam_update(weight, first, second, grad, count, decay, rate):
    first_new = BETA_ONE * first + (1.0 - BETA_ONE) * grad
    second_new = BETA_TWO * second + (1.0 - BETA_TWO) * grad * grad
    corr_one = 1.0 - jnp.exp(count * math.log(BETA_ONE))
    corr_two = 1.0 - jnp.exp(count * math.log(BETA_TWO))
    step_size = first_new / corr_one / (jnp.sqrt(second_new / corr_two) + ADAM_EPS)
    return (weight - rate * (step_size + decay * weight), first_new, second_new)

def reference(tokens, cotangent, lengths, w_qkv, w_out, w_up, w_down, vectors, m_qkv, m_out, m_up, m_down, m_vectors, v_qkv, v_out, v_up, v_down, v_vectors):
    masters = (w_qkv, w_out, w_up, w_down, vectors)
    firsts = (m_qkv, m_out, m_up, m_down, m_vectors)
    seconds = (v_qkv, v_out, v_up, v_down, v_vectors)
    working = tuple((item.astype(jnp.bfloat16) for item in masters))
    blocks_in = tokens.reshape(NDEV, TOK_DEV, D)
    blocks_cot = cotangent.reshape(NDEV, TOK_DEV, D)
    zeros_init = tuple((jnp.zeros(item.shape, jnp.float32) for item in masters))

    def visit(totals, block):
        block_in, block_cot, counts = block
        out_block, grad_block, grads = layer_pass(block_in, block_cot, counts, working)
        return (tuple((left + right for left, right in zip(totals, grads))), (out_block, grad_block))
    totals, (outs, in_grads) = lax.scan(visit, zeros_init, (blocks_in, blocks_cot, lengths))
    grad_scale = float(TOKENS) ** (-0.5)
    grads = tuple((item * grad_scale for item in totals))
    count = jnp.float32(ADAM_STEP)
    decays = (DECAY_RATE, DECAY_RATE, DECAY_RATE, DECAY_RATE, 0.0)
    rates = (LEARN_RATE, LEARN_RATE, LEARN_RATE, LEARN_RATE, VECTOR_RATE)
    results = [adam_update(masters[which], firsts[which], seconds[which], grads[which], count, decays[which], rates[which]) for which in range(5)]
    new_w = tuple((item[0] for item in results))
    new_m = tuple((item[1] for item in results))
    new_v = tuple((item[2] for item in results))
    output = outs.reshape(TOKENS, D)
    input_grad = in_grads.reshape(TOKENS, D)
    return (output, input_grad, grads[0], grads[1], grads[2], grads[3], grads[4], new_w[0], new_w[1], new_w[2], new_w[3], new_w[4], new_m[0], new_m[1], new_m[2], new_m[3], new_m[4], new_v[0], new_v[1], new_v[2], new_v[3], new_v[4])
```

```python
import math

import jax
import jax.numpy as jnp
from jax import lax
from jax.sharding import PartitionSpec as P

H = 16
HD = 64
ROT = 16
ADAM_STEP = 4


EPS_NORM = 1e-05
BETA_ONE = 0.9
BETA_TWO = 0.95
ADAM_EPS = 1e-08
LEARN_RATE = 0.01
VECTOR_RATE = 0.1
DECAY_RATE = 0.1
SQRT_HALF = 0.7071067811865476
INV_ROOT_TWO_PI = 0.3989422804014327

BF = jnp.bfloat16
F32 = jnp.float32
EXTRA = 16


def matmul(left, right):
    return jnp.dot(left, right, preferred_element_type=F32)


def left_t(left, right):
    return lax.dot_general(left, right, (((0,), (0,)), ((), ())), preferred_element_type=F32)


def right_t(left, right):
    return lax.dot_general(left, right, (((1,), (1,)), ((), ())), preferred_element_type=F32)


def heads_mix(form, left, right):
    return jnp.einsum(form, left, right, preferred_element_type=F32)


def normalize(values):
    centred = values - jnp.mean(values, axis=-1, keepdims=True)
    inv_std = lax.rsqrt(jnp.mean(centred * centred, axis=-1, keepdims=True) + EPS_NORM)
    return (centred * inv_std, inv_std)


def rotate(values, cosine, sine):
    half_dims = ROT // 2
    first = values[..., :half_dims]
    second = values[..., half_dims:ROT]
    return jnp.concatenate(
        [first * cosine - second * sine, second * cosine + first * sine, values[..., ROT:]], axis=-1
    )


def gelu_parts(values):
    gate = 0.5 * (1.0 + lax.erf(values * SQRT_HALF))
    slope = gate + values * jnp.exp(-0.5 * values * values) * INV_ROOT_TWO_PI
    return values * gate, slope


def adam_update(weight, first, second, grad, decay, rate):
    count = jnp.float32(ADAM_STEP)
    first_new = BETA_ONE * first + (1.0 - BETA_ONE) * grad
    second_new = BETA_TWO * second + (1.0 - BETA_TWO) * grad * grad
    corr_one = 1.0 - jnp.exp(count * math.log(BETA_ONE))
    corr_two = 1.0 - jnp.exp(count * math.log(BETA_TWO))
    step_size = first_new / corr_one / (jnp.sqrt(second_new / corr_two) + ADAM_EPS)
    return (weight - rate * (step_size + decay * weight), first_new, second_new)


def shard_swap(value, step):
    size = lax.axis_size("shard")
    return lax.ppermute(value, "shard", [(i, i ^ step) for i in range(size)])


def core_swap(value):
    size = lax.axis_size("dp")
    return lax.ppermute(value, "dp", [(i, i ^ 1) for i in range(size)])


def chain_sum(value):
    places = lax.axis_size("dp") // 2
    if places == 1:
        return value
    place = lax.axis_index("dp") // 2
    half = places // 2

    def send(item, pairs):
        return lax.ppermute(
            item, "dp", [(2 * a + core, 2 * b + core) for a, b in pairs for core in range(2)]
        )

    total = value
    for step in range(half - 1):
        got = send(total, [(step, step + 1), (places - 1 - step, places - 2 - step)])
        total = total + got
    total = total + send(total, [(half - 1, half), (half, half - 1)])
    for step in reversed(range(half - 1)):
        got = send(total, [(step + 1, step), (places - 2 - step, places - 1 - step)])
        mine = (place == step) | (place == places - 1 - step)
        total = jnp.where(mine, got, total)
    return total


def local(
    tokens, cotangent, lengths,
    w_qkv, w_out, w_up, w_down, vectors,
    m_qkv, m_out, m_up, m_down, m_vectors,
    v_qkv, v_out, v_up, v_down, v_vectors,
):
    groups = lax.axis_size("shard")
    me = lax.axis_index("shard")
    core = lax.axis_index("dp") % 2
    rows, width = tokens.shape
    hidden = w_up.shape[1]
    wide = width // groups
    half = wide // 2
    ff = hidden // groups
    heads = H // groups
    n_vec = vectors.shape[0]
    others = range(1, groups)

    def piece(matrix, parts, owner, first, count):
        block = lax.dynamic_slice_in_dim(matrix, first, count, 0)
        block = block.reshape(count, parts, groups, -1)
        block = lax.dynamic_slice_in_dim(block, owner, 1, 2)
        return block.reshape(count, -1).astype(BF)

    small = jnp.concatenate(
        [vectors.astype(BF), jnp.pad(lengths.astype(BF), ((0, 0), (0, wide - lengths.shape[1])))]
    )
    small = jnp.pad(small, ((0, EXTRA - n_vec - 1), (0, 3 * wide + ff - wide)))

    def payload(step):
        owner = me ^ step
        both = jnp.concatenate(
            [piece(w_qkv, 3, owner, core * half, half), piece(w_up, 1, owner, core * half, half)], axis=1
        )
        return jnp.concatenate([both, small])

    got_w = [shard_swap(payload(step), step) for step in others]
    got_x = [tokens] + [shard_swap(tokens, step) for step in others]
    got_c = [cotangent] + [shard_swap(cotangent, step) for step in others]
    stacked = jnp.stack([item[:half] for item in got_w])
    other_half = core_swap(stacked)
    own_rows = jnp.concatenate([piece(w_qkv, 3, me, 0, wide), piece(w_up, 1, me, 0, wide)], axis=1)
    full = jnp.zeros((groups, 2, half, 3 * wide + ff), BF)
    full = lax.dynamic_update_slice(full, own_rows.reshape(1, 2, half, -1), (me, 0, 0, 0))
    for step in others:
        at = me ^ step
        full = lax.dynamic_update_slice(full, stacked[step - 1][None, None], (at, core, 0, 0))
        full = lax.dynamic_update_slice(full, other_half[step - 1][None, None], (at, 1 - core, 0, 0))
    full = full.reshape(width, 3 * wide + ff)
    qkv_w = full[:, : 3 * wide]
    up_w = full[:, 3 * wide :]
    out_w = w_out.astype(BF)
    down_w = w_down.astype(BF)

    smalls = [small[:, :wide]] + [item[half:, :wide] for item in got_w]
    vec = jnp.zeros((n_vec, groups, wide), BF)
    counts = []
    for step in range(groups):
        vec = lax.dynamic_update_slice(vec, smalls[step][:n_vec, None], (0, me ^ step, 0))
        counts.append(smalls[step][n_vec, : lengths.shape[1]].astype(jnp.int32))
    vec = vec.reshape(n_vec, width).astype(F32)
    counts = jnp.stack(counts)

    index_rows = jnp.arange(rows, dtype=jnp.int32)
    ends = jnp.cumsum(counts, axis=1)
    passed = ends[:, None, :] <= index_rows[None, :, None]
    segment = jnp.sum(passed.astype(jnp.int32), axis=2)
    starts = jnp.sum(jnp.where(passed, counts[:, None, :], 0), axis=2)
    position = index_rows[None] - starts
    valid = (index_rows[None] < ends[:, -1:]).astype(F32)
    allowed = (segment[:, :, None] == segment[:, None, :]) & (
        index_rows[None, None, :] <= index_rows[None, :, None]
    )

    x_all = jnp.concatenate(got_x).astype(F32)
    normed, inv_std = normalize(x_all)
    in_attn = (normed * vec[0] + vec[1]).astype(BF)
    in_mlp = (normed * vec[2] + vec[3]).astype(BF)
    cot_all = jnp.concatenate(got_c).astype(F32)
    branch_b = (cot_all * valid.reshape(-1, 1)).astype(BF)

    qkv_bias = lax.dynamic_slice_in_dim(vec[6:9].reshape(3, groups, wide), me, 1, 1).reshape(-1)
    up_bias = lax.dynamic_slice_in_dim(vec[9:].reshape(-1), me * ff, ff)

    up_pre = matmul(in_mlp, up_w) + up_bias
    act, slope = gelu_parts(up_pre)
    act_b = act.astype(BF)
    d_up = right_t(branch_b, down_w) * slope
    d_up_b = d_up.astype(BF)
    token_total = rows * groups * lax.axis_size("dp")
    grad_scale = float(token_total) ** (-0.5)
    grad_down = (left_t(act_b, branch_b) * grad_scale).astype(BF)
    grad_up = (left_t(in_mlp, d_up_b) * grad_scale).astype(BF)
    bias_up = jnp.sum(d_up, axis=0)
    d_mlp_in = right_t(d_up_b, up_w)
    mlp = matmul(act_b, down_w)

    scale = HD ** (-0.5)
    projected = (matmul(in_attn, qkv_w) + qkv_bias).reshape(groups, rows, 3, heads, HD)
    half_dims = ROT // 2
    freq = jnp.exp(-jnp.arange(half_dims, dtype=F32) * (2.0 * math.log(10000.0) / ROT))
    angles = position.astype(F32)[:, :, None, None] * freq
    cosine, sine = jnp.cos(angles), jnp.sin(angles)
    query_b = rotate(projected[:, :, 0], cosine, sine).astype(BF)
    key_b = rotate(projected[:, :, 1], cosine, sine).astype(BF)
    value_b = projected[:, :, 2].astype(BF)
    scores = heads_mix("bqhd,bkhd->bhqk", query_b, key_b) * scale
    scores = jnp.where(allowed[:, None], scores, -1e30)
    top_score = jnp.max(scores, axis=-1, keepdims=True)
    log_total = top_score + jnp.log(jnp.sum(jnp.exp(scores - top_score), axis=-1, keepdims=True))
    probs = jnp.exp(scores - log_total)
    probs_b = probs.astype(BF)
    heads_b = heads_mix("bhqk,bkhd->bqhd", probs_b, value_b).astype(BF).reshape(groups * rows, wide)
    attn = matmul(heads_b, out_w)
    grad_out = (left_t(heads_b, branch_b) * grad_scale).astype(BF)
    d_heads = right_t(branch_b, out_w).astype(BF).reshape(groups, rows, heads, HD)
    d_probs = heads_mix("bqhd,bkhd->bhqk", d_heads, value_b)
    delta = jnp.sum(probs * d_probs, axis=-1, keepdims=True)
    d_scores = (probs * (d_probs - delta)).astype(BF)
    d_query = heads_mix("bhqk,bkhd->bqhd", d_scores, key_b) * scale
    d_key = heads_mix("bhqk,bqhd->bkhd", d_scores, query_b) * scale
    d_value = heads_mix("bhqk,bqhd->bkhd", probs_b, d_heads)
    d_proj = jnp.stack([rotate(d_query, cosine, -sine), rotate(d_key, cosine, -sine), d_value], axis=2)
    d_proj = d_proj.reshape(groups * rows, 3 * wide)
    bias_qkv = jnp.sum(d_proj, axis=0)
    d_proj_b = d_proj.astype(BF)
    grad_qkv = (left_t(in_attn, d_proj_b) * grad_scale).astype(BF)
    d_attn_in = right_t(d_proj_b, qkv_w)

    branch_out = attn + mlp
    scaled = d_attn_in * vec[0] + d_mlp_in * vec[2]

    def owners_sum(value):
        value = value.reshape(groups, rows, width)
        total = value[0]
        for step in others:
            total = total + shard_swap(value[step].astype(BF), step).astype(F32)
        return total

    branch_sum = owners_sum(branch_out) + vec[4] + vec[5]
    output = (tokens.astype(F32) + valid[0][:, None] * branch_sum).astype(BF)
    scaled_sum = owners_sum(scaled)
    own_normed, own_inv = normed[:rows], inv_std[:rows]
    d_tokens = own_inv * (
        scaled_sum
        - jnp.mean(scaled_sum, axis=-1, keepdims=True)
        - own_normed * jnp.mean(scaled_sum * own_normed, axis=-1, keepdims=True)
    )
    cot_float = cotangent.astype(F32)
    input_grad = (cot_float + d_tokens).astype(BF)

    bias_out = jnp.sum(cot_float * valid[0][:, None], axis=0)
    row_qkv = lax.dynamic_update_slice(
        jnp.zeros((3, groups, wide), F32), bias_qkv.reshape(3, 1, wide), (0, me, 0)
    ).reshape(3, width)
    row_up = lax.dynamic_update_slice(jnp.zeros((hidden,), F32), bias_up, (me * ff,)).reshape(-1, width)
    vec_grad = jnp.concatenate(
        [
            jnp.sum(d_attn_in * normed, axis=0)[None],
            jnp.sum(d_attn_in, axis=0)[None],
            jnp.sum(d_mlp_in * normed, axis=0)[None],
            jnp.sum(d_mlp_in, axis=0)[None],
            bias_out[None],
            bias_out[None],
            row_qkv,
            row_up,
        ]
    )
    vec_grad = jnp.pad((vec_grad * grad_scale).astype(BF), ((0, EXTRA - n_vec), (0, 0)))
    vec_grad = vec_grad.reshape(2, EXTRA // 2, groups, wide).transpose(2, 0, 1, 3)
    vec_grad = jnp.pad(vec_grad, ((0, 0), (0, 0), (0, EXTRA // 2), (0, 2 * wide)))

    def core_sum(value, axis):
        keep = lax.dynamic_index_in_dim(value, core, axis, keepdims=False)
        away = lax.dynamic_index_in_dim(value, 1 - core, axis, keepdims=False)
        return keep + core_swap(away)

    def core_join(value, axis):
        other = core_swap(value)
        return jnp.where(
            core == 0, jnp.stack([value, other], axis=axis), jnp.stack([other, value], axis=axis)
        )

    def to_owners(value):
        pieces = [lax.dynamic_index_in_dim(value, me, 0, keepdims=False)]
        for step in others:
            pieces.append(
                shard_swap(lax.dynamic_index_in_dim(value, me ^ step, 0, keepdims=False), step)
            )
        return jnp.stack(pieces)

    def natural(value):
        result = jnp.zeros(value.shape, value.dtype)
        for step in range(groups):
            result = lax.dynamic_update_slice_in_dim(result, value[step : step + 1], me ^ step, 0)
        return result

    sum_down = core_join(chain_sum(core_sum(grad_down.reshape(2, ff // 2, width), 0)), 0)
    sum_up = to_owners(core_sum(grad_up.reshape(groups, 2, half, ff), 1))
    sum_up = core_join(chain_sum(sum_up), 1)
    sum_out = core_join(chain_sum(core_sum(grad_out.reshape(2, half, width), 0)), 0)
    grad_qkv = jnp.concatenate([grad_qkv.reshape(groups, 2, half, 3 * wide), vec_grad], axis=2)
    sum_qkv = to_owners(core_sum(grad_qkv, 1))
    sum_qkv = core_join(chain_sum(sum_qkv), 1)
    sum_vec = jnp.sum(sum_qkv[:, :, half : half + EXTRA // 2, :wide].astype(F32), axis=0)
    sum_vec = sum_vec.reshape(EXTRA, wide)[:n_vec]

    full_grads = (
        natural(sum_qkv[:, :, :half])
        .reshape(groups, wide, 3, wide)
        .transpose(1, 2, 0, 3)
        .reshape(wide, 3 * width)
        .astype(F32),
        sum_out.reshape(wide, width).astype(F32),
        natural(sum_up).reshape(groups, wide, ff).transpose(1, 0, 2).reshape(wide, hidden).astype(F32),
        sum_down.reshape(ff, width).astype(F32),
        sum_vec,
    )
    masters = (w_qkv, w_out, w_up, w_down, vectors)
    firsts = (m_qkv, m_out, m_up, m_down, m_vectors)
    seconds = (v_qkv, v_out, v_up, v_down, v_vectors)
    decays = (DECAY_RATE, DECAY_RATE, DECAY_RATE, DECAY_RATE, 0.0)
    rates = (LEARN_RATE, LEARN_RATE, LEARN_RATE, LEARN_RATE, VECTOR_RATE)
    results = [
        adam_update(masters[i], firsts[i], seconds[i], full_grads[i], decays[i], rates[i]) for i in range(5)
    ]
    return (
        (output, input_grad)
        + full_grads
        + tuple(r[0] for r in results)
        + tuple(r[1] for r in results)
        + tuple(r[2] for r in results)
    )


def solution(mesh):
    by_token = P(("shard", "dp"), None)
    params = (P("shard", None),) * 4 + (P(None, "shard"),)
    return jax.shard_map(
        local,
        mesh=mesh,
        in_specs=(by_token,) * 3 + params * 3,
        out_specs=(by_token,) * 2 + params * 4,
        check_vma=False,
    )
```

```python
import functools
import math

import jax
import jax.numpy as jnp
from jax import lax
from jax.experimental import pallas as pl
from jax.experimental.pallas import tpu as pltpu
from jax.sharding import PartitionSpec as P

H = 16
HD = 64
ROT = 16
ADAM_STEP = 4


EPS_NORM = 1e-05
BETA_ONE = 0.9
BETA_TWO = 0.95
ADAM_EPS = 1e-08
LEARN_RATE = 0.01
VECTOR_RATE = 0.1
DECAY_RATE = 0.1
SQRT_HALF = 0.7071067811865476
INV_ROOT_TWO_PI = 0.3989422804014327

BF = jnp.bfloat16
F32 = jnp.float32
EXTRA = 16
LANES = 128
MIB = 2**20


def dot(left, right):
    return jnp.dot(left, right, preferred_element_type=F32)


def dot_lt(left, right):
    return lax.dot_general(left, right, (((0,), (0,)), ((), ())), preferred_element_type=F32)


def dot_rt(left, right):
    return lax.dot_general(left, right, (((1,), (1,)), ((), ())), preferred_element_type=F32)


def part(start, size, multiple=None):
    return pl.ds(pl.multiple_of(start, multiple or size), size)


def shard_swap(value, step):
    size = lax.axis_size("shard")
    return lax.ppermute(value, "shard", [(i, i ^ step) for i in range(size)])


def core_swap(value):
    size = lax.axis_size("dp")
    return lax.ppermute(value, "dp", [(i, i ^ 1) for i in range(size)])


def chain_stages():
    places = lax.axis_size("dp") // 2
    half = places // 2
    if places == 1:
        return []
    stages = []
    for step in range(half - 1):
        stages.append(([(step, step + 1), (places - 1 - step, places - 2 - step)], None))
    stages.append(([(half - 1, half), (half, half - 1)], None))
    for step in reversed(range(half - 1)):
        stages.append(
            ([(step + 1, step), (places - 2 - step, places - 1 - step)], (step, places - 1 - step))
        )
    return stages


def place_send(value, pairs):
    return lax.ppermute(
        value, "dp", [(2 * a + core, 2 * b + core) for a, b in pairs for core in range(2)]
    )


def after(value, *earlier):
    return lax.optimization_barrier((value, earlier))[0]


def combine(items):
    def body(flag_ref, *refs):
        count = len(items)
        for i, (_, _, taker) in enumerate(items):
            value, got, out = refs[2 * i], refs[2 * i + 1], refs[2 * count + i]
            if taker is None:
                out[...] = value[...] + got[...]
            else:
                out[...] = jnp.where(flag_ref[i] > 0, got[...], value[...])

    flags = [jnp.int32(0) if taker is None else taker.astype(jnp.int32) for _, _, taker in items]
    vmem = pl.BlockSpec(memory_space=pltpu.VMEM)
    return pl.pallas_call(
        body,
        out_shape=[jax.ShapeDtypeStruct(value.shape, value.dtype) for value, _, _ in items],
        in_specs=[pl.BlockSpec(memory_space=pltpu.SMEM)] + [vmem] * (2 * len(items)),
        out_specs=[vmem] * len(items),
        compiler_params=pltpu.CompilerParams(vmem_limit_bytes=12 * MIB),
        cost_estimate=pl.CostEstimate(flops=0, bytes_accessed=int(3.2e6), transcendentals=0),
    )(jnp.stack(flags), *[item for value, got, _ in items for item in (value, got)])


def advance(*moves):
    values = [value for value, _ in moves]
    depth = max(len(stages) for _, stages in moves)
    for step in range(depth):
        active = [i for i, (_, stages) in enumerate(moves) if step < len(stages)]
        items = []
        for i in active:
            pairs, takers = moves[i][1][step]
            flag = None
            if takers is not None:
                place = lax.axis_index("dp") // 2
                flag = functools.reduce(jnp.logical_or, [place == taker for taker in takers])
            items.append((values[i], place_send(values[i], pairs), flag))
        for i, item in zip(active, combine(items), strict=True):
            values[i] = item
    return values


def chain_parts():
    stages = chain_stages()
    half = (len(stages) + 1) // 2
    if not stages:
        return [], [], []
    return stages[: half - 1], stages[half - 1 : half], stages[half:]


def gather_rest(block, near):
    groups = lax.axis_size("shard")
    rows = block.shape[0]
    got = [[block], [near[0]], [near[1]]]
    got.append([shard_swap(near[0][: rows // 2], 2), shard_swap(near[1][rows // 2 :], 1)])
    for step in range(4, groups):
        got.append([shard_swap(block, step)])
    return got


def whole():
    return pl.BlockSpec(memory_space=pltpu.VMEM)


def full(shape):
    return pl.BlockSpec(memory_space=pltpu.VMEM)


def block_of(shape):
    return pl.BlockSpec(shape, lambda *_: (0,) * len(shape))


def by_row(shape):
    return pl.BlockSpec(shape, lambda i, *_: (i,) + (0,) * (len(shape) - 1))


def kernel_call(body, grid, in_specs, outs, scratch=(), time=1.0, limit=20):
    return pl.pallas_call(
        body,
        out_shape=[jax.ShapeDtypeStruct(shape, dtype) for shape, dtype, _ in outs],
        grid_spec=pltpu.PrefetchScalarGridSpec(
            num_scalar_prefetch=1,
            grid=grid,
            in_specs=in_specs,
            out_specs=[spec for _, _, spec in outs],
            scratch_shapes=list(scratch),
        ),
        compiler_params=pltpu.CompilerParams(vmem_limit_bytes=limit * MIB),
        cost_estimate=pl.CostEstimate(flops=0, bytes_accessed=int(3.2e6 * time), transcendentals=0),
    )


def flat(blocks):
    return [piece for block in blocks for piece in block]


def load_block(block, blocks, refs, scratch):
    at = 0
    for step, pieces in enumerate(blocks):
        mine = refs[at : at + len(pieces)]
        at += len(pieces)

        @pl.when(block == step)
        def _(mine=mine):
            row = 0
            for ref in mine:
                scratch[row : row + ref.shape[0], :] = ref[...]
                row += ref.shape[0]


def halves(value, core):
    size = value.shape[0] // 2
    first, second = value[:size], value[size:]
    return jnp.where(core == 0, first, second), jnp.where(core == 0, second, first)


def ends_of(lens_ref, block, slots):
    lengths = [lens_ref[block, 0:1, k : k + 1] for k in range(slots)]
    ends = []
    for item in lengths:
        ends.append(item if not ends else ends[-1] + item)
    return lengths, ends


def segments(index, ends):
    total = jnp.zeros(index.shape, F32)
    for end in ends:
        total = total + jnp.where(jnp.broadcast_to(end, index.shape) <= index, 1.0, 0.0)
    return total


def index_of(shape, axis):
    return lax.broadcasted_iota(jnp.int32, shape, axis).astype(F32)


def gelu_parts(values):
    gate = 0.5 * (1.0 + lax.erf(values * SQRT_HALF))
    slope = gate + values * jnp.exp(-0.5 * values * values) * INV_ROOT_TWO_PI
    return values * gate, slope


def adam_terms(weight, first, second, grad, decay, rate):
    corr_one = 1.0 - math.exp(ADAM_STEP * math.log(BETA_ONE))
    corr_two = 1.0 - math.exp(ADAM_STEP * math.log(BETA_TWO))
    first_new = BETA_ONE * first + (1.0 - BETA_ONE) * grad
    second_new = BETA_TWO * second + (1.0 - BETA_TWO) * grad * grad
    step_size = (first_new * (1.0 / corr_one)) / (jnp.sqrt(second_new * (1.0 / corr_two)) + ADAM_EPS)
    return weight - rate * (step_size + decay * weight), first_new, second_new


def pack(groups, sc, w_up, w_qkv, w_down, w_out, vectors, lengths):
    wide, hidden = w_up.shape
    half, ff = wide // 2, hidden // groups
    n_vec, slots = vectors.shape[0], lengths.shape[1]

    def body(s_ref, up_hbm, qkv_hbm, down_hbm, out_hbm, vec_ref, len_ref, *refs):
        out, (down_out, out_out) = refs[: 2 * groups], refs[2 * groups : 2 * groups + 2]
        up_scr, qkv_scr, down_scr, out_scr, sems, more = refs[2 * groups + 2 :]
        me, core = s_ref[0], s_ref[1]
        rest = [
            pltpu.make_async_copy(down_hbm, down_scr, more.at[0]),
            pltpu.make_async_copy(out_hbm, out_scr, more.at[1]),
        ]
        copies = []
        for step in range(groups):
            size = wide if step == 0 else half
            rows = pl.ds(0, wide) if step == 0 else part(core * half, half)
            owner = me ^ step
            at = pl.ds(0 if step == 0 else wide + (step - 1) * half, size)
            mine = [pltpu.make_async_copy(up_hbm.at[rows, part(owner * ff, ff)], up_scr.at[at], sems.at[step, 0])]
            for p in range(3):
                mine.append(
                    pltpu.make_async_copy(
                        qkv_hbm.at[rows, part(p * groups * wide + owner * wide, wide)],
                        qkv_scr.at[at, pl.ds(p * wide, wide)],
                        sems.at[step, 1 + p],
                    )
                )
            copies.append(mine)
        order = list(range(1, groups)) + [0]
        for step in order:
            for copy in copies[step]:
                copy.start()
        for copy in rest:
            copy.start()
        for step in order:
            for copy in copies[step]:
                copy.wait()
            up_out, qkv_out = out[2 * step], out[2 * step + 1]
            if step == 0:
                up_out[...] = up_scr[:wide].astype(BF)
                qkv_out[...] = qkv_scr[:wide].astype(BF)
                continue
            at = wide + (step - 1) * half
            up_out[:half, :] = up_scr[at : at + half].astype(BF)
            up_out[half:, :] = jnp.zeros((EXTRA, ff), BF)
            up_out[half : half + n_vec, :wide] = vec_ref[...].astype(BF)
            up_out[half + n_vec : half + n_vec + 1, :slots] = len_ref[...].astype(F32).astype(BF)
            qkv_out[...] = qkv_scr[at : at + half].astype(BF)
        for copy in rest:
            copy.wait()
        down_out[...] = down_scr[...].astype(BF)
        out_out[...] = out_scr[...].astype(BF)

    in_specs = [pl.BlockSpec(memory_space=pltpu.HBM)] * 4 + [full(vectors.shape), full(lengths.shape)]
    outs = []
    for step in range(groups):
        size = wide if step == 0 else half
        extra = 0 if step == 0 else EXTRA
        outs.append(((size + extra, ff), BF, full(None)))
        outs.append(((size, 3 * wide), BF, full(None)))
    outs += [(w_down.shape, BF, full(None)), (w_out.shape, BF, full(None))]
    rows = wide + (groups - 1) * half
    scratch = [pltpu.VMEM((rows, ff), F32), pltpu.VMEM((rows, 3 * wide), F32)]
    scratch += [pltpu.VMEM(w_down.shape, F32), pltpu.VMEM(w_out.shape, F32)]
    scratch += [pltpu.SemaphoreType.DMA((groups, 4)), pltpu.SemaphoreType.DMA((2,))]
    got = kernel_call(body, (1,), in_specs, outs, scratch, 7.0, 60)(sc, w_up, w_qkv, w_down, w_out, vectors, lengths)
    return got[0 : 2 * groups : 2], got[1 : 2 * groups : 2], got[2 * groups], got[2 * groups + 1]


def tables(sc, lens, groups, rows, slots):
    def body(s_ref, lens_ref, cos_ref, sin_ref):
        block = pl.program_id(0)
        lengths, ends = ends_of(lens_ref, block, slots)
        index = index_of((rows, LANES), 0)
        start = jnp.zeros((rows, LANES), F32)
        for length, end in zip(lengths, ends, strict=True):
            start = start + jnp.where(jnp.broadcast_to(end, index.shape) <= index, length, 0.0)
        lane = lax.broadcasted_iota(jnp.int32, (rows, LANES), 1) % HD
        pair = (lane % (ROT // 2)).astype(F32)
        freq = jnp.where(lane < ROT, jnp.exp(-pair * (2.0 * math.log(10000.0) / ROT)), 0.0)
        angle = (index - start) * freq
        cos_ref[...] = jnp.cos(angle)
        sin_ref[...] = jnp.sin(angle)

    out = ((groups * rows, LANES), F32, by_row((rows, LANES)))
    return kernel_call(body, (groups,), [full(lens.shape)], [out, out], (), 3.0)(sc, lens)


def forward_up(sc, xs, own, mine, other, vectors, lengths):
    groups, n_x = len(xs), len(flat(xs))
    rows, width = xs[0][0].shape
    wide, ff = own.shape
    half = wide // 2
    n_vec, slots = vectors.shape[0], lengths.shape[1]
    tok = groups * rows

    def body(s_ref, *refs):
        x_refs, refs = refs[:n_x], refs[n_x:]
        own_ref = refs[0]
        mine_refs = refs[1:groups]
        other_refs = refs[groups : 2 * groups - 1]
        vec_in, len_in = refs[2 * groups - 1 : 2 * groups + 1]
        attn_ref, mlp_ref, act_ref, slope_ref, stats_ref, w_ref, vec_ref, lens_ref, x_scr = refs[2 * groups + 1 :]
        me, core = s_ref[0], s_ref[1]
        block = pl.program_id(0)

        @pl.when(block == 0)
        def _():
            w_ref[part(me * wide, wide), :] = own_ref[...]
            vec_ref[...] = jnp.zeros_like(vec_ref)
            lens_ref[...] = jnp.zeros_like(lens_ref)
            vec_ref[0:n_vec, part(me * wide, wide)] = vec_in[...].astype(BF).astype(F32)
            lens_ref[0, 0:1, 0:slots] = len_in[...].astype(F32)
            for step in range(1, groups):
                at = (me ^ step) * wide
                w_ref[part(at + core * half, half), :] = mine_refs[step - 1][:half, :]
                w_ref[part(at + (1 - core) * half, half), :] = other_refs[step - 1][:half, :]
                vec_ref[0:n_vec, part(at, wide)] = mine_refs[step - 1][half : half + n_vec, :wide].astype(F32)
                lens_ref[step, 0:1, 0:slots] = mine_refs[step - 1][
                    half + n_vec : half + n_vec + 1, :slots
                ].astype(F32)

        load_block(block, xs, x_refs, x_scr)
        x = x_scr[...].astype(F32)
        mean = jnp.mean(x, axis=1, keepdims=True)
        centred = x - mean
        inv = lax.rsqrt(jnp.mean(centred * centred, axis=1, keepdims=True) + EPS_NORM)
        normed = centred * inv
        lane = lax.broadcasted_iota(jnp.int32, (rows, LANES), 1)
        stats_ref[...] = jnp.where(lane == 0, mean, inv)
        attn_ref[...] = (normed * vec_ref[0:1, :] + vec_ref[1:2, :]).astype(BF)
        in_mlp = (normed * vec_ref[2:3, :] + vec_ref[3:4, :]).astype(BF)
        mlp_ref[...] = in_mlp
        first = me * ff
        bias = vec_ref[pl.ds(9 + first // width, 1), part(lax.rem(me, width // ff) * ff, ff, LANES)]
        act, slope = gelu_parts(dot(in_mlp, w_ref[...]) + bias)
        act_ref[...] = act.astype(BF)
        slope_ref[...] = slope

    piece = (half + EXTRA, ff)
    in_specs = (
        [full(item.shape) for item in flat(xs)]
        + [full(own.shape)]
        + [full(piece)] * (2 * (groups - 1))
        + [full(vectors.shape), full(lengths.shape)]
    )
    outs = [
        ((tok, width), BF, by_row((rows, width))),
        ((tok, width), BF, by_row((rows, width))),
        ((tok, ff), BF, by_row((rows, ff))),
        ((tok, ff), F32, by_row((rows, ff))),
        ((tok, LANES), F32, by_row((rows, LANES))),
        ((width, ff), BF, full((width, ff))),
        ((EXTRA, width), F32, full((EXTRA, width))),
        ((groups, 8, LANES), F32, full((groups, 8, LANES))),
    ]
    return kernel_call(
        body, (groups,), in_specs, outs, [pltpu.VMEM((rows, width), BF)], 6.5
    )(sc, *flat(xs), own, *mine, *other, vectors, lengths)


def grad_of_down(sc, cots, lens, act, slots, scale):
    groups, n_c = len(cots), len(flat(cots))
    rows, width = cots[0][0].shape
    ff = act.shape[1]

    def body(s_ref, *refs):
        cot_refs = iter(refs[:n_c])
        lens_ref, act_ref, branch_ref, bias_ref, away_ref, keep_ref = refs[n_c:]
        core = s_ref[1]
        for step, pieces in enumerate(cots):
            _, ends = ends_of(lens_ref, step, slots)
            row = 0
            for piece in pieces:
                size = piece.shape[0]
                index = index_of((size, 1), 0) + float(row)
                valid = jnp.where(index < jnp.broadcast_to(ends[-1], (size, 1)), 1.0, 0.0)
                branch = next(cot_refs)[...].astype(F32) * valid
                at = step * rows + row
                branch_ref[at : at + size, :] = branch.astype(BF)
                row += size
                if step == 0:
                    bias_ref[...] = jnp.broadcast_to(jnp.sum(branch, axis=0, keepdims=True), bias_ref.shape)
        size = ff // 2
        for ref, which in ((away_ref, 1 - core), (keep_ref, core)):
            ref[...] = (dot_lt(act_ref[:, part(which * size, size)], branch_ref[...]) * scale).astype(BF)

    outs = [
        ((groups * rows, width), BF, full((groups * rows, width))),
        ((8, width), F32, full((8, width))),
        ((ff // 2, width), BF, full((ff // 2, width))),
        ((ff // 2, width), BF, full((ff // 2, width))),
    ]
    return kernel_call(
        body,
        (1,),
        [full(item.shape) for item in flat(cots) + [lens, act]],
        outs,
        (),
        3.5,
    )(sc, *flat(cots), lens, act)


def backward_up(sc, branch, slope, w_down, in_mlp, scale, groups):
    tok, width = branch.shape
    rows = tok // groups
    ff = slope.shape[1]
    half = width // groups // 2

    def body(s_ref, branch_ref, slope_ref, wd_ref, mlp_ref, away_ref, keep_ref, up_ref, bias_ref):
        me, core = s_ref[0], s_ref[1]
        block = pl.program_id(0)

        @pl.when(block == 0)
        def _():
            bias_ref[...] = jnp.zeros_like(bias_ref)

        d_up = dot_rt(branch_ref[...], wd_ref[...]) * slope_ref[...]
        bias_ref[0:1, :] += jnp.sum(d_up, axis=0, keepdims=True)
        up_ref[part(block * rows, rows), :] = d_up.astype(BF)

        @pl.when(block == groups - 1)
        def _():
            def piece(i, carry):
                grad = (dot_lt(mlp_ref[:, part((me ^ i) * (2 * half), 2 * half)], up_ref[...]) * scale).astype(BF)
                keep_ref[i], away_ref[i] = halves(grad, core)
                return carry

            lax.fori_loop(0, groups, piece, 0)

    in_specs = [by_row((rows, width)), by_row((rows, ff)), full(w_down.shape), full(in_mlp.shape)]
    outs = [
        ((groups, half, ff), BF, full((groups, half, ff))),
        ((groups, half, ff), BF, full((groups, half, ff))),
        ((tok, ff), BF, full((tok, ff))),
        ((8, ff), F32, full((8, ff))),
    ]
    return kernel_call(body, (groups,), in_specs, outs, (), 6.8)(
        sc, branch, slope, w_down, in_mlp
    )


def attention(sc, in_attn, branch, cosine, sine, lens, vec, own, mine, other, w_out, groups, slots):
    tok, width = in_attn.shape
    rows = tok // groups
    wide = width // groups
    half = wide // 2
    scale = HD ** (-0.5)

    def body(s_ref, *refs):
        a_ref, branch_ref, cos_ref, sin_ref, lens_ref, vec_ref = refs[:6]
        own_ref = refs[6]
        mine_refs = refs[7 : 6 + groups]
        other_refs = refs[6 + groups : 5 + 2 * groups]
        wo_ref, heads_ref, proj_ref, bias_ref, w_ref = refs[5 + 2 * groups :]
        me, core = s_ref[0], s_ref[1]
        block = pl.program_id(0)

        @pl.when(block == 0)
        def _():
            w_ref[part(me * wide, wide), :] = own_ref[...]
            for step in range(1, groups):
                at = (me ^ step) * wide
                w_ref[part(at + core * half, half), :] = mine_refs[step - 1][...]
                w_ref[part(at + (1 - core) * half, half), :] = other_refs[step - 1][...]
            bias_ref[...] = jnp.zeros_like(bias_ref)

        bias = [vec_ref[6 + p : 7 + p, part(me * wide, wide)] for p in range(3)]
        projected = dot(a_ref[...], w_ref[...])
        d_heads = dot_rt(branch_ref[...], wo_ref[...]).astype(BF)
        _, ends = ends_of(lens_ref, block, slots)
        key_index = index_of((rows, 1), 0)
        query_index = index_of((1, rows), 1)
        allowed = (segments(key_index, ends) == segments(query_index, ends)) & (key_index <= query_index)
        lane = lax.broadcasted_iota(jnp.int32, (rows, LANES), 1)
        cosine, sine = cos_ref[...], sin_ref[...]
        low = jnp.where(lane % HD < ROT // 2, sine, 0.0)
        high = jnp.where(lane % HD >= ROT // 2, sine, 0.0)

        def turn(values, sign):
            ahead = pltpu.roll(values, LANES - ROT // 2, 1)
            behind = pltpu.roll(values, ROT // 2, 1)
            return values * cosine + sign * (behind * high - ahead * low)

        first_half = lane < HD
        for pair in range(wide // LANES):
            lo, hi = pair * LANES, (pair + 1) * LANES
            query = turn(projected[:, lo:hi] + bias[0][:, lo:hi], 1.0).astype(BF)
            key = turn(projected[:, wide + lo : wide + hi] + bias[1][:, lo:hi], 1.0).astype(BF)
            value = (projected[:, 2 * wide + lo : 2 * wide + hi] + bias[2][:, lo:hi]).astype(BF)
            d_out = d_heads[:, lo:hi]
            key_t, value_t = key.T, value.T
            heads_t, query_t, d_keys, d_values = [], [], [], []
            for head in range(2):
                mask = first_half if head == 0 else ~first_half
                only_key = jnp.where(mask, key, jnp.zeros_like(key))
                only_value = jnp.where(mask, value, jnp.zeros_like(value))
                scores = jnp.where(allowed, dot_rt(only_key, query) * scale, -1e30)
                top = jnp.max(scores, axis=0, keepdims=True)
                weights = jnp.exp(scores - top)
                probs = weights * (1.0 / jnp.sum(weights, axis=0, keepdims=True))
                probs_b = probs.astype(BF)
                d_probs = dot_rt(only_value, d_out)
                delta = jnp.sum(probs * d_probs, axis=0, keepdims=True)
                d_scores = (probs * (d_probs - delta)).astype(BF)
                heads_t.append(dot(value_t[head * HD : (head + 1) * HD], probs_b))
                query_t.append(dot(key_t[head * HD : (head + 1) * HD], d_scores))
                d_keys.append(dot(d_scores, query))
                d_values.append(dot(probs_b, d_out))
            heads_ref[:, lo:hi] = jnp.concatenate(heads_t, axis=0).T.astype(BF)
            d_query = turn(jnp.concatenate(query_t, axis=0).T * scale, -1.0)
            d_key = turn(jnp.where(first_half, d_keys[0], d_keys[1]) * scale, -1.0)
            d_value = jnp.where(first_half, d_values[0], d_values[1])
            for p, item in enumerate((d_query, d_key, d_value)):
                proj_ref[:, p * wide + lo : p * wide + hi] = item.astype(BF)
                bias_ref[0:1, p * wide + lo : p * wide + hi] += jnp.sum(item, axis=0, keepdims=True)

    in_specs = (
        [by_row((rows, width)), by_row((rows, width)), by_row((rows, LANES)), by_row((rows, LANES))]
        + [full(lens.shape), full(vec.shape)]
        + [full((half, 3 * wide))] * (1 + 2 * (groups - 1))
        + [full(w_out.shape)]
    )
    outs = [
        ((tok, wide), BF, by_row((rows, wide))),
        ((tok, 3 * wide), BF, by_row((rows, 3 * wide))),
        ((8, 3 * wide), F32, full((8, 3 * wide))),
        ((width, 3 * wide), BF, full((width, 3 * wide))),
    ]
    return kernel_call(body, (groups,), in_specs, outs, (), 11.3)(
        sc, in_attn, branch, cosine, sine, lens, vec, own, *mine, *other, w_out
    )


def back_to_tokens(sc, xs, heads, act, d_proj, d_up, stats, vec, w_out, w_down, w_qkv, w_up, bias_up, bias_qkv, bias_out):
    groups, n_x = len(xs), len(flat(xs))
    rows, width = xs[0][0].shape
    wide = width // groups
    ff = act.shape[1]

    def body(s_ref, *refs):
        x_refs, refs = refs[:n_x], refs[n_x:]
        (
            heads_ref, act_ref, proj_ref, d_up_ref, stats_ref, vec_ref, wo_ref, wd_ref, wq_ref, wu_ref,
            up_ref, qkv_ref, out_ref,
        ) = refs[:13]
        own_ref = refs[13]
        piece_refs = refs[14 : 13 + groups]
        grad_ref, x_scr = refs[13 + groups :]
        me = s_ref[0]
        block = pl.program_id(0)
        load_block(block, xs, x_refs, x_scr)

        @pl.when(block == 0)
        def _():
            grad_ref[...] = jnp.zeros_like(grad_ref)
            grad_ref[4:6, :] = out_ref[0:2, :]
            for p in range(3):
                grad_ref[6 + p : 7 + p, part(me * wide, wide)] = qkv_ref[0:1, p * wide : (p + 1) * wide]
            first = me * ff
            grad_ref[pl.ds(9 + first // width, 1), part(lax.rem(me, width // ff) * ff, ff, LANES)] = up_ref[0:1, :]

        normed = (x_scr[...].astype(F32) - stats_ref[:, 0:1]) * stats_ref[:, 1:2]
        branch_out = dot(heads_ref[...], wo_ref[...]) + dot(act_ref[...], wd_ref[...])
        total = None
        for row, left, right in ((0, proj_ref, wq_ref), (2, d_up_ref, wu_ref)):
            d_in = dot_rt(left[...], right[...])
            grad_ref[row : row + 1, :] += jnp.sum(d_in * normed, axis=0, keepdims=True)
            grad_ref[row + 1 : row + 2, :] += jnp.sum(d_in, axis=0, keepdims=True)
            term = d_in * vec_ref[row : row + 1, :]
            total = term if total is None else total + term

        @pl.when(block == 0)
        def _():
            own_ref[:, :width] = branch_out
            own_ref[:, width:] = total

        for step in range(1, groups):

            @pl.when(block == step)
            def _(step=step):
                piece_refs[step - 1][:, :width] = branch_out.astype(BF)
                piece_refs[step - 1][:, width:] = total.astype(BF)

    constant = [vec, w_out, w_down, w_qkv, w_up, bias_up, bias_qkv, bias_out]
    in_specs = (
        [block_of(item.shape) for item in flat(xs)]
        + [by_row((rows, item.shape[1])) for item in (heads, act, d_proj, d_up, stats)]
        + [block_of(item.shape) for item in constant]
    )
    outs = [((rows, 2 * width), F32, full((rows, 2 * width)))]
    outs += [((rows, 2 * width), BF, full((rows, 2 * width)))] * (groups - 1)
    outs += [((EXTRA, width), F32, full((EXTRA, width)))]
    got = kernel_call(
        body,
        (groups,),
        in_specs,
        outs,
        [pltpu.VMEM((rows, width), BF)],
        9.4,
        58,
    )(sc, *flat(xs), heads, act, d_proj, d_up, stats, *constant)
    return got[0], got[1:groups], got[groups]


def grads_of_attention(sc, in_attn, d_proj, heads, branch, scale, groups):
    tok, width = in_attn.shape
    wide = heads.shape[1]
    half = wide // 2

    def body(s_ref, a_ref, proj_ref, heads_ref, branch_ref, out_away, out_keep, qkv_away, qkv_keep):
        me, core = s_ref[0], s_ref[1]

        def piece(i, carry):
            grad = (dot_lt(a_ref[:, part((me ^ i) * wide, wide)], proj_ref[...]) * scale).astype(BF)
            qkv_keep[i], qkv_away[i] = halves(grad, core)
            return carry

        lax.fori_loop(0, groups, piece, 0)
        grad = (dot_lt(heads_ref[...], branch_ref[...]) * scale).astype(BF)
        out_keep[...], out_away[...] = halves(grad, core)

    ops = (in_attn, d_proj, heads, branch)
    out = ((half, width), BF, full((half, width)))
    qkv = ((groups, half, 3 * wide), BF, full((groups, half, 3 * wide)))
    return kernel_call(
        body, (1,), [full(item.shape) for item in ops], [out, out, qkv, qkv], (), 4.0
    )(sc, *ops)


def finish(sc, own, got, tokens, cotangent, lens, stats, vec, slots):
    rows, width = tokens.shape

    def body(s_ref, own_ref, *refs):
        got_refs = refs[: len(got)]
        tok_ref, cot_ref, lens_ref, stats_ref, vec_ref, out_ref, grad_ref = refs[len(got) :]
        branch = own_ref[:, :width]
        scaled = own_ref[:, width:]
        for ref in got_refs:
            branch = branch + ref[:, :width].astype(F32)
            scaled = scaled + ref[:, width:].astype(F32)
        size = branch.shape[0]
        _, ends = ends_of(lens_ref, 0, slots)
        index = index_of((size, 1), 0) + (pl.program_id(0) * size).astype(F32)
        valid = jnp.where(index < jnp.broadcast_to(ends[-1], (size, 1)), 1.0, 0.0)
        x = tok_ref[...].astype(F32)
        out_ref[...] = (x + valid * (branch + vec_ref[4:5, :] + vec_ref[5:6, :])).astype(BF)
        inv = stats_ref[:, 1:2]
        normed = (x - stats_ref[:, 0:1]) * inv
        d_tokens = inv * (
            scaled
            - jnp.mean(scaled, axis=1, keepdims=True)
            - normed * jnp.mean(scaled * normed, axis=1, keepdims=True)
        )
        grad_ref[...] = (cot_ref[...].astype(F32) + d_tokens).astype(BF)

    size = rows // 2
    in_specs = [by_row((size, 2 * width))] * (1 + len(got)) + [by_row((size, width))] * 2
    in_specs += [full(lens.shape), by_row((size, LANES)), full(vec.shape)]
    out = ((rows, width), BF, by_row((size, width)))
    return kernel_call(body, (2,), in_specs, [out, out], (), 2.4)(
        sc, own, *got, tokens, cotangent, lens, stats, vec
    )


def assemble(shape, arrays, plan):
    def body(*refs):
        ins, out = refs[: len(arrays)], refs[len(arrays)]
        me, core = lax.axis_index("shard"), lax.rem(lax.axis_index("dp"), 2)
        for which, index, row, column, size in plan(me, core):
            out[part(row, size[0]), part(column, size[1])] = ins[which][index]

    return pl.pallas_call(
        body,
        out_shape=jax.ShapeDtypeStruct(shape, arrays[0].dtype),
        in_specs=[pl.BlockSpec(memory_space=pltpu.VMEM)] * len(arrays),
        out_specs=pl.BlockSpec(memory_space=pltpu.VMEM),
        compiler_params=pltpu.CompilerParams(vmem_limit_bytes=20 * MIB),
        cost_estimate=pl.CostEstimate(flops=0, bytes_accessed=0, transcendentals=0),
    )(*arrays)


def adam(masters, grad, decay=DECAY_RATE, rate=LEARN_RATE):
    weight, first, second = masters
    grad = grad.astype(F32)
    return (grad,) + adam_terms(weight, first, second, grad, decay, rate)


def local(
    tokens, cotangent, lengths,
    w_qkv, w_out, w_up, w_down, vectors,
    m_qkv, m_out, m_up, m_down, m_vectors,
    v_qkv, v_out, v_up, v_down, v_vectors,
):
    groups = lax.axis_size("shard")
    me = lax.axis_index("shard")
    core = lax.axis_index("dp") % 2
    rows, width = tokens.shape
    hidden = w_up.shape[1]
    wide = width // groups
    half = wide // 2
    ff = hidden // groups
    n_vec = vectors.shape[0]
    slots = lengths.shape[1]
    others = range(1, groups)
    sc = jnp.stack([me, core]).astype(jnp.int32)
    scale = float(rows * groups * lax.axis_size("dp")) ** (-0.5)

    size = ff // 2
    inward, across, outward = chain_parts()
    fence = lax.optimization_barrier

    up_parts, qkv_parts, down_w, out_w = pack(groups, sc, w_up, w_qkv, w_down, w_out, vectors, lengths)
    near = [shard_swap(tokens, step) for step in (1, 2)]
    near, up_parts = fence((near, up_parts))
    up_mine = [shard_swap(item, step) for item, step in zip(up_parts[1:], others, strict=True)]
    xs = gather_rest(tokens, near)
    cot_near = [shard_swap(after(cotangent, near), step) for step in (1, 2)]
    up_other = [core_swap(item) for item in up_mine]
    in_attn, in_mlp, act, slope, stats, up_w, vec, lens = forward_up(
        sc, xs, up_parts[0], up_mine, up_other, vectors, lengths
    )
    cot_near, act = fence((cot_near, act))
    cots = gather_rest(cotangent, cot_near)
    qkv_mine = [shard_swap(item, step) for item, step in zip(after(qkv_parts[1:], cot_near), others, strict=True)]
    cosine, sine = tables(sc, after(lens, cot_near), groups, rows, slots)
    cots, cosine = fence((cots, cosine))

    branch, bias_out, down_away, down_keep = grad_of_down(sc, cots, lens, act, slots, scale)
    down_got = core_swap(down_away)
    up_away, up_keep, d_up, bias_up = backward_up(sc, branch, slope, down_w, in_mlp, scale, groups)
    down_got, d_up, up_away, qkv_mine = fence((down_got, d_up, up_away, qkv_mine))
    down = down_keep + down_got
    up_got = core_swap(up_away)
    qkv_other = [core_swap(item) for item in qkv_mine]
    down, up_got, qkv_other, branch_a = fence((down, up_got, qkv_other, branch))
    up_sums = [up_keep[i] + up_got[i] for i in range(groups)]
    up_sums, down, branch_a = fence((up_sums, down, branch_a))

    [down] = advance((down, inward))
    up_rows = [up_sums[0]] + [shard_swap(up_sums[step], step) for step in others]
    heads, d_proj, bias_qkv, qkv_w = attention(
        sc, in_attn, branch_a, cosine, sine, lens, vec, qkv_parts[0], qkv_mine, qkv_other, out_w, groups, slots
    )
    out_away, out_keep, qkv_away, qkv_keep = grads_of_attention(sc, in_attn, d_proj, heads, branch, scale, groups)
    down, up_rows, qkv_away, out_away = fence((down, up_rows, qkv_away, out_away))
    qkv_got = core_swap(qkv_away)
    up = jnp.stack(up_rows)
    qkv_got, up, down = fence((qkv_got, up, down))
    qkv_sums = [qkv_keep[i] + qkv_got[i] for i in range(groups)]
    qkv_sums, up, down, d_proj = fence((qkv_sums, up, down, d_proj))

    down, up = advance((down, across), (up, inward))
    qkv_rows = [qkv_sums[0]] + [shard_swap(qkv_sums[step], step) for step in others]
    own, pieces, vec_grad = back_to_tokens(
        sc, xs, heads, act, d_proj, d_up, stats, vec, out_w, down_w, qkv_w, up_w, bias_up, bias_qkv, bias_out
    )
    down, up, qkv_rows, vec_grad, pieces = fence((down, up, qkv_rows, vec_grad, pieces))
    qkv = jnp.stack(qkv_rows)
    vec_grad = (vec_grad * scale).reshape(EXTRA, groups, wide)
    vec_parts = [lax.dynamic_index_in_dim(vec_grad, me ^ step, 1, keepdims=False) for step in range(groups)]
    down, up, qkv, vec_parts, pieces = fence((down, up, qkv, vec_parts, pieces))

    down, up, qkv = advance((down, outward), (up, across), (qkv, inward))
    vec_rows = [vec_parts[0]] + [shard_swap(vec_parts[step], step) for step in others]
    got = [shard_swap(pieces[0], 1)]
    down, up, qkv, vec_rows, got, pieces = fence((down, up, qkv, vec_rows, got, pieces))
    vec_sum = jnp.pad(sum(vec_rows).astype(BF), ((0, 0), (0, width - wide)))
    out_away, out_keep = (jnp.concatenate([item, vec_sum]) for item in (out_away, out_keep))
    out_got = core_swap(out_away)
    down_other = core_swap(down)
    out_got, down_other, up, qkv, pieces = fence((out_got, down_other, up, qkv, pieces))
    out = out_keep + out_got
    out, down_other, up, qkv, pieces = fence((out, down_other, up, qkv, pieces))

    up, qkv, out = advance((up, outward), (qkv, across), (out, inward))
    got.append(shard_swap(pieces[1], 2))
    down_grad = assemble(
        (ff, width),
        [down, down_other],
        lambda me, core: [(side, slice(None), (core ^ side) * size, 0, (size, width)) for side in range(2)],
    )
    new_down = adam((w_down, m_down, v_down), down_grad)
    up, qkv, out, new_down, got, pieces = fence((up, qkv, out, new_down, got, pieces))
    up_other = core_swap(up)
    up_other, qkv, out, pieces = fence((up_other, qkv, out, pieces))

    qkv, out = advance((qkv, outward), (out, across))
    got += [shard_swap(item, step) for item, step in zip(pieces[2:], others[2:], strict=True)]
    up_grad = assemble(
        (wide, hidden),
        [up, up_other],
        lambda me, core: [
            (side, step, (core ^ side) * half, (me ^ step) * ff, (half, ff))
            for side in range(2)
            for step in range(groups)
        ],
    )
    new_up = adam((w_up, m_up, v_up), up_grad)
    qkv, out, new_up, got = fence((qkv, out, new_up, got))
    qkv_other = core_swap(qkv)
    qkv_other, out = fence((qkv_other, out))

    [out] = advance((out, outward))
    qkv_grad = assemble(
        (wide, 3 * width),
        [qkv, qkv_other],
        lambda me, core: [
            (
                side,
                (step, slice(None), slice(p * wide, (p + 1) * wide)),
                (core ^ side) * half,
                p * width + (me ^ step) * wide,
                (half, wide),
            )
            for side in range(2)
            for step in range(groups)
            for p in range(3)
        ],
    )
    new_qkv = adam((w_qkv, m_qkv, v_qkv), qkv_grad)
    output, input_grad = finish(sc, own, got, tokens, cotangent, lens, stats, vec, slots)
    out, new_qkv, output, input_grad = fence((out, new_qkv, output, input_grad))
    out_other = core_swap(out)
    out_grad = jnp.where(
        (jnp.arange(2) == core)[:, None, None], out[None, :half], out_other[None, :half]
    ).reshape(wide, width)
    vec_total = out[half : half + n_vec, :wide]

    news = (
        new_qkv,
        adam((w_out, m_out, v_out), out_grad),
        new_up,
        new_down,
        adam((vectors, m_vectors, v_vectors), vec_total, 0.0, VECTOR_RATE),
    )
    return (output, input_grad) + tuple(item[kind] for kind in range(4) for item in news)


def solution(mesh):
    by_token = P(("shard", "dp"), None)
    params = (P("shard", None),) * 4 + (P(None, "shard"),)
    return jax.shard_map(
        local,
        mesh=mesh,
        in_specs=(by_token,) * 3 + params * 3,
        out_specs=(by_token,) * 2 + params * 4,
        check_vma=False,
    )
```

```python
import functools
import math

import jax
import jax.numpy as jnp
from jax import lax
from jax.experimental import pallas as pl
from jax.experimental.pallas import tpu as pltpu
from jax.sharding import PartitionSpec as P

H = 16
HD = 64
ROT = 16
ADAM_STEP = 4


EPS_NORM = 1e-05
BETA_ONE = 0.9
BETA_TWO = 0.95
ADAM_EPS = 1e-08
LEARN_RATE = 0.01
VECTOR_RATE = 0.1
DECAY_RATE = 0.1
SQRT_HALF = 0.7071067811865476
INV_ROOT_TWO_PI = 0.3989422804014327

BF = jnp.bfloat16
F32 = jnp.float32
EXTRA = 16
LANES = 128
MIB = 2**20


def dot(left, right):
    return jnp.dot(left, right, preferred_element_type=F32)


def dot_lt(left, right):
    return lax.dot_general(left, right, (((0,), (0,)), ((), ())), preferred_element_type=F32)


def dot_rt(left, right):
    return lax.dot_general(left, right, (((1,), (1,)), ((), ())), preferred_element_type=F32)


def part(start, size, multiple=None):
    return pl.ds(pl.multiple_of(start, multiple or size), size)


def shard_swap(value, step):
    size = lax.axis_size("shard")
    return lax.ppermute(value, "shard", [(i, i ^ step) for i in range(size)])


def exchange(stay, away):
    size = lax.axis_size("shard")
    rows = stay.shape[0] // (size // 2)
    got = shard_swap(away, 1)
    pieces = [(got if step % 2 else stay)[step // 2 * rows : (step // 2 + 1) * rows] for step in range(size)]
    bit = 2
    while bit < size:
        sent = [step for step in range(size) if step & bit]
        got = shard_swap(jnp.concatenate([pieces[step] for step in sent]), bit)
        for i, step in enumerate(sent):
            pieces[step] = got[i * rows : (i + 1) * rows]
        bit *= 2
    return pieces


def core_swap(value):
    size = lax.axis_size("dp")
    return lax.ppermute(value, "dp", [(i, i ^ 1) for i in range(size)])


def chain_stages():
    places = lax.axis_size("dp") // 2
    half = places // 2
    if places == 1:
        return []
    stages = []
    for step in range(half - 1):
        stages.append(([(step, step + 1), (places - 1 - step, places - 2 - step)], None))
    stages.append(([(half - 1, half), (half, half - 1)], None))
    for step in reversed(range(half - 1)):
        stages.append(
            ([(step + 1, step), (places - 2 - step, places - 1 - step)], (step, places - 1 - step))
        )
    return stages


def place_send(value, pairs):
    return lax.ppermute(
        value, "dp", [(2 * a + core, 2 * b + core) for a, b in pairs for core in range(2)]
    )


def after(value, *earlier):
    return lax.optimization_barrier((value, earlier))[0]


def combine(items):
    def body(flag_ref, *refs):
        count = len(items)
        for i, (_, _, taker) in enumerate(items):
            value, got, out = refs[2 * i], refs[2 * i + 1], refs[2 * count + i]
            if taker is None:
                out[...] = value[...] + got[...]
            else:
                out[...] = jnp.where(flag_ref[i] > 0, got[...], value[...])

    flags = [jnp.int32(0) if taker is None else taker.astype(jnp.int32) for _, _, taker in items]
    vmem = pl.BlockSpec(memory_space=pltpu.VMEM)
    return pl.pallas_call(
        body,
        out_shape=[jax.ShapeDtypeStruct(value.shape, value.dtype) for value, _, _ in items],
        in_specs=[pl.BlockSpec(memory_space=pltpu.SMEM)] + [vmem] * (2 * len(items)),
        out_specs=[vmem] * len(items),
        compiler_params=pltpu.CompilerParams(vmem_limit_bytes=12 * MIB),
        cost_estimate=pl.CostEstimate(flops=0, bytes_accessed=int(3.2e6), transcendentals=0),
    )(jnp.stack(flags), *[item for value, got, _ in items for item in (value, got)])


def advance(*moves):
    values = [value for value, _ in moves]
    depth = max(len(stages) for _, stages in moves)
    for step in range(depth):
        active = [i for i, (_, stages) in enumerate(moves) if step < len(stages)]
        items = []
        for i in active:
            pairs, takers = moves[i][1][step]
            flag = None
            if takers is not None:
                place = lax.axis_index("dp") // 2
                flag = functools.reduce(jnp.logical_or, [place == taker for taker in takers])
            items.append((values[i], place_send(values[i], pairs), flag))
        for i, item in zip(active, combine(items), strict=True):
            values[i] = item
    return values


def chain_parts():
    stages = chain_stages()
    half = (len(stages) + 1) // 2
    if not stages:
        return [], [], []
    return stages[: half - 1], stages[half - 1 : half], stages[half:]


def dp_round(sc, fresh, inner, total, upcoming=None, rows=None):
    parts = chain_parts()
    if lax.axis_size("dp") // 2 != 4:
        moves = [(value, stages) for value, stages in zip((fresh, inner, total), parts, strict=True) if value is not None]
        moved = iter(advance(*moves))
        return [None if value is None else next(moved) for value in (fresh, inner, total)]
    if fresh is None:
        sent, pairs = total, [(1, 0), (2, 3)]
    elif total is None:
        sent, pairs = fresh, [(0, 1), (3, 2)]
    else:
        sent, pairs = total, [(0, 1), (1, 0), (2, 3), (3, 2)]
    edge = place_send(sent, pairs)
    centre = None if inner is None else place_send(inner, [(1, 2), (2, 1)])
    arrays, shapes, steps = [], [], []

    def plan(kind, items, shape):
        steps.append((kind, len(arrays), len(shapes)))
        arrays.extend(items)
        shapes.append(shape)

    if fresh is not None:
        plan("sum", [fresh, edge], fresh)
    if inner is not None and upcoming is None:
        plan("sum", [inner, centre], inner)
    if inner is not None and upcoming is not None:
        plan("next", [inner, centre, upcoming], max(inner, upcoming, key=lambda item: item.shape[0]))
    if total is not None:
        shape = total if rows is None else jax.ShapeDtypeStruct((rows, total.shape[1]), total.dtype)
        plan("last", [total, edge], shape)

    def body(s_ref, *refs):
        outs = refs[len(arrays) :]
        for kind, at, place in steps:
            value, got, out = refs[at], refs[at + 1], outs[place]
            size = min(value.shape[0], out.shape[0])
            if kind == "sum":
                out[...] = value[...] + got[:size, :]
                continue

            @pl.when(s_ref[2] == 0)
            def _(kind=kind, value=value, got=got, out=out, size=size):
                out[:size, :] = value[:size, :] + got[:size, :] if kind == "next" else value[:size, :]

            @pl.when(s_ref[2] > 0)
            def _(kind=kind, got=got, out=out, at=at, size=size):
                if kind == "next":
                    out[: refs[at + 2].shape[0], :] = refs[at + 2][...]
                else:
                    out[...] = got[:size, :]

    moved = iter(on_vmem(body, shapes, sc, arrays))
    return [None if value is None else next(moved) for value in (fresh, inner, total)]


def on_vmem(body, shapes, sc, arrays, limit=8):
    vmem = pl.BlockSpec(memory_space=pltpu.VMEM)
    return pl.pallas_call(
        body,
        out_shape=[jax.ShapeDtypeStruct(item.shape, item.dtype) for item in shapes],
        in_specs=[pl.BlockSpec(memory_space=pltpu.SMEM)] + [vmem] * len(arrays),
        out_specs=[vmem] * len(shapes),
        compiler_params=pltpu.CompilerParams(vmem_limit_bytes=limit * MIB),
        cost_estimate=pl.CostEstimate(flops=0, bytes_accessed=int(3.2e6), transcendentals=0),
    )(sc, *arrays)


def gather_rest(block, near):
    groups = lax.axis_size("shard")
    rows = block.shape[0]
    got = [[block], [near[0]], [near[1]]]
    got.append([shard_swap(near[0][: rows // 2], 2), shard_swap(near[1][rows // 2 :], 1)])
    for step in range(4, groups):
        got.append([shard_swap(block, step)])
    return got


def whole():
    return pl.BlockSpec(memory_space=pltpu.VMEM)


def full(shape):
    return pl.BlockSpec(memory_space=pltpu.VMEM)


def by_row(shape):
    return pl.BlockSpec(shape, lambda i, *_: (i,) + (0,) * (len(shape) - 1))


def kernel_call(body, grid, in_specs, outs, scratch=(), time=1.0, limit=12):
    return pl.pallas_call(
        body,
        out_shape=[jax.ShapeDtypeStruct(shape, dtype) for shape, dtype, _ in outs],
        grid_spec=pltpu.PrefetchScalarGridSpec(
            num_scalar_prefetch=1,
            grid=grid,
            in_specs=in_specs,
            out_specs=[spec for _, _, spec in outs],
            scratch_shapes=list(scratch),
        ),
        compiler_params=pltpu.CompilerParams(vmem_limit_bytes=limit * MIB),
        cost_estimate=pl.CostEstimate(flops=0, bytes_accessed=int(3.2e6 * time), transcendentals=0),
    )


def flat(blocks):
    return [piece for block in blocks for piece in block]


def load_block(block, blocks, refs, scratch):
    at = 0
    for step, pieces in enumerate(blocks):
        mine = refs[at : at + len(pieces)]
        at += len(pieces)

        @pl.when(block == step)
        def _(mine=mine):
            row = 0
            for ref in mine:
                scratch[row : row + ref.shape[0], :] = ref[...]
                row += ref.shape[0]


def halves(value, core):
    size = value.shape[0] // 2
    first, second = value[:size], value[size:]
    return jnp.where(core == 0, first, second), jnp.where(core == 0, second, first)


def ends_of(lens_ref, block, slots):
    lengths = [lens_ref[block, 0:1, k : k + 1] for k in range(slots)]
    ends = []
    for item in lengths:
        ends.append(item if not ends else ends[-1] + item)
    return lengths, ends


def segments(index, ends):
    total = jnp.zeros(index.shape, F32)
    for end in ends:
        total = total + jnp.where(jnp.broadcast_to(end, index.shape) <= index, 1.0, 0.0)
    return total


def index_of(shape, axis):
    return lax.broadcasted_iota(jnp.int32, shape, axis).astype(F32)


def gelu_parts(values):
    gate = 0.5 * (1.0 + lax.erf(values * SQRT_HALF))
    slope = gate + values * jnp.exp(-0.5 * values * values) * INV_ROOT_TWO_PI
    return values * gate, slope


def adam_terms(weight, first, second, grad, decay, rate):
    corr_one = 1.0 - math.exp(ADAM_STEP * math.log(BETA_ONE))
    corr_two = 1.0 - math.exp(ADAM_STEP * math.log(BETA_TWO))
    first_new = BETA_ONE * first + (1.0 - BETA_ONE) * grad
    second_new = BETA_TWO * second + (1.0 - BETA_TWO) * grad * grad
    step_size = (first_new * (1.0 / corr_one)) / (jnp.sqrt(second_new * (1.0 / corr_two)) + ADAM_EPS)
    return weight - rate * (step_size + decay * weight), first_new, second_new


def pack(groups, sc, w_up, w_qkv, w_down, w_out, vectors, lengths):
    wide, hidden = w_up.shape
    half, ff = wide // 2, hidden // groups
    n_vec, slots = vectors.shape[0], lengths.shape[1]

    def body(s_ref, up_hbm, qkv_hbm, down_hbm, out_hbm, vec_ref, len_ref, *refs):
        out, (down_out, out_out) = refs[: 2 * groups], refs[2 * groups : 2 * groups + 2]
        up_scr, qkv_scr, down_scr, out_scr, sems, more = refs[2 * groups + 2 :]
        me, core = s_ref[0], s_ref[1]
        rest = [
            pltpu.make_async_copy(down_hbm, down_scr, more.at[0]),
            pltpu.make_async_copy(out_hbm, out_scr, more.at[1]),
        ]
        copies = []
        for step in range(groups):
            size = wide if step == 0 else half
            rows = pl.ds(0, wide) if step == 0 else part(core * half, half)
            owner = me ^ step
            at = pl.ds(0 if step == 0 else wide + (step - 1) * half, size)
            mine = [pltpu.make_async_copy(up_hbm.at[rows, part(owner * ff, ff)], up_scr.at[at], sems.at[step, 0])]
            for p in range(3):
                mine.append(
                    pltpu.make_async_copy(
                        qkv_hbm.at[rows, part(p * groups * wide + owner * wide, wide)],
                        qkv_scr.at[at, pl.ds(p * wide, wide)],
                        sems.at[step, 1 + p],
                    )
                )
            copies.append(mine)
        order = list(range(1, groups)) + [0]
        for step in order:
            for copy in copies[step]:
                copy.start()
        for copy in rest:
            copy.start()
        for step in order:
            for copy in copies[step]:
                copy.wait()
            up_out, qkv_out = out[2 * step], out[2 * step + 1]
            if step == 0:
                up_out[...] = up_scr[:wide].astype(BF)
                qkv_out[...] = qkv_scr[:wide].astype(BF)
                continue
            at = wide + (step - 1) * half
            up_out[:half, :] = up_scr[at : at + half].astype(BF)
            up_out[half:, :] = jnp.zeros((EXTRA, ff), BF)
            up_out[half : half + n_vec, :wide] = vec_ref[...].astype(BF)
            up_out[half + n_vec : half + n_vec + 1, :slots] = len_ref[...].astype(F32).astype(BF)
            qkv_out[...] = qkv_scr[at : at + half].astype(BF)
        for copy in rest:
            copy.wait()
        down_out[...] = down_scr[...].astype(BF)
        out_out[...] = out_scr[...].astype(BF)

    in_specs = [pl.BlockSpec(memory_space=pltpu.HBM)] * 4 + [full(vectors.shape), full(lengths.shape)]
    outs = []
    for step in range(groups):
        size = wide if step == 0 else half
        extra = 0 if step == 0 else EXTRA
        outs.append(((size + extra, ff), BF, full(None)))
        outs.append(((size, 3 * wide), BF, full(None)))
    outs += [(w_down.shape, BF, full(None)), (w_out.shape, BF, full(None))]
    rows = wide + (groups - 1) * half
    scratch = [pltpu.VMEM((rows, ff), F32), pltpu.VMEM((rows, 3 * wide), F32)]
    scratch += [pltpu.VMEM(w_down.shape, F32), pltpu.VMEM(w_out.shape, F32)]
    scratch += [pltpu.SemaphoreType.DMA((groups, 4)), pltpu.SemaphoreType.DMA((2,))]
    got = kernel_call(body, (1,), in_specs, outs, scratch, 7.0, 60)(sc, w_up, w_qkv, w_down, w_out, vectors, lengths)
    return got[0 : 2 * groups : 2], got[1 : 2 * groups : 2], got[2 * groups], got[2 * groups + 1]


def tables(sc, lens, groups, rows, slots):
    def body(s_ref, lens_ref, cos_ref, sin_ref):
        block = pl.program_id(0)
        lengths, ends = ends_of(lens_ref, block, slots)
        index = index_of((rows, LANES), 0)
        start = jnp.zeros((rows, LANES), F32)
        for length, end in zip(lengths, ends, strict=True):
            start = start + jnp.where(jnp.broadcast_to(end, index.shape) <= index, length, 0.0)
        lane = lax.broadcasted_iota(jnp.int32, (rows, LANES), 1) % HD
        pair = (lane % (ROT // 2)).astype(F32)
        freq = jnp.where(lane < ROT, jnp.exp(-pair * (2.0 * math.log(10000.0) / ROT)), 0.0)
        angle = (index - start) * freq
        cos_ref[...] = jnp.cos(angle)
        sin_ref[...] = jnp.sin(angle)

    out = ((groups * rows, LANES), F32, by_row((rows, LANES)))
    return kernel_call(body, (groups,), [full(lens.shape)], [out, out], (), 3.0)(sc, lens)


def forward_up(sc, xs, own, mine, other, vectors, lengths):
    groups, n_x = len(xs), len(flat(xs))
    rows, width = xs[0][0].shape
    wide, ff = own.shape
    half = wide // 2
    n_vec, slots = vectors.shape[0], lengths.shape[1]
    tok = groups * rows

    def body(s_ref, *refs):
        x_refs, refs = refs[:n_x], refs[n_x:]
        own_ref = refs[0]
        mine_refs = refs[1:groups]
        other_refs = refs[groups : 2 * groups - 1]
        vec_in, len_in = refs[2 * groups - 1 : 2 * groups + 1]
        attn_ref, mlp_ref, act_ref, slope_ref, stats_ref, w_ref, vec_ref, lens_ref, x_scr = refs[2 * groups + 1 :]
        me, core = s_ref[0], s_ref[1]
        block = pl.program_id(0)

        @pl.when(block == 0)
        def _():
            w_ref[part(me * wide, wide), :] = own_ref[...]
            vec_ref[...] = jnp.zeros_like(vec_ref)
            lens_ref[...] = jnp.zeros_like(lens_ref)
            vec_ref[0:n_vec, part(me * wide, wide)] = vec_in[...].astype(BF).astype(F32)
            lens_ref[0, 0:1, 0:slots] = len_in[...].astype(F32)
            for step in range(1, groups):
                at = (me ^ step) * wide
                w_ref[part(at + core * half, half), :] = mine_refs[step - 1][:half, :]
                w_ref[part(at + (1 - core) * half, half), :] = other_refs[step - 1][:half, :]
                vec_ref[0:n_vec, part(at, wide)] = mine_refs[step - 1][half : half + n_vec, :wide].astype(F32)
                lens_ref[step, 0:1, 0:slots] = mine_refs[step - 1][
                    half + n_vec : half + n_vec + 1, :slots
                ].astype(F32)

        load_block(block, xs, x_refs, x_scr)
        x = x_scr[...].astype(F32)
        mean = jnp.mean(x, axis=1, keepdims=True)
        centred = x - mean
        inv = lax.rsqrt(jnp.mean(centred * centred, axis=1, keepdims=True) + EPS_NORM)
        normed = centred * inv
        lane = lax.broadcasted_iota(jnp.int32, (rows, LANES), 1)
        stats_ref[...] = jnp.where(lane == 0, mean, inv)
        attn_ref[...] = (normed * vec_ref[0:1, :] + vec_ref[1:2, :]).astype(BF)
        in_mlp = (normed * vec_ref[2:3, :] + vec_ref[3:4, :]).astype(BF)
        mlp_ref[...] = in_mlp
        first = me * ff
        bias = vec_ref[pl.ds(9 + first // width, 1), part(lax.rem(me, width // ff) * ff, ff, LANES)]
        act, slope = gelu_parts(dot(in_mlp, w_ref[...]) + bias)
        act_ref[...] = act.astype(BF)
        slope_ref[...] = slope

    piece = (half + EXTRA, ff)
    in_specs = (
        [full(item.shape) for item in flat(xs)]
        + [full(own.shape)]
        + [full(piece)] * (2 * (groups - 1))
        + [full(vectors.shape), full(lengths.shape)]
    )
    outs = [
        ((tok, width), BF, by_row((rows, width))),
        ((tok, width), BF, by_row((rows, width))),
        ((tok, ff), BF, by_row((rows, ff))),
        ((tok, ff), F32, by_row((rows, ff))),
        ((tok, LANES), F32, by_row((rows, LANES))),
        ((width, ff), BF, full((width, ff))),
        ((EXTRA, width), F32, full((EXTRA, width))),
        ((groups, 8, LANES), F32, full((groups, 8, LANES))),
    ]
    return kernel_call(
        body, (groups,), in_specs, outs, [pltpu.VMEM((rows, width), BF)], 6.5, 20
    )(sc, *flat(xs), own, *mine, *other, vectors, lengths)


def mask_rows(sc, cots, lens, slots):
    n_c = len(flat(cots))
    rows, width = cots[0][0].shape

    def body(s_ref, *refs):
        cot_refs = iter(refs[:n_c])
        lens_ref, branch_ref, bias_ref = refs[n_c:]
        for step, pieces in enumerate(cots):
            _, ends = ends_of(lens_ref, step, slots)
            row = 0
            for piece in pieces:
                size = piece.shape[0]
                index = index_of((size, 1), 0) + float(row)
                valid = jnp.where(index < jnp.broadcast_to(ends[-1], (size, 1)), 1.0, 0.0)
                branch = next(cot_refs)[...].astype(F32) * valid
                at = step * rows + row
                branch_ref[at : at + size, :] = branch.astype(BF)
                row += size
                if step == 0:
                    bias_ref[...] = jnp.broadcast_to(jnp.sum(branch, axis=0, keepdims=True), bias_ref.shape)

    outs = [((len(cots) * rows, width), BF, full(None)), ((8, width), F32, full(None))]
    in_specs = [full(item.shape) for item in flat(cots) + [lens]]
    return kernel_call(body, (1,), in_specs, outs, (), 1.0)(sc, *flat(cots), lens)


def grad_of_down(sc, branch, act, scale):
    tok, width = branch.shape
    size = act.shape[1] // 2

    def body(s_ref, branch_ref, act_ref, away_ref, keep_ref):
        core = s_ref[1]
        for ref, which in ((away_ref, 1 - core), (keep_ref, core)):
            ref[...] = (dot_lt(act_ref[:, part(which * size, size)], branch_ref[...]) * scale).astype(BF)

    outs = [((size, width), BF, full(None))] * 2
    return kernel_call(body, (1,), [full(branch.shape), full(act.shape)], outs, (), 3.0)(sc, branch, act)


def feed_out(sc, act, w_down, groups):
    tok, ff = act.shape
    rows = tok // groups

    def body(s_ref, act_ref, wd_ref, out_ref):
        out_ref[...] = dot(act_ref[...], wd_ref[...]).astype(BF)

    width = w_down.shape[1]
    outs = [((tok, width), BF, by_row((rows, width)))]
    return kernel_call(body, (groups,), [by_row((rows, ff)), full(None)], outs, (), 3.0)(sc, act, w_down)[0]


def backward_up(sc, branch, slope, w_down, in_mlp, scale, groups):
    tok, width = branch.shape
    rows = tok // groups
    ff = slope.shape[1]
    half = width // groups // 2

    def body(s_ref, branch_ref, slope_ref, wd_ref, mlp_ref, away_ref, keep_ref, up_ref, bias_ref):
        me, core = s_ref[0], s_ref[1]
        block = pl.program_id(0)

        @pl.when(block == 0)
        def _():
            bias_ref[...] = jnp.zeros_like(bias_ref)

        d_up = dot_rt(branch_ref[...], wd_ref[...]) * slope_ref[...]
        bias_ref[0:1, :] += jnp.sum(d_up, axis=0, keepdims=True)
        up_ref[part(block * rows, rows), :] = d_up.astype(BF)

        @pl.when(block == groups - 1)
        def _():
            def piece(i, carry):
                grad = (dot_lt(mlp_ref[:, part((me ^ i) * (2 * half), 2 * half)], up_ref[...]) * scale).astype(BF)
                keep_ref[i], away_ref[i] = halves(grad, core)
                return carry

            lax.fori_loop(0, groups, piece, 0)

    in_specs = [by_row((rows, width)), by_row((rows, ff)), full(w_down.shape), full(in_mlp.shape)]
    outs = [
        ((groups, half, ff), BF, full((groups, half, ff))),
        ((groups, half, ff), BF, full((groups, half, ff))),
        ((tok, ff), BF, full((tok, ff))),
        ((8, ff), F32, full((8, ff))),
    ]
    return kernel_call(body, (groups,), in_specs, outs, (), 6.8)(
        sc, branch, slope, w_down, in_mlp
    )


def attention(sc, in_attn, branch, cosine, sine, lens, vec, own, mine, other, w_out, groups, slots):
    tok, width = in_attn.shape
    rows = tok // groups
    wide = width // groups
    half = wide // 2
    scale = HD ** (-0.5)

    def body(s_ref, *refs):
        a_ref, branch_ref, cos_ref, sin_ref, lens_ref, vec_ref = refs[:6]
        own_ref = refs[6]
        mine_refs = refs[7 : 6 + groups]
        other_refs = refs[6 + groups : 5 + 2 * groups]
        wo_ref, heads_ref, proj_ref, bias_ref, w_ref = refs[5 + 2 * groups :]
        me, core = s_ref[0], s_ref[1]
        block = pl.program_id(0)

        @pl.when(block == 0)
        def _():
            w_ref[part(me * wide, wide), :] = own_ref[...]
            for step in range(1, groups):
                at = (me ^ step) * wide
                w_ref[part(at + core * half, half), :] = mine_refs[step - 1][...]
                w_ref[part(at + (1 - core) * half, half), :] = other_refs[step - 1][...]
            bias_ref[...] = jnp.zeros_like(bias_ref)

        bias = [vec_ref[6 + p : 7 + p, part(me * wide, wide)] for p in range(3)]
        projected = dot(a_ref[...], w_ref[...])
        d_heads = dot_rt(branch_ref[...], wo_ref[...]).astype(BF)
        _, ends = ends_of(lens_ref, block, slots)
        key_index = index_of((rows, 1), 0)
        query_index = index_of((1, rows), 1)
        allowed = (segments(key_index, ends) == segments(query_index, ends)) & (key_index <= query_index)
        lane = lax.broadcasted_iota(jnp.int32, (rows, LANES), 1)
        cosine, sine = cos_ref[...], sin_ref[...]
        low = jnp.where(lane % HD < ROT // 2, sine, 0.0)
        high = jnp.where(lane % HD >= ROT // 2, sine, 0.0)

        def turn(values, sign):
            ahead = pltpu.roll(values, LANES - ROT // 2, 1)
            behind = pltpu.roll(values, ROT // 2, 1)
            return values * cosine + sign * (behind * high - ahead * low)

        first_half = lane < HD
        for pair in range(wide // LANES):
            lo, hi = pair * LANES, (pair + 1) * LANES
            query = turn(projected[:, lo:hi] + bias[0][:, lo:hi], 1.0).astype(BF)
            key = turn(projected[:, wide + lo : wide + hi] + bias[1][:, lo:hi], 1.0).astype(BF)
            value = (projected[:, 2 * wide + lo : 2 * wide + hi] + bias[2][:, lo:hi]).astype(BF)
            d_out = d_heads[:, lo:hi]
            key_t, value_t = key.T, value.T
            heads_t, query_t, d_keys, d_values = [], [], [], []
            for head in range(2):
                mask = first_half if head == 0 else ~first_half
                only_key = jnp.where(mask, key, jnp.zeros_like(key))
                only_value = jnp.where(mask, value, jnp.zeros_like(value))
                scores = jnp.where(allowed, dot_rt(only_key, query) * scale, -1e30)
                top = jnp.max(scores, axis=0, keepdims=True)
                weights = jnp.exp(scores - top)
                probs = weights * (1.0 / jnp.sum(weights, axis=0, keepdims=True))
                probs_b = probs.astype(BF)
                d_probs = dot_rt(only_value, d_out)
                delta = jnp.sum(probs * d_probs, axis=0, keepdims=True)
                d_scores = (probs * (d_probs - delta)).astype(BF)
                heads_t.append(dot(value_t[head * HD : (head + 1) * HD], probs_b))
                query_t.append(dot(key_t[head * HD : (head + 1) * HD], d_scores))
                d_keys.append(dot(d_scores, query))
                d_values.append(dot(probs_b, d_out))
            heads_ref[:, lo:hi] = jnp.concatenate(heads_t, axis=0).T.astype(BF)
            d_query = turn(jnp.concatenate(query_t, axis=0).T * scale, -1.0)
            d_key = turn(jnp.where(first_half, d_keys[0], d_keys[1]) * scale, -1.0)
            d_value = jnp.where(first_half, d_values[0], d_values[1])
            for p, item in enumerate((d_query, d_key, d_value)):
                proj_ref[:, p * wide + lo : p * wide + hi] = item.astype(BF)
                bias_ref[0:1, p * wide + lo : p * wide + hi] += jnp.sum(item, axis=0, keepdims=True)

    in_specs = (
        [by_row((rows, width)), by_row((rows, width)), by_row((rows, LANES)), by_row((rows, LANES))]
        + [full(lens.shape), full(vec.shape)]
        + [full((half, 3 * wide))] * (1 + 2 * (groups - 1))
        + [full(w_out.shape)]
    )
    outs = [
        ((tok, wide), BF, by_row((rows, wide))),
        ((tok, 3 * wide), BF, by_row((rows, 3 * wide))),
        ((8, 3 * wide), F32, full((8, 3 * wide))),
        ((width, 3 * wide), BF, full((width, 3 * wide))),
    ]
    return kernel_call(body, (groups,), in_specs, outs, (), 0.0)(
        sc, in_attn, branch, cosine, sine, lens, vec, own, *mine, *other, w_out
    )


def back_to_tokens(sc, xs, heads, mlp, d_proj, d_up, stats, vec, w_out, w_qkv, w_up, bias_up, bias_qkv, bias_out):
    groups, n_x = len(xs), len(flat(xs))
    rows, width = xs[0][0].shape
    wide = width // groups
    ff = d_up.shape[1]

    def body(s_ref, *refs):
        x_refs, refs = refs[:n_x], refs[n_x:]
        (
            heads_ref, mlp_ref, proj_ref, d_up_ref, stats_ref, vec_ref, wo_ref, wq_ref, wu_ref,
            up_ref, qkv_ref, out_ref,
        ) = refs[:12]
        own_ref = refs[12]
        piece_refs = refs[13 : 12 + groups]
        grad_ref, x_scr = refs[12 + groups :]
        me = s_ref[0]
        block = pl.program_id(0)
        load_block(block, xs, x_refs, x_scr)

        @pl.when(block == 0)
        def _():
            grad_ref[...] = jnp.zeros_like(grad_ref)
            grad_ref[4:6, :] = out_ref[0:2, :]
            for p in range(3):
                grad_ref[6 + p : 7 + p, part(me * wide, wide)] = qkv_ref[0:1, p * wide : (p + 1) * wide]
            first = me * ff
            grad_ref[pl.ds(9 + first // width, 1), part(lax.rem(me, width // ff) * ff, ff, LANES)] = up_ref[0:1, :]

        normed = (x_scr[...].astype(F32) - stats_ref[:, 0:1]) * stats_ref[:, 1:2]
        branch_out = dot(heads_ref[...], wo_ref[...]) + mlp_ref[...].astype(F32)
        total = None
        for row, left, right in ((0, proj_ref, wq_ref), (2, d_up_ref, wu_ref)):
            d_in = dot_rt(left[...], right[...])
            grad_ref[row : row + 1, :] += jnp.sum(d_in * normed, axis=0, keepdims=True)
            grad_ref[row + 1 : row + 2, :] += jnp.sum(d_in, axis=0, keepdims=True)
            term = d_in * vec_ref[row : row + 1, :]
            total = term if total is None else total + term

        @pl.when(block == 0)
        def _():
            own_ref[:, :width] = branch_out.astype(BF)
            own_ref[:, width:] = total.astype(BF)

        for step in range(1, groups):

            @pl.when(block == step)
            def _(step=step):
                piece_refs[step - 1][:, :width] = branch_out.astype(BF)
                piece_refs[step - 1][:, width:] = total.astype(BF)

    constant = [vec, w_out, w_qkv, w_up, bias_up, bias_qkv, bias_out]
    in_specs = (
        [full(item.shape) for item in flat(xs)]
        + [by_row((rows, item.shape[1])) for item in (heads, mlp, d_proj, d_up, stats)]
        + [full(item.shape) for item in constant]
    )
    outs = [((rows, 2 * width), BF, full((rows, 2 * width)))]
    outs += [((rows, 2 * width), BF, full((rows, 2 * width)))] * (groups - 1)
    outs += [((EXTRA, width), F32, full((EXTRA, width)))]
    got = kernel_call(
        body,
        (groups,),
        in_specs,
        outs,
        [pltpu.VMEM((rows, width), BF)],
        0.0,
    )(sc, *flat(xs), heads, mlp, d_proj, d_up, stats, *constant)
    return got[0], got[1:groups], got[groups]


def grads_of_attention(sc, in_attn, d_proj, heads, branch, scale, groups):
    tok, width = in_attn.shape
    wide = heads.shape[1]
    half = wide // 2

    def body(s_ref, a_ref, proj_ref, heads_ref, branch_ref, out_away, out_keep, qkv_away, qkv_keep):
        me, core = s_ref[0], s_ref[1]

        def piece(i, carry):
            grad = (dot_lt(a_ref[:, part((me ^ i) * wide, wide)], proj_ref[...]) * scale).astype(BF)
            qkv_keep[i], qkv_away[i] = halves(grad, core)
            return carry

        lax.fori_loop(0, groups, piece, 0)
        grad = (dot_lt(heads_ref[...], branch_ref[...]) * scale).astype(BF)
        out_keep[...], out_away[...] = halves(grad, core)

    ops = (in_attn, d_proj, heads, branch)
    out = ((half, width), BF, full(None))
    qkv = ((groups, half, 3 * wide), BF, full(None))
    return kernel_call(body, (1,), [full(None)] * len(ops), [out, out, qkv, qkv], (), 0.0)(sc, *ops)


def merge(sc, qkv_keep, qkv_got, vec_grad, scale):
    groups, half, columns = qkv_keep.shape
    wide = columns // 3
    rows = half + EXTRA

    def body(s_ref, keep_ref, got_ref, vec_ref, stay_ref, away_ref):
        me = s_ref[0]
        for i in range(groups):
            ref, at = (away_ref if i % 2 else stay_ref), i // 2 * rows
            ref[at : at + half, :] = keep_ref[i] + got_ref[i]
            ref[at + half : at + rows, :] = jnp.zeros((EXTRA, columns), BF)
            ref[at + half : at + rows, :wide] = (vec_ref[:, part((me ^ i) * wide, wide)] * scale).astype(BF)

    shape = jax.ShapeDtypeStruct((groups // 2 * rows, columns), BF)
    return on_vmem(body, [shape, shape], sc, [qkv_keep, qkv_got, vec_grad])


def join(sc, qkv_rows, out_keep, out_got):
    groups = len(qkv_rows)
    half, width = out_keep.shape
    wide = 2 * half
    share = width // groups

    def body(s_ref, *refs):
        rows, (keep_ref, got_ref, out) = refs[:groups], refs[groups:]
        vec = jnp.zeros((EXTRA, wide), F32)
        out[groups * half :, :] = jnp.zeros((EXTRA, 3 * wide + share), BF)
        for i in range(groups):
            at = slice(i * half, (i + 1) * half)
            columns = slice(i * share, (i + 1) * share)
            out[at, : 3 * wide] = rows[i][:half, :]
            out[at, 3 * wide :] = keep_ref[:, columns] + got_ref[:, columns]
            vec = vec + rows[i][half:, :wide].astype(F32)
        out[groups * half :, :wide] = vec.astype(BF)

    shape = jax.ShapeDtypeStruct((groups * half + EXTRA, 3 * wide + share), BF)
    return on_vmem(body, [shape], sc, [*qkv_rows, out_keep, out_got])[0]


def finish(sc, own, got, tokens, cotangent, lens, stats, vec, slots):
    rows, width = tokens.shape

    def body(s_ref, own_ref, *refs):
        got_refs = refs[: len(got)]
        tok_ref, cot_ref, lens_ref, stats_ref, vec_ref, out_ref, grad_ref = refs[len(got) :]
        branch = own_ref[:, :width].astype(F32)
        scaled = own_ref[:, width:].astype(F32)
        for ref in got_refs:
            branch = branch + ref[:, :width].astype(F32)
            scaled = scaled + ref[:, width:].astype(F32)
        size = branch.shape[0]
        _, ends = ends_of(lens_ref, 0, slots)
        index = index_of((size, 1), 0) + (pl.program_id(0) * size).astype(F32)
        valid = jnp.where(index < jnp.broadcast_to(ends[-1], (size, 1)), 1.0, 0.0)
        x = tok_ref[...].astype(F32)
        out_ref[...] = (x + valid * (branch + vec_ref[4:5, :] + vec_ref[5:6, :])).astype(BF)
        inv = stats_ref[:, 1:2]
        normed = (x - stats_ref[:, 0:1]) * inv
        d_tokens = inv * (
            scaled
            - jnp.mean(scaled, axis=1, keepdims=True)
            - normed * jnp.mean(scaled * normed, axis=1, keepdims=True)
        )
        grad_ref[...] = (cot_ref[...].astype(F32) + d_tokens).astype(BF)

    size = rows // 2
    in_specs = [by_row((size, 2 * width))] * (1 + len(got)) + [by_row((size, width))] * 2
    in_specs += [full(lens.shape), by_row((size, LANES)), full(vec.shape)]
    out = ((rows, width), BF, by_row((size, width)))
    return kernel_call(body, (2,), in_specs, [out, out], (), 2.4)(
        sc, own, *got, tokens, cotangent, lens, stats, vec
    )


def assemble(shapes, arrays, plan):
    def body(*refs):
        ins, outs = refs[: len(arrays)], refs[len(arrays) :]
        me, core = lax.axis_index("shard"), lax.rem(lax.axis_index("dp"), 2)
        for target, row, column, size, which, index in plan(me, core):
            outs[target][part(row, size[0]), part(column, size[1])] = ins[which][index]

    vmem = pl.BlockSpec(memory_space=pltpu.VMEM)
    return pl.pallas_call(
        body,
        out_shape=[jax.ShapeDtypeStruct(shape, arrays[0].dtype) for shape in shapes],
        in_specs=[vmem] * len(arrays),
        out_specs=[vmem] * len(shapes),
        compiler_params=pltpu.CompilerParams(vmem_limit_bytes=8 * MIB),
        cost_estimate=pl.CostEstimate(flops=0, bytes_accessed=int(3.2e6), transcendentals=0),
    )(*arrays)


def adam_blocks(sc, grads, masters, grid, block, where, fill, time):
    shape = masters[0].shape

    def body(s_ref, *refs):
        grad_refs = refs[: len(grads)]
        w_ref, m_ref, v_ref, g_out, w_out, m_out, v_out = refs[len(grads) :]
        fill(s_ref, grad_refs, g_out)
        w_out[...], m_out[...], v_out[...] = adam_terms(
            w_ref[...], m_ref[...], v_ref[...], g_out[...], DECAY_RATE, LEARN_RATE
        )

    spec = pl.BlockSpec(block, where)
    return kernel_call(
        body, grid, [full(None)] * len(grads) + [spec] * 3, [(shape, F32, spec)] * 4, (), time, 30
    )(sc, *grads, *masters)


def choose(condition, yes, no, out):
    @pl.when(condition)
    def _():
        out[...] = yes().astype(F32)

    @pl.when(jnp.logical_not(condition))
    def _():
        out[...] = no().astype(F32)


def adam(masters, grad, decay=DECAY_RATE, rate=LEARN_RATE):
    weight, first, second = masters
    grad = grad.astype(F32)
    return (grad,) + adam_terms(weight, first, second, grad, decay, rate)


def local(
    tokens, cotangent, lengths,
    w_qkv, w_out, w_up, w_down, vectors,
    m_qkv, m_out, m_up, m_down, m_vectors,
    v_qkv, v_out, v_up, v_down, v_vectors,
):
    groups = lax.axis_size("shard")
    me = lax.axis_index("shard")
    core = lax.axis_index("dp") % 2
    rows, width = tokens.shape
    hidden = w_up.shape[1]
    wide = width // groups
    half = wide // 2
    ff = hidden // groups
    n_vec = vectors.shape[0]
    slots = lengths.shape[1]
    others = range(1, groups)
    places = lax.axis_size("dp") // 2
    place = lax.axis_index("dp") // 2
    outer = (place == 0) | (place == places - 1)
    sc = jnp.stack([me, core, outer]).astype(jnp.int32)
    scale = float(rows * groups * lax.axis_size("dp")) ** (-0.5)

    size = ff // 2
    fence = lax.optimization_barrier

    up_parts, qkv_parts, down_w, out_w = pack(groups, sc, w_up, w_qkv, w_down, w_out, vectors, lengths)
    near = [shard_swap(tokens, step) for step in (1, 2)]
    near, up_parts = fence((near, up_parts))
    up_mine = [shard_swap(item, step) for item, step in zip(up_parts[1:], others, strict=True)]
    xs = gather_rest(tokens, near)
    cot_near = [shard_swap(after(cotangent, xs[3]), step) for step in (1, 2)]
    up_other = [core_swap(item) for item in up_mine]
    in_attn, in_mlp, act, slope, stats, up_w, vec, lens = forward_up(
        sc, xs, up_parts[0], up_mine, up_other, vectors, lengths
    )
    cot_near, act = fence((cot_near, act))
    cots = gather_rest(cotangent, cot_near)
    qkv_mine = [shard_swap(item, step) for item, step in zip(after(qkv_parts[1:], cot_near), others, strict=True)]
    mlp = feed_out(sc, after(act, cot_near), down_w, groups)
    cosine, sine = tables(sc, after(lens, mlp), groups, rows, slots)
    cots, cosine = fence((cots, cosine))

    branch, bias_out = mask_rows(sc, cots, lens, slots)
    up_away, up_keep, d_up, bias_up = backward_up(sc, branch, slope, down_w, in_mlp, scale, groups)
    up_away, up_keep, qkv_mine, branch = fence((up_away, up_keep, qkv_mine, branch))
    up_got = core_swap(up_away)
    qkv_other = [core_swap(item) for item in qkv_mine]
    down_away, down_keep = grad_of_down(sc, branch, act, scale)
    down_away, down_keep, up_got, qkv_other = fence((down_away, down_keep, up_got, qkv_other))
    down_got = core_swap(down_away)
    up_sums = [up_keep[i] + up_got[i] for i in range(groups)]
    up_sums, down_got = fence((up_sums, down_got))
    down = down_keep + down_got
    down, branch_a = fence((down, branch))

    down, _, _ = dp_round(sc, down, None, None)
    up_rows = [up_sums[0]] + [shard_swap(up_sums[step], step) for step in others]
    heads, d_proj, bias_qkv, qkv_w = attention(
        sc, in_attn, branch_a, cosine, sine, lens, vec, qkv_parts[0], qkv_mine, qkv_other, out_w, groups, slots
    )
    up_rows, d_proj = fence((up_rows, d_proj))
    out_away, out_keep, qkv_away, qkv_keep = grads_of_attention(sc, in_attn, d_proj, heads, branch, scale, groups)
    out_away, qkv_away, d_proj = fence((out_away, qkv_away, d_proj))
    qkv_got = core_swap(qkv_away)
    out_got = core_swap(out_away)
    own, pieces, vec_grad = back_to_tokens(
        sc, xs, heads, mlp, d_proj, d_up, stats, vec, out_w, qkv_w, up_w, bias_up, bias_qkv, bias_out
    )
    down, up_rows, qkv_got, out_got, vec_grad = fence((down, up_rows, qkv_got, out_got, vec_grad))
    up = jnp.concatenate(up_rows)
    stay, away = merge(sc, qkv_keep, qkv_got, vec_grad, scale)
    up, down, stay, away = fence((up, down, stay, away))

    qkv_rows = exchange(stay, away)
    rest = join(sc, qkv_rows, out_keep, out_got)
    up, down, _ = dp_round(sc, up, down, None, rest)
    down, up, rest, pieces = fence((down, up, rest, pieces))

    rest, up, down = dp_round(sc, rest, up, down, rows=size)
    got = [shard_swap(item, step) for item, step in zip(pieces[:2], (1, 2), strict=True)]
    down, up, rest, got, pieces = fence((down, up, rest, got, pieces))

    down_other = core_swap(down)
    _, rest, up = dp_round(sc, None, rest, up)
    got += [shard_swap(item, step) for item, step in zip(pieces[2:], others[2:], strict=True)]

    def fill_down(s_ref, refs, out):
        step = pl.program_id(0)
        at = part((step % 2) * (size // 2), size // 2)
        choose(step // 2 == s_ref[1], lambda: refs[0][at, :], lambda: refs[1][at, :], out)

    new_down = adam_blocks(
        sc, [down, down_other], (w_down, m_down, v_down),
        (4,), (size // 2, width), lambda i, s: (i, 0), fill_down, 0.0,
    )
    up, rest, new_down, got = fence((up, rest, new_down, got))

    up_other = core_swap(up)
    _, _, rest = dp_round(sc, None, None, rest)

    def fill_up(s_ref, refs, out):
        at = part((s_ref[0] ^ pl.program_id(1)) * half, half)
        choose(pl.program_id(0) == s_ref[1], lambda: refs[0][at, :], lambda: refs[1][at, :], out)

    new_up = adam_blocks(
        sc, [up, up_other], (w_up, m_up, v_up),
        (2, groups), (half, ff), lambda i, j, s: (i, j), fill_up, 0.0,
    )
    output, input_grad = finish(sc, own, got, tokens, cotangent, lens, stats, vec, slots)
    rest, new_up, output, input_grad = fence((rest, new_up, output, input_grad))
    rest_other = core_swap(rest)

    def rest_plan(me, core):
        plan = []
        for side in range(2):
            row = (core ^ side) * half
            for step in range(groups):
                at = slice(step * half, (step + 1) * half)
                for p in range(3):
                    columns = slice(p * wide, (p + 1) * wide)
                    plan.append((0, row, p * width + (me ^ step) * wide, (half, wide), side, (at, columns)))
                columns = slice(3 * wide, 4 * wide)
                plan.append((1, row, step * wide, (half, wide), side, (at, columns)))
        return plan

    qkv_grad, out_grad = assemble([(wide, 3 * width), (wide, width)], [rest, rest_other], rest_plan)
    vec_rows = slice(groups * half, groups * half + n_vec)
    vec_total = rest[vec_rows, :wide].astype(F32) + rest_other[vec_rows, :wide].astype(F32)

    news = (
        adam((w_qkv, m_qkv, v_qkv), qkv_grad),
        adam((w_out, m_out, v_out), out_grad),
        new_up,
        new_down,
        adam((vectors, m_vectors, v_vectors), vec_total, 0.0, VECTOR_RATE),
    )
    return (output, input_grad) + tuple(item[kind] for kind in range(4) for item in news)


def solution(mesh):
    by_token = P(("shard", "dp"), None)
    params = (P("shard", None),) * 4 + (P(None, "shard"),)
    return jax.shard_map(
        local,
        mesh=mesh,
        in_specs=(by_token,) * 3 + params * 3,
        out_specs=(by_token,) * 2 + params * 4,
        check_vma=False,
    )
```

```python
import functools
import math

import jax
import jax.numpy as jnp
from jax import lax
from jax.experimental import pallas as pl
from jax.experimental.pallas import tpu as pltpu
from jax.sharding import PartitionSpec as P

H = 16
HD = 64
ROT = 16
ADAM_STEP = 4


EPS_NORM = 1e-05
BETA_ONE = 0.9
BETA_TWO = 0.95
ADAM_EPS = 1e-08
LEARN_RATE = 0.01
VECTOR_RATE = 0.1
DECAY_RATE = 0.1
SQRT_HALF = 0.7071067811865476
INV_ROOT_TWO_PI = 0.3989422804014327

BF = jnp.bfloat16
F32 = jnp.float32
EXTRA = 16
LANES = 128
MIB = 2**20


def dot(left, right):
    return jnp.dot(left, right, preferred_element_type=F32)


def dot_lt(left, right):
    return lax.dot_general(left, right, (((0,), (0,)), ((), ())), preferred_element_type=F32)


def dot_rt(left, right):
    return lax.dot_general(left, right, (((1,), (1,)), ((), ())), preferred_element_type=F32)


def part(start, size, multiple=None):
    return pl.ds(pl.multiple_of(start, multiple or size), size)


def shard_swap(value, step):
    size = lax.axis_size("shard")
    return lax.ppermute(value, "shard", [(i, i ^ step) for i in range(size)])


def exchange(stay, away):
    size = lax.axis_size("shard")
    rows = stay.shape[0] // (size // 2)
    got = shard_swap(away, 1)
    pieces = [(got if step % 2 else stay)[step // 2 * rows : (step // 2 + 1) * rows] for step in range(size)]
    bit = 2
    while bit < size:
        sent = [step for step in range(size) if step & bit]
        got = shard_swap(jnp.concatenate([pieces[step] for step in sent]), bit)
        for i, step in enumerate(sent):
            pieces[step] = got[i * rows : (i + 1) * rows]
        bit *= 2
    return pieces


def core_swap(value):
    size = lax.axis_size("dp")
    return lax.ppermute(value, "dp", [(i, i ^ 1) for i in range(size)])


def chain_stages():
    places = lax.axis_size("dp") // 2
    half = places // 2
    if places == 1:
        return []
    stages = []
    for step in range(half - 1):
        stages.append(([(step, step + 1), (places - 1 - step, places - 2 - step)], None))
    stages.append(([(half - 1, half), (half, half - 1)], None))
    for step in reversed(range(half - 1)):
        stages.append(
            ([(step + 1, step), (places - 2 - step, places - 1 - step)], (step, places - 1 - step))
        )
    return stages


def place_send(value, pairs):
    return lax.ppermute(
        value, "dp", [(2 * a + core, 2 * b + core) for a, b in pairs for core in range(2)]
    )


def after(value, *earlier):
    return lax.optimization_barrier((value, earlier))[0]


def combine(items):
    def body(flag_ref, *refs):
        count = len(items)
        for i, (_, _, taker) in enumerate(items):
            value, got, out = refs[2 * i], refs[2 * i + 1], refs[2 * count + i]
            if taker is None:
                out[...] = value[...] + got[...]
            else:
                out[...] = jnp.where(flag_ref[i] > 0, got[...], value[...])

    flags = [jnp.int32(0) if taker is None else taker.astype(jnp.int32) for _, _, taker in items]
    vmem = pl.BlockSpec(memory_space=pltpu.VMEM)
    return pl.pallas_call(
        body,
        out_shape=[jax.ShapeDtypeStruct(value.shape, value.dtype) for value, _, _ in items],
        in_specs=[pl.BlockSpec(memory_space=pltpu.SMEM)] + [vmem] * (2 * len(items)),
        out_specs=[vmem] * len(items),
        compiler_params=pltpu.CompilerParams(vmem_limit_bytes=12 * MIB),
        cost_estimate=pl.CostEstimate(flops=0, bytes_accessed=int(3.2e6), transcendentals=0),
    )(jnp.stack(flags), *[item for value, got, _ in items for item in (value, got)])


def advance(*moves):
    values = [value for value, _ in moves]
    depth = max(len(stages) for _, stages in moves)
    for step in range(depth):
        active = [i for i, (_, stages) in enumerate(moves) if step < len(stages)]
        items = []
        for i in active:
            pairs, takers = moves[i][1][step]
            flag = None
            if takers is not None:
                place = lax.axis_index("dp") // 2
                flag = functools.reduce(jnp.logical_or, [place == taker for taker in takers])
            items.append((values[i], place_send(values[i], pairs), flag))
        for i, item in zip(active, combine(items), strict=True):
            values[i] = item
    return values


def chain_parts():
    stages = chain_stages()
    half = (len(stages) + 1) // 2
    if not stages:
        return [], [], []
    return stages[: half - 1], stages[half - 1 : half], stages[half:]


def dp_round(sc, fresh, inner, total, upcoming=None, rows=None):
    parts = chain_parts()
    if lax.axis_size("dp") // 2 != 4:
        moves = [(value, stages) for value, stages in zip((fresh, inner, total), parts, strict=True) if value is not None]
        moved = iter(advance(*moves))
        return [None if value is None else next(moved) for value in (fresh, inner, total)]
    if fresh is None:
        sent, pairs = total, [(1, 0), (2, 3)]
    elif total is None:
        sent, pairs = fresh, [(0, 1), (3, 2)]
    else:
        sent, pairs = total, [(0, 1), (1, 0), (2, 3), (3, 2)]
    edge = place_send(sent, pairs)
    centre = None if inner is None else place_send(inner, [(1, 2), (2, 1)])
    arrays, shapes, steps = [], [], []

    def plan(kind, items, shape):
        steps.append((kind, len(arrays), len(shapes)))
        arrays.extend(items)
        shapes.append(shape)

    if fresh is not None:
        plan("sum", [fresh, edge], fresh)
    if inner is not None and upcoming is None:
        plan("sum", [inner, centre], inner)
    if inner is not None and upcoming is not None:
        plan("next", [inner, centre, upcoming], max(inner, upcoming, key=lambda item: item.shape[0]))
    if total is not None:
        shape = total if rows is None else jax.ShapeDtypeStruct((rows, total.shape[1]), total.dtype)
        plan("last", [total, edge], shape)

    def body(s_ref, *refs):
        outs = refs[len(arrays) :]
        for kind, at, place in steps:
            value, got, out = refs[at], refs[at + 1], outs[place]
            size = min(value.shape[0], out.shape[0])
            if kind == "sum":
                out[...] = value[...] + got[:size, :]
                continue

            @pl.when(s_ref[2] == 0)
            def _(kind=kind, value=value, got=got, out=out, size=size):
                out[:size, :] = value[:size, :] + got[:size, :] if kind == "next" else value[:size, :]

            @pl.when(s_ref[2] > 0)
            def _(kind=kind, got=got, out=out, at=at, size=size):
                if kind == "next":
                    out[: refs[at + 2].shape[0], :] = refs[at + 2][...]
                else:
                    out[...] = got[:size, :]

    moved = iter(on_vmem(body, shapes, sc, arrays))
    return [None if value is None else next(moved) for value in (fresh, inner, total)]


def on_vmem(body, shapes, sc, arrays, limit=8):
    vmem = pl.BlockSpec(memory_space=pltpu.VMEM)
    return pl.pallas_call(
        body,
        out_shape=[jax.ShapeDtypeStruct(item.shape, item.dtype) for item in shapes],
        in_specs=[pl.BlockSpec(memory_space=pltpu.SMEM)] + [vmem] * len(arrays),
        out_specs=[vmem] * len(shapes),
        compiler_params=pltpu.CompilerParams(vmem_limit_bytes=limit * MIB),
        cost_estimate=pl.CostEstimate(flops=0, bytes_accessed=int(3.2e6), transcendentals=0),
    )(sc, *arrays)


def gather_rest(block, near):
    groups = lax.axis_size("shard")
    rows = block.shape[0]
    got = [[block], [near[0]], [near[1]]]
    got.append([shard_swap(near[0][: rows // 2], 2), shard_swap(near[1][rows // 2 :], 1)])
    for step in range(4, groups):
        got.append([shard_swap(block, step)])
    return got


def whole():
    return pl.BlockSpec(memory_space=pltpu.VMEM)


def full(shape):
    return pl.BlockSpec(memory_space=pltpu.VMEM)


def by_row(shape):
    return pl.BlockSpec(shape, lambda i, *_: (i,) + (0,) * (len(shape) - 1))


def kernel_call(body, grid, in_specs, outs, scratch=(), time=1.0, limit=12):
    return pl.pallas_call(
        body,
        out_shape=[jax.ShapeDtypeStruct(shape, dtype) for shape, dtype, _ in outs],
        grid_spec=pltpu.PrefetchScalarGridSpec(
            num_scalar_prefetch=1,
            grid=grid,
            in_specs=in_specs,
            out_specs=[spec for _, _, spec in outs],
            scratch_shapes=list(scratch),
        ),
        compiler_params=pltpu.CompilerParams(vmem_limit_bytes=limit * MIB),
        cost_estimate=pl.CostEstimate(flops=0, bytes_accessed=int(3.2e6 * time), transcendentals=0),
    )


def flat(blocks):
    return [piece for block in blocks for piece in block]


def load_block(block, blocks, refs, scratch):
    at = 0
    for step, pieces in enumerate(blocks):
        mine = refs[at : at + len(pieces)]
        at += len(pieces)

        @pl.when(block == step)
        def _(mine=mine):
            row = 0
            for ref in mine:
                scratch[row : row + ref.shape[0], :] = ref[...]
                row += ref.shape[0]


def halves(value, core):
    size = value.shape[0] // 2
    first, second = value[:size], value[size:]
    return jnp.where(core == 0, first, second), jnp.where(core == 0, second, first)


def ends_of(lens_ref, block, slots):
    lengths = [lens_ref[block, 0:1, k : k + 1] for k in range(slots)]
    ends = []
    for item in lengths:
        ends.append(item if not ends else ends[-1] + item)
    return lengths, ends


def segments(index, ends):
    total = jnp.zeros(index.shape, F32)
    for end in ends:
        total = total + jnp.where(jnp.broadcast_to(end, index.shape) <= index, 1.0, 0.0)
    return total


def index_of(shape, axis):
    return lax.broadcasted_iota(jnp.int32, shape, axis).astype(F32)


def gelu_parts(values):
    gate = 0.5 * (1.0 + lax.erf(values * SQRT_HALF))
    slope = gate + values * jnp.exp(-0.5 * values * values) * INV_ROOT_TWO_PI
    return values * gate, slope


def adam_terms(weight, first, second, grad, decay, rate):
    corr_one = 1.0 - math.exp(ADAM_STEP * math.log(BETA_ONE))
    corr_two = 1.0 - math.exp(ADAM_STEP * math.log(BETA_TWO))
    first_new = BETA_ONE * first + (1.0 - BETA_ONE) * grad
    second_new = BETA_TWO * second + (1.0 - BETA_TWO) * grad * grad
    step_size = (first_new * (1.0 / corr_one)) / (jnp.sqrt(second_new * (1.0 / corr_two)) + ADAM_EPS)
    return weight - rate * (step_size + decay * weight), first_new, second_new


def pack(groups, sc, w_up, w_qkv, w_down, w_out, vectors, lengths):
    wide, hidden = w_up.shape
    half, quarter, ff = wide // 2, wide // 4, hidden // groups
    n_vec, slots = vectors.shape[0], lengths.shape[1]

    def body(s_ref, up_hbm, qkv_hbm, down_hbm, out_hbm, vec_ref, len_ref, *refs):
        out, (down_out, out_out) = refs[: 2 * groups], refs[2 * groups : 2 * groups + 2]
        up_scr, qkv_scr, down_scr, out_scr, sems, more = refs[2 * groups + 2 :]
        me, core = s_ref[0], s_ref[1]
        rest = [
            pltpu.make_async_copy(down_hbm, down_scr, more.at[0]),
            pltpu.make_async_copy(out_hbm, out_scr, more.at[1]),
        ]
        copies = []
        for step in range(groups):
            size = wide if step == 0 else quarter
            rows = pl.ds(0, wide) if step == 0 else part((2 * s_ref[3] + core) * quarter, quarter)
            owner = me ^ step
            at = pl.ds(0 if step == 0 else wide + (step - 1) * quarter, size)
            mine = [pltpu.make_async_copy(up_hbm.at[rows, part(owner * ff, ff)], up_scr.at[at], sems.at[step, 0])]
            size = wide if step == 0 else half
            rows = pl.ds(0, wide) if step == 0 else part(core * half, half)
            at = pl.ds(0 if step == 0 else wide + (step - 1) * half, size)
            for p in range(3):
                mine.append(
                    pltpu.make_async_copy(
                        qkv_hbm.at[rows, part(p * groups * wide + owner * wide, wide)],
                        qkv_scr.at[at, pl.ds(p * wide, wide)],
                        sems.at[step, 1 + p],
                    )
                )
            copies.append(mine)
        order = list(range(1, groups)) + [0]
        for step in order:
            for copy in copies[step]:
                copy.start()
        for copy in rest:
            copy.start()
        for step in order:
            for copy in copies[step]:
                copy.wait()
            up_out, qkv_out = out[2 * step], out[2 * step + 1]
            if step == 0:
                up_out[...] = up_scr[:wide].astype(BF)
                qkv_out[...] = qkv_scr[:wide].astype(BF)
                continue
            at = wide + (step - 1) * quarter
            up_out[:quarter, :] = up_scr[at : at + quarter].astype(BF)
            up_out[quarter:, :] = jnp.zeros((EXTRA, ff), BF)
            up_out[quarter : quarter + n_vec, :wide] = vec_ref[...].astype(BF)
            up_out[quarter + n_vec : quarter + n_vec + 1, :slots] = len_ref[...].astype(F32).astype(BF)
            at = wide + (step - 1) * half
            qkv_out[...] = qkv_scr[at : at + half].astype(BF)
        for copy in rest:
            copy.wait()
        down_out[...] = down_scr[...].astype(BF)
        out_out[...] = out_scr[...].astype(BF)

    in_specs = [pl.BlockSpec(memory_space=pltpu.HBM)] * 4 + [full(vectors.shape), full(lengths.shape)]
    outs = []
    for step in range(groups):
        size = wide if step == 0 else half
        outs.append(((wide if step == 0 else quarter + EXTRA, ff), BF, full(None)))
        outs.append(((size, 3 * wide), BF, full(None)))
    outs += [(w_down.shape, BF, full(None)), (w_out.shape, BF, full(None))]
    rows = wide + (groups - 1) * half
    scratch = [pltpu.VMEM((wide + (groups - 1) * quarter, ff), F32), pltpu.VMEM((rows, 3 * wide), F32)]
    scratch += [pltpu.VMEM(w_down.shape, F32), pltpu.VMEM(w_out.shape, F32)]
    scratch += [pltpu.SemaphoreType.DMA((groups, 4)), pltpu.SemaphoreType.DMA((2,))]
    got = kernel_call(body, (1,), in_specs, outs, scratch, 7.0, 60)(sc, w_up, w_qkv, w_down, w_out, vectors, lengths)
    return got[0 : 2 * groups : 2], got[1 : 2 * groups : 2], got[2 * groups], got[2 * groups + 1]


def tables(sc, lens, groups, rows, slots):
    def body(s_ref, lens_ref, cos_ref, sin_ref):
        lane = lax.broadcasted_iota(jnp.int32, (8, LANES), 1) % HD
        pair = (lane % (ROT // 2)).astype(F32)
        freq = jnp.where(lane < ROT, jnp.exp(-pair * (2.0 * math.log(10000.0) / ROT)), 0.0)[0:1, :]
        index = index_of((rows, LANES), 0)
        angle = index * freq
        cos_index, sin_index = jnp.cos(angle), jnp.sin(angle)
        for block in range(groups):
            lengths, ends = ends_of(lens_ref, block, slots)
            cos_start = jnp.ones((rows, LANES), F32)
            sin_start = jnp.zeros((rows, LANES), F32)
            for length, end in zip(lengths, ends, strict=True):
                turn = jnp.broadcast_to(end, (8, LANES)) * jnp.broadcast_to(freq, (8, LANES))
                inside = jnp.broadcast_to(end, index.shape) <= index
                cos_start = jnp.where(inside, jnp.cos(turn)[0:1, :], cos_start)
                sin_start = jnp.where(inside, jnp.sin(turn)[0:1, :], sin_start)
            at = slice(block * rows, (block + 1) * rows)
            cos_ref[at, :] = cos_index * cos_start + sin_index * sin_start
            sin_ref[at, :] = sin_index * cos_start - cos_index * sin_start

    out = ((groups * rows, LANES), F32, full(None))
    return kernel_call(body, (1,), [full(lens.shape)], [out, out], (), 1.5)(sc, lens)


def forward_up(sc, xs, own, mine, other, vectors, lengths):
    groups, n_x = len(xs), len(flat(xs))
    rows, width = xs[0][0].shape
    wide, ff = own.shape
    quarter = wide // 4
    n_vec, slots = vectors.shape[0], lengths.shape[1]
    tok = groups * rows

    def body(s_ref, *refs):
        x_refs, refs = refs[:n_x], refs[n_x:]
        own_ref = refs[0]
        mine_refs = refs[1:groups]
        other_refs = refs[groups : groups + 3]
        vec_in, len_in = refs[groups + 3 : groups + 5]
        attn_ref, mlp_ref, act_ref, slope_ref, stats_ref, w_ref, vec_ref, lens_ref, x_scr = refs[groups + 5 :]
        me, core, side = s_ref[0], s_ref[1], s_ref[3]
        block = pl.program_id(0)

        @pl.when(block == 0)
        def _():
            w_ref[part(me * wide, wide), :] = own_ref[...]
            vec_ref[...] = jnp.zeros_like(vec_ref)
            lens_ref[...] = jnp.zeros_like(lens_ref)
            vec_ref[0:n_vec, part(me * wide, wide)] = vec_in[...].astype(BF).astype(F32)
            lens_ref[0, 0:1, 0:slots] = len_in[...].astype(F32)
            for step in range(1, groups):
                at = (me ^ step) * wide
                w_ref[part(at + (2 * side + core) * quarter, quarter), :] = mine_refs[step - 1][:quarter, :]
                for ref, which in zip(
                    other_refs, (2 * (1 - side) + core, 2 * side + 1 - core, 2 * (1 - side) + 1 - core), strict=True
                ):
                    w_ref[part(at + which * quarter, quarter), :] = ref[(step - 1) * quarter : step * quarter, :]
                vec_ref[0:n_vec, part(at, wide)] = mine_refs[step - 1][quarter : quarter + n_vec, :wide].astype(F32)
                lens_ref[step, 0:1, 0:slots] = mine_refs[step - 1][
                    quarter + n_vec : quarter + n_vec + 1, :slots
                ].astype(F32)

        load_block(block, xs, x_refs, x_scr)
        x = x_scr[...].astype(F32)
        mean = jnp.mean(x, axis=1, keepdims=True)
        centred = x - mean
        inv = lax.rsqrt(jnp.mean(centred * centred, axis=1, keepdims=True) + EPS_NORM)
        normed = centred * inv
        lane = lax.broadcasted_iota(jnp.int32, (rows, LANES), 1)
        stats_ref[...] = jnp.where(lane == 0, mean, inv)
        attn_ref[...] = (normed * vec_ref[0:1, :] + vec_ref[1:2, :]).astype(BF)
        in_mlp = (normed * vec_ref[2:3, :] + vec_ref[3:4, :]).astype(BF)
        mlp_ref[...] = in_mlp
        first = me * ff
        bias = vec_ref[pl.ds(9 + first // width, 1), part(lax.rem(me, width // ff) * ff, ff, LANES)]
        act, slope = gelu_parts(dot(in_mlp, w_ref[...]) + bias)
        act_ref[...] = act.astype(BF)
        slope_ref[...] = slope

    in_specs = (
        [full(item.shape) for item in flat(xs)]
        + [full(own.shape)]
        + [full(None)] * (groups + 2)
        + [full(vectors.shape), full(lengths.shape)]
    )
    outs = [
        ((tok, width), BF, by_row((rows, width))),
        ((tok, width), BF, by_row((rows, width))),
        ((tok, ff), BF, by_row((rows, ff))),
        ((tok, ff), F32, by_row((rows, ff))),
        ((tok, LANES), F32, by_row((rows, LANES))),
        ((width, ff), BF, full((width, ff))),
        ((EXTRA, width), F32, full((EXTRA, width))),
        ((groups, 8, LANES), F32, full((groups, 8, LANES))),
    ]
    return kernel_call(
        body, (groups,), in_specs, outs, [pltpu.VMEM((rows, width), BF)], 6.5, 20
    )(sc, *flat(xs), own, *mine, *other, vectors, lengths)


def mask_rows(sc, cots, lens, slots):
    n_c = len(flat(cots))
    rows, width = cots[0][0].shape

    def body(s_ref, *refs):
        cot_refs = iter(refs[:n_c])
        lens_ref, branch_ref, bias_ref = refs[n_c:]
        for step, pieces in enumerate(cots):
            _, ends = ends_of(lens_ref, step, slots)
            row = 0
            for piece in pieces:
                size = piece.shape[0]
                index = index_of((size, 1), 0) + float(row)
                valid = jnp.where(index < jnp.broadcast_to(ends[-1], (size, 1)), 1.0, 0.0)
                branch = next(cot_refs)[...].astype(F32) * valid
                at = step * rows + row
                branch_ref[at : at + size, :] = branch.astype(BF)
                row += size
                if step == 0:
                    bias_ref[...] = jnp.broadcast_to(jnp.sum(branch, axis=0, keepdims=True), bias_ref.shape)

    outs = [((len(cots) * rows, width), BF, full(None)), ((8, width), F32, full(None))]
    in_specs = [full(item.shape) for item in flat(cots) + [lens]]
    return kernel_call(body, (1,), in_specs, outs, (), 1.0)(sc, *flat(cots), lens)


def grad_of_down(sc, branch, act, scale):
    tok, width = branch.shape
    size = act.shape[1] // 2

    def body(s_ref, branch_ref, act_ref, away_ref, keep_ref):
        core = s_ref[1]
        for ref, which in ((away_ref, 1 - core), (keep_ref, core)):
            ref[...] = (dot_lt(act_ref[:, part(which * size, size)], branch_ref[...]) * scale).astype(BF)

    outs = [((size, width), BF, full(None))] * 2
    return kernel_call(body, (1,), [full(branch.shape), full(act.shape)], outs, (), 3.0)(sc, branch, act)


def feed_out(sc, act, w_down, groups):
    tok, ff = act.shape
    rows = tok // groups

    def body(s_ref, act_ref, wd_ref, out_ref):
        out_ref[...] = dot(act_ref[...], wd_ref[...]).astype(BF)

    width = w_down.shape[1]
    outs = [((tok, width), BF, by_row((rows, width)))]
    return kernel_call(body, (groups,), [by_row((rows, ff)), full(None)], outs, (), 3.0)(sc, act, w_down)[0]


def backward_up(sc, branch, slope, w_down, in_mlp, scale, groups):
    tok, width = branch.shape
    rows = tok // groups
    ff = slope.shape[1]
    half = width // groups // 2

    def body(s_ref, branch_ref, slope_ref, wd_ref, mlp_ref, away_ref, keep_ref, up_ref, bias_ref):
        me, core = s_ref[0], s_ref[1]
        block = pl.program_id(0)

        @pl.when(block == 0)
        def _():
            bias_ref[...] = jnp.zeros_like(bias_ref)

        d_up = dot_rt(branch_ref[...], wd_ref[...]) * slope_ref[...]
        bias_ref[0:1, :] += jnp.sum(d_up, axis=0, keepdims=True)
        up_ref[part(block * rows, rows), :] = d_up.astype(BF)

        @pl.when(block == groups - 1)
        def _():
            def piece(i, carry):
                grad = (dot_lt(mlp_ref[:, part((me ^ i) * (2 * half), 2 * half)], up_ref[...]) * scale).astype(BF)
                keep_ref[i], away_ref[i] = halves(grad, core)
                return carry

            lax.fori_loop(0, groups, piece, 0)

    in_specs = [by_row((rows, width)), by_row((rows, ff)), full(w_down.shape), full(in_mlp.shape)]
    outs = [
        ((groups, half, ff), BF, full((groups, half, ff))),
        ((groups, half, ff), BF, full((groups, half, ff))),
        ((tok, ff), BF, full((tok, ff))),
        ((8, ff), F32, full((8, ff))),
    ]
    return kernel_call(body, (groups,), in_specs, outs, (), 6.8)(
        sc, branch, slope, w_down, in_mlp
    )


def attention(sc, in_attn, branch, cosine, sine, lens, vec, own, mine, other, w_out, groups, slots):
    tok, width = in_attn.shape
    rows = tok // groups
    wide = width // groups
    half = wide // 2
    scale = HD ** (-0.5)

    def body(s_ref, *refs):
        a_ref, branch_ref, cos_ref, sin_ref, lens_ref, vec_ref = refs[:6]
        own_ref = refs[6]
        mine_refs = refs[7 : 6 + groups]
        other_refs = refs[6 + groups : 5 + 2 * groups]
        wo_ref, heads_ref, proj_ref, bias_ref, w_ref = refs[5 + 2 * groups :]
        me, core = s_ref[0], s_ref[1]
        block = pl.program_id(0)

        @pl.when(block == 0)
        def _():
            w_ref[part(me * wide, wide), :] = own_ref[...]
            for step in range(1, groups):
                at = (me ^ step) * wide
                w_ref[part(at + core * half, half), :] = mine_refs[step - 1][...]
                w_ref[part(at + (1 - core) * half, half), :] = other_refs[step - 1][...]
            bias_ref[...] = jnp.zeros_like(bias_ref)

        bias = [vec_ref[6 + p : 7 + p, part(me * wide, wide)] for p in range(3)]
        projected = dot(a_ref[...], w_ref[...])
        d_heads = dot_rt(branch_ref[...], wo_ref[...]).astype(BF)
        _, ends = ends_of(lens_ref, block, slots)
        key_index = index_of((rows, 1), 0)
        query_index = index_of((1, rows), 1)
        allowed = (segments(key_index, ends) == segments(query_index, ends)) & (key_index <= query_index)
        lane = lax.broadcasted_iota(jnp.int32, (rows, LANES), 1)
        cosine, sine = cos_ref[...], sin_ref[...]
        low = jnp.where(lane % HD < ROT // 2, sine, 0.0)
        high = jnp.where(lane % HD >= ROT // 2, sine, 0.0)

        def turn(values, sign):
            ahead = pltpu.roll(values, LANES - ROT // 2, 1)
            behind = pltpu.roll(values, ROT // 2, 1)
            return values * cosine + sign * (behind * high - ahead * low)

        first_half = lane < HD
        for pair in range(wide // LANES):
            lo, hi = pair * LANES, (pair + 1) * LANES
            query = turn(projected[:, lo:hi] + bias[0][:, lo:hi], 1.0).astype(BF)
            key = turn(projected[:, wide + lo : wide + hi] + bias[1][:, lo:hi], 1.0).astype(BF)
            value = (projected[:, 2 * wide + lo : 2 * wide + hi] + bias[2][:, lo:hi]).astype(BF)
            d_out = d_heads[:, lo:hi]
            key_t, value_t = key.T, value.T
            heads_t, query_t, d_keys, d_values = [], [], [], []
            for head in range(2):
                mask = first_half if head == 0 else ~first_half
                only_key = jnp.where(mask, key, jnp.zeros_like(key))
                only_value = jnp.where(mask, value, jnp.zeros_like(value))
                scores = jnp.where(allowed, dot_rt(only_key, query) * scale, -1e30)
                top = jnp.max(scores, axis=0, keepdims=True)
                weights = jnp.exp(scores - top)
                probs = weights * (1.0 / jnp.sum(weights, axis=0, keepdims=True))
                probs_b = probs.astype(BF)
                d_probs = dot_rt(only_value, d_out)
                delta = jnp.sum(probs * d_probs, axis=0, keepdims=True)
                d_scores = (probs * (d_probs - delta)).astype(BF)
                heads_t.append(dot(value_t[head * HD : (head + 1) * HD], probs_b))
                query_t.append(dot(key_t[head * HD : (head + 1) * HD], d_scores))
                d_keys.append(dot(d_scores, query))
                d_values.append(dot(probs_b, d_out))
            heads_ref[:, lo:hi] = jnp.concatenate(heads_t, axis=0).T.astype(BF)
            d_query = turn(jnp.concatenate(query_t, axis=0).T * scale, -1.0)
            d_key = turn(jnp.where(first_half, d_keys[0], d_keys[1]) * scale, -1.0)
            d_value = jnp.where(first_half, d_values[0], d_values[1])
            for p, item in enumerate((d_query, d_key, d_value)):
                proj_ref[:, p * wide + lo : p * wide + hi] = item.astype(BF)
                bias_ref[0:1, p * wide + lo : p * wide + hi] += jnp.sum(item, axis=0, keepdims=True)

    in_specs = (
        [by_row((rows, width)), by_row((rows, width)), by_row((rows, LANES)), by_row((rows, LANES))]
        + [full(lens.shape), full(vec.shape)]
        + [full((half, 3 * wide))] * (1 + 2 * (groups - 1))
        + [full(w_out.shape)]
    )
    outs = [
        ((tok, wide), BF, by_row((rows, wide))),
        ((tok, 3 * wide), BF, by_row((rows, 3 * wide))),
        ((8, 3 * wide), F32, full((8, 3 * wide))),
        ((width, 3 * wide), BF, full((width, 3 * wide))),
    ]
    return kernel_call(body, (groups,), in_specs, outs, (), 0.0)(
        sc, in_attn, branch, cosine, sine, lens, vec, own, *mine, *other, w_out
    )


def back_to_tokens(sc, xs, heads, mlp, d_proj, d_up, stats, vec, w_out, w_qkv, w_up, bias_up, bias_qkv, bias_out):
    groups, n_x = len(xs), len(flat(xs))
    rows, width = xs[0][0].shape
    wide = width // groups
    ff = d_up.shape[1]

    def body(s_ref, *refs):
        x_refs, refs = refs[:n_x], refs[n_x:]
        (
            heads_ref, mlp_ref, proj_ref, d_up_ref, stats_ref, vec_ref, wo_ref, wq_ref, wu_ref,
            up_ref, qkv_ref, out_ref,
        ) = refs[:12]
        own_ref = refs[12]
        piece_refs = refs[13 : 12 + groups]
        grad_ref, x_scr = refs[12 + groups :]
        me = s_ref[0]
        block = pl.program_id(0)
        load_block(block, xs, x_refs, x_scr)

        @pl.when(block == 0)
        def _():
            grad_ref[...] = jnp.zeros_like(grad_ref)
            grad_ref[4:6, :] = out_ref[0:2, :]
            for p in range(3):
                grad_ref[6 + p : 7 + p, part(me * wide, wide)] = qkv_ref[0:1, p * wide : (p + 1) * wide]
            first = me * ff
            grad_ref[pl.ds(9 + first // width, 1), part(lax.rem(me, width // ff) * ff, ff, LANES)] = up_ref[0:1, :]

        normed = (x_scr[...].astype(F32) - stats_ref[:, 0:1]) * stats_ref[:, 1:2]
        branch_out = dot(heads_ref[...], wo_ref[...]) + mlp_ref[...].astype(F32)
        total = None
        for row, left, right in ((0, proj_ref, wq_ref), (2, d_up_ref, wu_ref)):
            d_in = dot_rt(left[...], right[...])
            grad_ref[row : row + 1, :] += jnp.sum(d_in * normed, axis=0, keepdims=True)
            grad_ref[row + 1 : row + 2, :] += jnp.sum(d_in, axis=0, keepdims=True)
            term = d_in * vec_ref[row : row + 1, :]
            total = term if total is None else total + term

        @pl.when(block == 0)
        def _():
            own_ref[:, :width] = branch_out.astype(BF)
            own_ref[:, width:] = total.astype(BF)

        for step in range(1, groups):

            @pl.when(block == step)
            def _(step=step):
                piece_refs[step - 1][:, :width] = branch_out.astype(BF)
                piece_refs[step - 1][:, width:] = total.astype(BF)

    constant = [vec, w_out, w_qkv, w_up, bias_up, bias_qkv, bias_out]
    in_specs = (
        [full(item.shape) for item in flat(xs)]
        + [by_row((rows, item.shape[1])) for item in (heads, mlp, d_proj, d_up, stats)]
        + [full(item.shape) for item in constant]
    )
    outs = [((rows, 2 * width), BF, full((rows, 2 * width)))]
    outs += [((rows, 2 * width), BF, full((rows, 2 * width)))] * (groups - 1)
    outs += [((EXTRA, width), F32, full((EXTRA, width)))]
    got = kernel_call(
        body,
        (groups,),
        in_specs,
        outs,
        [pltpu.VMEM((rows, width), BF)],
        0.0,
    )(sc, *flat(xs), heads, mlp, d_proj, d_up, stats, *constant)
    return got[0], got[1:groups], got[groups]


def grads_of_attention(sc, in_attn, d_proj, heads, branch, scale, groups):
    tok, width = in_attn.shape
    wide = heads.shape[1]
    half = wide // 2

    def body(s_ref, a_ref, proj_ref, heads_ref, branch_ref, out_away, out_keep, qkv_away, qkv_keep):
        me, core = s_ref[0], s_ref[1]

        def piece(i, carry):
            grad = (dot_lt(a_ref[:, part((me ^ i) * wide, wide)], proj_ref[...]) * scale).astype(BF)
            qkv_keep[i], qkv_away[i] = halves(grad, core)
            return carry

        lax.fori_loop(0, groups, piece, 0)
        grad = (dot_lt(heads_ref[...], branch_ref[...]) * scale).astype(BF)
        out_keep[...], out_away[...] = halves(grad, core)

    ops = (in_attn, d_proj, heads, branch)
    out = ((half, width), BF, full(None))
    qkv = ((groups, half, 3 * wide), BF, full(None))
    return kernel_call(body, (1,), [full(None)] * len(ops), [out, out, qkv, qkv], (), 0.0)(sc, *ops)


def merge(sc, qkv_keep, qkv_got):
    groups, half, columns = qkv_keep.shape

    def body(s_ref, keep_ref, got_ref, stay_ref, away_ref):
        for i in range(groups):
            ref, at = (away_ref if i % 2 else stay_ref), i // 2 * half
            ref[at : at + half, :] = keep_ref[i] + got_ref[i]

    shape = jax.ShapeDtypeStruct((groups // 2 * half, columns), BF)
    return on_vmem(body, [shape, shape], sc, [qkv_keep, qkv_got])


def join(sc, qkv_rows, out_keep, out_got, vec_sum):
    groups = len(qkv_rows)
    half, width = out_keep.shape
    wide = 2 * half
    share = width // groups

    def body(s_ref, *refs):
        rows, (keep_ref, got_ref, vec_ref, out) = refs[:groups], refs[groups:]
        out[groups * half :, :] = jnp.zeros((EXTRA, 3 * wide + share), BF)
        for i in range(groups):
            at = slice(i * half, (i + 1) * half)
            columns = slice(i * share, (i + 1) * share)
            out[at, : 3 * wide] = rows[i][...]
            out[at, 3 * wide :] = keep_ref[:, columns] + got_ref[:, columns]
        out[groups * half :, :wide] = vec_ref[:, part(s_ref[0] * wide, wide)].astype(BF)

    shape = jax.ShapeDtypeStruct((groups * half + EXTRA, 3 * wide + share), BF)
    return on_vmem(body, [shape], sc, [*qkv_rows, out_keep, out_got, vec_sum])[0]


def sum_along(value, axis):
    size = lax.axis_size(axis)
    bit = 1
    while bit < size:
        value = value + lax.ppermute(value, axis, [(i, i ^ bit) for i in range(size)])
        bit *= 2
    return value


def finish(sc, own, got, left, right, tokens, cotangent, lens, stats, vec, slots):
    rows, width = tokens.shape

    def body(s_ref, own_ref, *refs):
        count = len(got) + 2 * len(left)
        got_refs, left_refs, right_refs = refs[: len(got)], refs[len(got) : len(got) + len(left)], refs[len(got) + len(left) : count]
        tok_ref, cot_ref, lens_ref, stats_ref, vec_ref, out_ref, grad_ref = refs[count:]
        branch = own_ref[:, :width].astype(F32)
        scaled = own_ref[:, width:].astype(F32)
        for ref in got_refs:
            branch = branch + ref[:, :width].astype(F32)
            scaled = scaled + ref[:, width:].astype(F32)
        for ref in left_refs:
            branch = branch + ref[...].astype(F32)
        for ref in right_refs:
            scaled = scaled + ref[...].astype(F32)
        size = branch.shape[0]
        _, ends = ends_of(lens_ref, 0, slots)
        index = index_of((size, 1), 0) + (pl.program_id(0) * size).astype(F32)
        valid = jnp.where(index < jnp.broadcast_to(ends[-1], (size, 1)), 1.0, 0.0)
        x = tok_ref[...].astype(F32)
        out_ref[...] = (x + valid * (branch + vec_ref[4:5, :] + vec_ref[5:6, :])).astype(BF)
        inv = stats_ref[:, 1:2]
        normed = (x - stats_ref[:, 0:1]) * inv
        d_tokens = inv * (
            scaled
            - jnp.mean(scaled, axis=1, keepdims=True)
            - normed * jnp.mean(scaled * normed, axis=1, keepdims=True)
        )
        grad_ref[...] = (cot_ref[...].astype(F32) + d_tokens).astype(BF)

    size = rows // 2
    in_specs = [by_row((size, 2 * width))] * (1 + len(got)) + [by_row((size, width))] * (2 * len(left) + 2)
    in_specs += [full(lens.shape), by_row((size, LANES)), full(vec.shape)]
    out = ((rows, width), BF, by_row((size, width)))
    return kernel_call(body, (2,), in_specs, [out, out], (), 2.4)(
        sc, own, *got, *left, *right, tokens, cotangent, lens, stats, vec
    )


def assemble(shapes, arrays, plan):
    def body(*refs):
        ins, outs = refs[: len(arrays)], refs[len(arrays) :]
        me, core = lax.axis_index("shard"), lax.rem(lax.axis_index("dp"), 2)
        for target, row, column, size, which, index in plan(me, core):
            outs[target][part(row, size[0]), part(column, size[1])] = ins[which][index]

    vmem = pl.BlockSpec(memory_space=pltpu.VMEM)
    return pl.pallas_call(
        body,
        out_shape=[jax.ShapeDtypeStruct(shape, arrays[0].dtype) for shape in shapes],
        in_specs=[vmem] * len(arrays),
        out_specs=[vmem] * len(shapes),
        compiler_params=pltpu.CompilerParams(vmem_limit_bytes=8 * MIB),
        cost_estimate=pl.CostEstimate(flops=0, bytes_accessed=int(3.2e6), transcendentals=0),
    )(*arrays)


def adam_blocks(sc, grads, masters, grid, block, where, fill, time):
    shape = masters[0].shape

    def body(s_ref, *refs):
        grad_refs = refs[: len(grads)]
        w_ref, m_ref, v_ref, g_out, w_out, m_out, v_out = refs[len(grads) :]
        fill(s_ref, grad_refs, g_out)
        w_out[...], m_out[...], v_out[...] = adam_terms(
            w_ref[...], m_ref[...], v_ref[...], g_out[...], DECAY_RATE, LEARN_RATE
        )

    spec = pl.BlockSpec(block, where)
    return kernel_call(
        body, grid, [full(None)] * len(grads) + [spec] * 3, [(shape, F32, spec)] * 4, (), time, 30
    )(sc, *grads, *masters)


def choose(condition, yes, no, out):
    @pl.when(condition)
    def _():
        out[...] = yes().astype(F32)

    @pl.when(jnp.logical_not(condition))
    def _():
        out[...] = no().astype(F32)


def adam(masters, grad, decay=DECAY_RATE, rate=LEARN_RATE):
    weight, first, second = masters
    grad = grad.astype(F32)
    return (grad,) + adam_terms(weight, first, second, grad, decay, rate)


def local(
    tokens, cotangent, lengths,
    w_qkv, w_out, w_up, w_down, vectors,
    m_qkv, m_out, m_up, m_down, m_vectors,
    v_qkv, v_out, v_up, v_down, v_vectors,
):
    groups = lax.axis_size("shard")
    me = lax.axis_index("shard")
    core = lax.axis_index("dp") % 2
    rows, width = tokens.shape
    hidden = w_up.shape[1]
    wide = width // groups
    half = wide // 2
    ff = hidden // groups
    n_vec = vectors.shape[0]
    slots = lengths.shape[1]
    others = range(1, groups)
    quarter = wide // 4
    places = lax.axis_size("dp") // 2
    place = lax.axis_index("dp") // 2
    outer = (place == 0) | (place == places - 1)
    sc = jnp.stack([me, core, outer, place % 2]).astype(jnp.int32)
    scale = float(rows * groups * lax.axis_size("dp")) ** (-0.5)

    size = ff // 2
    fence = lax.optimization_barrier

    up_parts, qkv_parts, down_w, out_w = pack(groups, sc, w_up, w_qkv, w_down, w_out, vectors, lengths)
    near = [shard_swap(tokens, step) for step in (1, 2)]
    near, up_parts = fence((near, up_parts))
    up_mine = [shard_swap(item, step) for item, step in zip(up_parts[1:], others, strict=True)]
    xs = gather_rest(tokens, near)
    cot_near = [shard_swap(after(cotangent, xs[3]), step) for step in (1, 2)]
    up_stack = jnp.concatenate([item[:quarter] for item in up_mine])
    up_side = place_send(up_stack, [(i, i ^ 1) for i in range(places)])
    up_other = [up_side, core_swap(up_stack), core_swap(up_side)]
    in_attn, in_mlp, act, slope, stats, up_w, vec, lens = forward_up(
        sc, xs, up_parts[0], up_mine, up_other, vectors, lengths
    )
    cot_near, act = fence((cot_near, act))
    cots = gather_rest(cotangent, cot_near)
    qkv_mine = [shard_swap(item, step) for item, step in zip(after(qkv_parts[1:], cot_near), others, strict=True)]
    cots, act = fence((cots, act))

    branch, bias_out = mask_rows(sc, cots, lens, slots)
    up_away, up_keep, d_up, bias_up = backward_up(sc, branch, slope, down_w, in_mlp, scale, groups)
    up_away, up_keep, qkv_mine, branch = fence((up_away, up_keep, qkv_mine, branch))
    up_got = core_swap(up_away)
    qkv_other = [core_swap(item) for item in qkv_mine]
    down_away, down_keep = grad_of_down(sc, branch, act, scale)
    down_away, down_keep, up_got, qkv_other = fence((down_away, down_keep, up_got, qkv_other))
    down_got = core_swap(down_away)
    cosine, sine = tables(sc, after(lens, down_away), groups, rows, slots)
    down = down_keep + down_got
    down, branch_a, up_got, cosine = fence((down, branch, up_got, cosine))

    down, _, _ = dp_round(sc, down, None, None)
    up_sums = [up_keep[i] + up_got[i] for i in range(groups)]
    up_sums, branch_a = fence((up_sums, branch_a))
    up_rows = [up_sums[0]] + [shard_swap(up_sums[step], step) for step in others]
    heads, d_proj, bias_qkv, qkv_w = attention(
        sc, in_attn, branch_a, cosine, sine, lens, vec, qkv_parts[0], qkv_mine, qkv_other, out_w, groups, slots
    )
    out_away, out_keep, qkv_away, qkv_keep = grads_of_attention(sc, in_attn, d_proj, heads, branch, scale, groups)
    up_rows, out_away, qkv_away = fence((up_rows, out_away, qkv_away))
    qkv_got = core_swap(qkv_away)
    out_got = core_swap(out_away)
    mlp = feed_out(sc, after(act, out_away), down_w, groups)
    down, up_rows, qkv_got, out_got, d_proj, mlp = fence((down, up_rows, qkv_got, out_got, d_proj, mlp))
    up = jnp.concatenate(up_rows)
    stay, away = merge(sc, qkv_keep, qkv_got)
    up, down, stay, away, d_proj = fence((up, down, stay, away, d_proj))

    qkv_rows = exchange(stay, away)
    own, pieces, vec_grad = back_to_tokens(
        sc, xs, heads, mlp, d_proj, d_up, stats, vec, out_w, qkv_w, up_w, bias_up, bias_qkv, bias_out
    )
    vec_sum = sum_along(vec_grad * scale, "shard")
    rest = join(sc, qkv_rows, out_keep, out_got, vec_sum)
    up, down, _ = dp_round(sc, up, down, None, rest)
    down, up, rest, pieces = fence((down, up, rest, pieces))

    rest, up, down = dp_round(sc, rest, up, down, rows=size)
    got = [shard_swap(item, step) for item, step in zip(pieces[:2], (1, 2), strict=True)]
    down, up, rest, got, pieces = fence((down, up, rest, got, pieces))

    down_other = core_swap(down)
    _, rest, up = dp_round(sc, None, rest, up)
    left = [shard_swap(item[:, :width], step) for item, step in zip(pieces[2:], others[2:], strict=True)]

    def fill_down(s_ref, refs, out):
        step = pl.program_id(0)
        at = part((step % 2) * (size // 2), size // 2)
        choose(step // 2 == s_ref[1], lambda: refs[0][at, :], lambda: refs[1][at, :], out)

    new_down = adam_blocks(
        sc, [down, down_other], (w_down, m_down, v_down),
        (4,), (size // 2, width), lambda i, s: (i, 0), fill_down, 0.0,
    )
    up, rest, new_down, left, pieces = fence((up, rest, new_down, left, pieces))
    right = [shard_swap(item[:, width:], step) for item, step in zip(pieces[2:], others[2:], strict=True)]

    up_other = core_swap(up)
    _, _, rest = dp_round(sc, None, None, rest)

    def fill_up(s_ref, refs, out):
        at = part((s_ref[0] ^ pl.program_id(1)) * half, half)
        choose(pl.program_id(0) == s_ref[1], lambda: refs[0][at, :], lambda: refs[1][at, :], out)

    new_up = adam_blocks(
        sc, [up, up_other], (w_up, m_up, v_up),
        (2, groups), (half, ff), lambda i, j, s: (i, j), fill_up, 0.0,
    )
    output, input_grad = finish(
        sc, own, got, left, after(right, new_up), tokens, cotangent, lens, stats, vec, slots
    )
    rest, new_up, output, input_grad = fence((rest, new_up, output, input_grad))
    rest_other = core_swap(rest)

    def rest_plan(me, core):
        plan = []
        for side in range(2):
            row = (core ^ side) * half
            for step in range(groups):
                at = slice(step * half, (step + 1) * half)
                for p in range(3):
                    columns = slice(p * wide, (p + 1) * wide)
                    plan.append((0, row, p * width + (me ^ step) * wide, (half, wide), side, (at, columns)))
                columns = slice(3 * wide, 4 * wide)
                plan.append((1, row, step * wide, (half, wide), side, (at, columns)))
        return plan

    qkv_grad, out_grad = assemble([(wide, 3 * width), (wide, width)], [rest, rest_other], rest_plan)
    vec_rows = slice(groups * half, groups * half + n_vec)
    vec_total = rest[vec_rows, :wide].astype(F32) + rest_other[vec_rows, :wide].astype(F32)

    news = (
        adam((w_qkv, m_qkv, v_qkv), qkv_grad),
        adam((w_out, m_out, v_out), out_grad),
        new_up,
        new_down,
        adam((vectors, m_vectors, v_vectors), vec_total, 0.0, VECTOR_RATE),
    )
    return (output, input_grad) + tuple(item[kind] for kind in range(4) for item in news)


def solution(mesh):
    by_token = P(("shard", "dp"), None)
    params = (P("shard", None),) * 4 + (P(None, "shard"),)
    return jax.shard_map(
        local,
        mesh=mesh,
        in_specs=(by_token,) * 3 + params * 3,
        out_specs=(by_token,) * 2 + params * 4,
        check_vma=False,
    )
```

```python
import functools
import math

import jax
import jax.numpy as jnp
from jax import lax
from jax.experimental import pallas as pl
from jax.experimental.pallas import tpu as pltpu
from jax.sharding import PartitionSpec as P

H = 16
HD = 64
ROT = 16
ADAM_STEP = 4


EPS_NORM = 1e-05
BETA_ONE = 0.9
BETA_TWO = 0.95
ADAM_EPS = 1e-08
LEARN_RATE = 0.01
VECTOR_RATE = 0.1
DECAY_RATE = 0.1
SQRT_HALF = 0.7071067811865476
INV_ROOT_TWO_PI = 0.3989422804014327

BF = jnp.bfloat16
F32 = jnp.float32
EXTRA = 16
LANES = 128
MIB = 2**20


def dot(left, right):
    return jnp.dot(left, right, preferred_element_type=F32)


def dot_lt(left, right):
    return lax.dot_general(left, right, (((0,), (0,)), ((), ())), preferred_element_type=F32)


def dot_rt(left, right):
    return lax.dot_general(left, right, (((1,), (1,)), ((), ())), preferred_element_type=F32)


def part(start, size, multiple=None):
    return pl.ds(pl.multiple_of(start, multiple or size), size)


def shard_swap(value, step):
    size = lax.axis_size("shard")
    return lax.ppermute(value, "shard", [(i, i ^ step) for i in range(size)])


def exchange(stay, away):
    size = lax.axis_size("shard")
    rows = stay.shape[0] // (size // 2)
    got = shard_swap(away, 1)
    pieces = [(got if step % 2 else stay)[step // 2 * rows : (step // 2 + 1) * rows] for step in range(size)]
    bit = 2
    while bit < size:
        sent = [step for step in range(size) if step & bit]
        got = shard_swap(jnp.concatenate([pieces[step] for step in sent]), bit)
        for i, step in enumerate(sent):
            pieces[step] = got[i * rows : (i + 1) * rows]
        bit *= 2
    return pieces


def core_swap(value):
    size = lax.axis_size("dp")
    return lax.ppermute(value, "dp", [(i, i ^ 1) for i in range(size)])


def chain_stages():
    places = lax.axis_size("dp") // 2
    half = places // 2
    if places == 1:
        return []
    stages = []
    for step in range(half - 1):
        stages.append(([(step, step + 1), (places - 1 - step, places - 2 - step)], None))
    stages.append(([(half - 1, half), (half, half - 1)], None))
    for step in reversed(range(half - 1)):
        stages.append(
            ([(step + 1, step), (places - 2 - step, places - 1 - step)], (step, places - 1 - step))
        )
    return stages


def place_send(value, pairs):
    return lax.ppermute(
        value, "dp", [(2 * a + core, 2 * b + core) for a, b in pairs for core in range(2)]
    )


def after(value, *earlier):
    return lax.optimization_barrier((value, earlier))[0]


def combine(items):
    def body(flag_ref, *refs):
        count = len(items)
        for i, (_, _, taker) in enumerate(items):
            value, got, out = refs[2 * i], refs[2 * i + 1], refs[2 * count + i]
            if taker is None:
                out[...] = value[...] + got[...]
            else:
                out[...] = jnp.where(flag_ref[i] > 0, got[...], value[...])

    flags = [jnp.int32(0) if taker is None else taker.astype(jnp.int32) for _, _, taker in items]
    vmem = pl.BlockSpec(memory_space=pltpu.VMEM)
    return pl.pallas_call(
        body,
        out_shape=[jax.ShapeDtypeStruct(value.shape, value.dtype) for value, _, _ in items],
        in_specs=[pl.BlockSpec(memory_space=pltpu.SMEM)] + [vmem] * (2 * len(items)),
        out_specs=[vmem] * len(items),
        compiler_params=pltpu.CompilerParams(vmem_limit_bytes=12 * MIB),
        cost_estimate=pl.CostEstimate(flops=0, bytes_accessed=int(3.2e6), transcendentals=0),
    )(jnp.stack(flags), *[item for value, got, _ in items for item in (value, got)])


def advance(*moves):
    values = [value for value, _ in moves]
    depth = max(len(stages) for _, stages in moves)
    for step in range(depth):
        active = [i for i, (_, stages) in enumerate(moves) if step < len(stages)]
        items = []
        for i in active:
            pairs, takers = moves[i][1][step]
            flag = None
            if takers is not None:
                place = lax.axis_index("dp") // 2
                flag = functools.reduce(jnp.logical_or, [place == taker for taker in takers])
            items.append((values[i], place_send(values[i], pairs), flag))
        for i, item in zip(active, combine(items), strict=True):
            values[i] = item
    return values


def chain_parts():
    stages = chain_stages()
    half = (len(stages) + 1) // 2
    if not stages:
        return [], [], []
    return stages[: half - 1], stages[half - 1 : half], stages[half:]


def dp_round(sc, fresh, inner, total, upcoming=None, rows=None):
    parts = chain_parts()
    if lax.axis_size("dp") // 2 != 4:
        moves = [(value, stages) for value, stages in zip((fresh, inner, total), parts, strict=True) if value is not None]
        moved = iter(advance(*moves))
        return [None if value is None else next(moved) for value in (fresh, inner, total)]
    if fresh is None:
        sent, pairs = total, [(1, 0), (2, 3)]
    elif total is None:
        sent, pairs = fresh, [(0, 1), (3, 2)]
    else:
        sent, pairs = total, [(0, 1), (1, 0), (2, 3), (3, 2)]
    edge = place_send(sent, pairs)
    centre = None if inner is None else place_send(inner, [(1, 2), (2, 1)])
    arrays, shapes, steps = [], [], []

    def plan(kind, items, shape):
        steps.append((kind, len(arrays), len(shapes)))
        arrays.extend(items)
        shapes.append(shape)

    if fresh is not None:
        plan("sum", [fresh, edge], fresh)
    if inner is not None and upcoming is None:
        plan("sum", [inner, centre], inner)
    if inner is not None and upcoming is not None:
        plan("next", [inner, centre, upcoming], max(inner, upcoming, key=lambda item: item.shape[0]))
    if total is not None:
        shape = total if rows is None else jax.ShapeDtypeStruct((rows, total.shape[1]), total.dtype)
        plan("last", [total, edge], shape)

    def body(s_ref, *refs):
        outs = refs[len(arrays) :]
        for kind, at, place in steps:
            value, got, out = refs[at], refs[at + 1], outs[place]
            size = min(value.shape[0], out.shape[0])
            if kind == "sum":
                out[...] = value[...] + got[:size, :]
                continue

            @pl.when(s_ref[2] == 0)
            def _(kind=kind, value=value, got=got, out=out, size=size):
                out[:size, :] = value[:size, :] + got[:size, :] if kind == "next" else value[:size, :]

            @pl.when(s_ref[2] > 0)
            def _(kind=kind, got=got, out=out, at=at, size=size):
                if kind == "next":
                    out[: refs[at + 2].shape[0], :] = refs[at + 2][...]
                else:
                    out[...] = got[:size, :]

    moved = iter(on_vmem(body, shapes, sc, arrays))
    return [None if value is None else next(moved) for value in (fresh, inner, total)]


def on_vmem(body, shapes, sc, arrays, limit=8):
    vmem = pl.BlockSpec(memory_space=pltpu.VMEM)
    return pl.pallas_call(
        body,
        out_shape=[jax.ShapeDtypeStruct(item.shape, item.dtype) for item in shapes],
        in_specs=[pl.BlockSpec(memory_space=pltpu.SMEM)] + [vmem] * len(arrays),
        out_specs=[vmem] * len(shapes),
        compiler_params=pltpu.CompilerParams(vmem_limit_bytes=limit * MIB),
        cost_estimate=pl.CostEstimate(flops=0, bytes_accessed=int(3.2e6), transcendentals=0),
    )(sc, *arrays)


def gather_rest(block, near):
    groups = lax.axis_size("shard")
    rows = block.shape[0]
    got = [[block], [near[0]], [near[1]]]
    got.append([shard_swap(near[0][: rows // 2], 2), shard_swap(near[1][rows // 2 :], 1)])
    for step in range(4, groups):
        got.append([shard_swap(block, step)])
    return got


def whole():
    return pl.BlockSpec(memory_space=pltpu.VMEM)


def full(shape):
    return pl.BlockSpec(memory_space=pltpu.VMEM)


def by_row(shape):
    return pl.BlockSpec(shape, lambda i, *_: (i,) + (0,) * (len(shape) - 1))


def kernel_call(body, grid, in_specs, outs, scratch=(), time=1.0, limit=12):
    return pl.pallas_call(
        body,
        out_shape=[jax.ShapeDtypeStruct(shape, dtype) for shape, dtype, _ in outs],
        grid_spec=pltpu.PrefetchScalarGridSpec(
            num_scalar_prefetch=1,
            grid=grid,
            in_specs=in_specs,
            out_specs=[spec for _, _, spec in outs],
            scratch_shapes=list(scratch),
        ),
        compiler_params=pltpu.CompilerParams(vmem_limit_bytes=limit * MIB),
        cost_estimate=pl.CostEstimate(flops=0, bytes_accessed=int(3.2e6 * time), transcendentals=0),
    )


def flat(blocks):
    return [piece for block in blocks for piece in block]


def load_block(block, blocks, refs, scratch):
    at = 0
    for step, pieces in enumerate(blocks):
        mine = refs[at : at + len(pieces)]
        at += len(pieces)

        @pl.when(block == step)
        def _(mine=mine):
            row = 0
            for ref in mine:
                scratch[row : row + ref.shape[0], :] = ref[...]
                row += ref.shape[0]


def halves(value, core):
    size = value.shape[0] // 2
    first, second = value[:size], value[size:]
    return jnp.where(core == 0, first, second), jnp.where(core == 0, second, first)


def ends_of(lens_ref, block, slots):
    lengths = [lens_ref[block, 0:1, k : k + 1] for k in range(slots)]
    ends = []
    for item in lengths:
        ends.append(item if not ends else ends[-1] + item)
    return lengths, ends


def segments(index, ends):
    total = jnp.zeros(index.shape, F32)
    for end in ends:
        total = total + jnp.where(jnp.broadcast_to(end, index.shape) <= index, 1.0, 0.0)
    return total


def index_of(shape, axis):
    return lax.broadcasted_iota(jnp.int32, shape, axis).astype(F32)


def gelu_parts(values):
    gate = 0.5 * (1.0 + lax.erf(values * SQRT_HALF))
    slope = gate + values * jnp.exp(-0.5 * values * values) * INV_ROOT_TWO_PI
    return values * gate, slope


def adam_terms(weight, first, second, grad, decay, rate):
    corr_one = 1.0 - math.exp(ADAM_STEP * math.log(BETA_ONE))
    corr_two = 1.0 - math.exp(ADAM_STEP * math.log(BETA_TWO))
    first_new = BETA_ONE * first + (1.0 - BETA_ONE) * grad
    second_new = BETA_TWO * second + (1.0 - BETA_TWO) * grad * grad
    step_size = (first_new * (1.0 / corr_one)) / (jnp.sqrt(second_new * (1.0 / corr_two)) + ADAM_EPS)
    return weight - rate * (step_size + decay * weight), first_new, second_new


def pack(groups, sc, w_up, w_qkv, w_down, w_out, vectors, lengths):
    wide, hidden = w_up.shape
    half, quarter, ff = wide // 2, wide // 4, hidden // groups
    n_vec, slots = vectors.shape[0], lengths.shape[1]

    def body(s_ref, up_hbm, qkv_hbm, down_hbm, out_hbm, vec_ref, len_ref, *refs):
        out, (down_out, out_out) = refs[: 2 * groups], refs[2 * groups : 2 * groups + 2]
        up_scr, qkv_scr, down_scr, out_scr, sems, more = refs[2 * groups + 2 :]
        me, core = s_ref[0], s_ref[1]
        rest = [
            pltpu.make_async_copy(down_hbm, down_scr, more.at[0]),
            pltpu.make_async_copy(out_hbm, out_scr, more.at[1]),
        ]
        copies = []
        for step in range(groups):
            size = wide if step == 0 else quarter
            rows = pl.ds(0, wide) if step == 0 else part((2 * s_ref[3] + core) * quarter, quarter)
            owner = me ^ step
            at = pl.ds(0 if step == 0 else wide + (step - 1) * quarter, size)
            mine = [pltpu.make_async_copy(up_hbm.at[rows, part(owner * ff, ff)], up_scr.at[at], sems.at[step, 0])]
            size = wide if step == 0 else half
            rows = pl.ds(0, wide) if step == 0 else part(core * half, half)
            at = pl.ds(0 if step == 0 else wide + (step - 1) * half, size)
            for p in range(3):
                mine.append(
                    pltpu.make_async_copy(
                        qkv_hbm.at[rows, part(p * groups * wide + owner * wide, wide)],
                        qkv_scr.at[at, pl.ds(p * wide, wide)],
                        sems.at[step, 1 + p],
                    )
                )
            copies.append(mine)
        order = list(range(1, groups)) + [0]
        for step in order:
            for copy in copies[step]:
                copy.start()
        for copy in rest:
            copy.start()
        for step in order:
            for copy in copies[step]:
                copy.wait()
            up_out, qkv_out = out[2 * step], out[2 * step + 1]
            if step == 0:
                up_out[...] = up_scr[:wide].astype(BF)
                qkv_out[...] = qkv_scr[:wide].astype(BF)
                continue
            at = wide + (step - 1) * quarter
            up_out[:quarter, :] = up_scr[at : at + quarter].astype(BF)
            up_out[quarter:, :] = jnp.zeros((EXTRA, ff), BF)
            up_out[quarter : quarter + n_vec, :wide] = vec_ref[...].astype(BF)
            up_out[quarter + n_vec : quarter + n_vec + 1, :slots] = len_ref[...].astype(F32).astype(BF)
            at = wide + (step - 1) * half
            qkv_out[...] = qkv_scr[at : at + half].astype(BF)
        for copy in rest:
            copy.wait()
        down_out[...] = down_scr[...].astype(BF)
        out_out[...] = out_scr[...].astype(BF)

    in_specs = [pl.BlockSpec(memory_space=pltpu.HBM)] * 4 + [full(vectors.shape), full(lengths.shape)]
    outs = []
    for step in range(groups):
        size = wide if step == 0 else half
        outs.append(((wide if step == 0 else quarter + EXTRA, ff), BF, full(None)))
        outs.append(((size, 3 * wide), BF, full(None)))
    outs += [(w_down.shape, BF, full(None)), (w_out.shape, BF, full(None))]
    rows = wide + (groups - 1) * half
    scratch = [pltpu.VMEM((wide + (groups - 1) * quarter, ff), F32), pltpu.VMEM((rows, 3 * wide), F32)]
    scratch += [pltpu.VMEM(w_down.shape, F32), pltpu.VMEM(w_out.shape, F32)]
    scratch += [pltpu.SemaphoreType.DMA((groups, 4)), pltpu.SemaphoreType.DMA((2,))]
    got = kernel_call(body, (1,), in_specs, outs, scratch, 7.0, 60)(sc, w_up, w_qkv, w_down, w_out, vectors, lengths)
    return got[0 : 2 * groups : 2], got[1 : 2 * groups : 2], got[2 * groups], got[2 * groups + 1]


def tables(sc, lens, groups, rows, slots):
    def body(s_ref, lens_ref, cos_ref, sin_ref):
        lane = lax.broadcasted_iota(jnp.int32, (8, LANES), 1) % HD
        pair = (lane % (ROT // 2)).astype(F32)
        freq = jnp.where(lane < ROT, jnp.exp(-pair * (2.0 * math.log(10000.0) / ROT)), 0.0)[0:1, :]
        index = index_of((rows, LANES), 0)
        angle = index * freq
        cos_index, sin_index = jnp.cos(angle), jnp.sin(angle)
        for block in range(groups):
            lengths, ends = ends_of(lens_ref, block, slots)
            cos_start = jnp.ones((rows, LANES), F32)
            sin_start = jnp.zeros((rows, LANES), F32)
            for length, end in zip(lengths, ends, strict=True):
                turn = jnp.broadcast_to(end, (8, LANES)) * jnp.broadcast_to(freq, (8, LANES))
                inside = jnp.broadcast_to(end, index.shape) <= index
                cos_start = jnp.where(inside, jnp.cos(turn)[0:1, :], cos_start)
                sin_start = jnp.where(inside, jnp.sin(turn)[0:1, :], sin_start)
            at = slice(block * rows, (block + 1) * rows)
            cos_ref[at, :] = cos_index * cos_start + sin_index * sin_start
            sin_ref[at, :] = sin_index * cos_start - cos_index * sin_start

    out = ((groups * rows, LANES), F32, full(None))
    return kernel_call(body, (1,), [full(lens.shape)], [out, out], (), 1.5)(sc, lens)


def forward_up(sc, xs, own, mine, other, vectors, lengths):
    groups, n_x = len(xs), len(flat(xs))
    rows, width = xs[0][0].shape
    wide, ff = own.shape
    quarter = wide // 4
    n_vec, slots = vectors.shape[0], lengths.shape[1]
    tok = groups * rows

    def body(s_ref, *refs):
        x_refs, refs = refs[:n_x], refs[n_x:]
        own_ref = refs[0]
        mine_refs = refs[1:groups]
        other_refs = refs[groups : groups + 3]
        vec_in, len_in = refs[groups + 3 : groups + 5]
        attn_ref, mlp_ref, act_ref, slope_ref, stats_ref, w_ref, vec_ref, lens_ref, x_scr = refs[groups + 5 :]
        me, core, side = s_ref[0], s_ref[1], s_ref[3]
        block = pl.program_id(0)

        @pl.when(block == 0)
        def _():
            w_ref[part(me * wide, wide), :] = own_ref[...]
            vec_ref[...] = jnp.zeros_like(vec_ref)
            lens_ref[...] = jnp.zeros_like(lens_ref)
            vec_ref[0:n_vec, part(me * wide, wide)] = vec_in[...].astype(BF).astype(F32)
            lens_ref[0, 0:1, 0:slots] = len_in[...].astype(F32)
            for step in range(1, groups):
                at = (me ^ step) * wide
                w_ref[part(at + (2 * side + core) * quarter, quarter), :] = mine_refs[step - 1][:quarter, :]
                for ref, which in zip(
                    other_refs, (2 * (1 - side) + core, 2 * side + 1 - core, 2 * (1 - side) + 1 - core), strict=True
                ):
                    w_ref[part(at + which * quarter, quarter), :] = ref[(step - 1) * quarter : step * quarter, :]
                vec_ref[0:n_vec, part(at, wide)] = mine_refs[step - 1][quarter : quarter + n_vec, :wide].astype(F32)
                lens_ref[step, 0:1, 0:slots] = mine_refs[step - 1][
                    quarter + n_vec : quarter + n_vec + 1, :slots
                ].astype(F32)

        load_block(block, xs, x_refs, x_scr)
        x = x_scr[...].astype(F32)
        mean = jnp.mean(x, axis=1, keepdims=True)
        centred = x - mean
        inv = lax.rsqrt(jnp.mean(centred * centred, axis=1, keepdims=True) + EPS_NORM)
        normed = centred * inv
        lane = lax.broadcasted_iota(jnp.int32, (rows, LANES), 1)
        stats_ref[...] = jnp.where(lane == 0, mean, inv)
        attn_ref[...] = (normed * vec_ref[0:1, :] + vec_ref[1:2, :]).astype(BF)
        in_mlp = (normed * vec_ref[2:3, :] + vec_ref[3:4, :]).astype(BF)
        mlp_ref[...] = in_mlp
        first = me * ff
        bias = vec_ref[pl.ds(9 + first // width, 1), part(lax.rem(me, width // ff) * ff, ff, LANES)]
        act, slope = gelu_parts(dot(in_mlp, w_ref[...]) + bias)
        act_ref[...] = act.astype(BF)
        slope_ref[...] = slope

    in_specs = (
        [full(item.shape) for item in flat(xs)]
        + [full(own.shape)]
        + [full(None)] * (groups + 2)
        + [full(vectors.shape), full(lengths.shape)]
    )
    outs = [
        ((tok, width), BF, by_row((rows, width))),
        ((tok, width), BF, by_row((rows, width))),
        ((tok, ff), BF, by_row((rows, ff))),
        ((tok, ff), F32, by_row((rows, ff))),
        ((tok, LANES), F32, by_row((rows, LANES))),
        ((width, ff), BF, full((width, ff))),
        ((EXTRA, width), F32, full((EXTRA, width))),
        ((groups, 8, LANES), F32, full((groups, 8, LANES))),
    ]
    return kernel_call(
        body, (groups,), in_specs, outs, [pltpu.VMEM((rows, width), BF)], 6.5, 20
    )(sc, *flat(xs), own, *mine, *other, vectors, lengths)


def grad_of_down(sc, branch, act, scale):
    tok, width = branch.shape
    size = act.shape[1] // 2

    def body(s_ref, branch_ref, act_ref, away_ref, keep_ref):
        core = s_ref[1]
        for ref, which in ((away_ref, 1 - core), (keep_ref, core)):
            ref[...] = (dot_lt(act_ref[:, part(which * size, size)], branch_ref[...]) * scale).astype(BF)

    outs = [((size, width), BF, full(None))] * 2
    return kernel_call(body, (1,), [full(branch.shape), full(act.shape)], outs, (), 3.0)(sc, branch, act)


def feed_out(sc, act, w_down, groups):
    tok, ff = act.shape
    rows = tok // groups

    def body(s_ref, act_ref, wd_ref, out_ref):
        out_ref[...] = dot(act_ref[...], wd_ref[...]).astype(BF)

    width = w_down.shape[1]
    outs = [((tok, width), BF, by_row((rows, width)))]
    return kernel_call(body, (groups,), [by_row((rows, ff)), full(None)], outs, (), 3.0)(sc, act, w_down)[0]


def backward_up(sc, cots, lens, slots, slope, w_down, in_mlp, scale):
    groups, n_c = len(cots), len(flat(cots))
    rows, width = cots[0][0].shape
    tok = groups * rows
    ff = slope.shape[1]
    half = width // groups // 2

    def body(s_ref, *refs):
        cot_refs, refs = refs[:n_c], refs[n_c:]
        lens_ref, slope_ref, wd_ref, mlp_ref, branch_ref, sum_ref, away_ref, keep_ref, up_ref, bias_ref, scratch = refs
        me, core = s_ref[0], s_ref[1]
        block = pl.program_id(0)

        @pl.when(block == 0)
        def _():
            bias_ref[...] = jnp.zeros_like(bias_ref)

        load_block(block, cots, cot_refs, scratch)
        total = jnp.zeros((1, 1), F32)
        for slot in range(slots):
            total = total + lens_ref[block, 0:1, slot : slot + 1]
        valid = jnp.where(index_of((rows, 1), 0) < jnp.broadcast_to(total, (rows, 1)), 1.0, 0.0)
        branch_f = scratch[...].astype(F32) * valid
        branch = branch_f.astype(BF)
        branch_ref[...] = branch

        @pl.when(block == 0)
        def _():
            sum_ref[...] = jnp.broadcast_to(jnp.sum(branch_f, axis=0, keepdims=True), sum_ref.shape)

        d_up = dot_rt(branch, wd_ref[...]) * slope_ref[...]
        bias_ref[0:1, :] += jnp.sum(d_up, axis=0, keepdims=True)
        up_ref[part(block * rows, rows), :] = d_up.astype(BF)

        @pl.when(block == groups - 1)
        def _():
            def piece(i, carry):
                grad = (dot_lt(mlp_ref[:, part((me ^ i) * (2 * half), 2 * half)], up_ref[...]) * scale).astype(BF)
                keep_ref[i], away_ref[i] = halves(grad, core)
                return carry

            lax.fori_loop(0, groups, piece, 0)

    in_specs = [full(None)] * (n_c + 1) + [by_row((rows, ff)), full(w_down.shape), full(in_mlp.shape)]
    outs = [
        ((tok, width), BF, by_row((rows, width))),
        ((8, width), F32, full(None)),
        ((groups, half, ff), BF, full((groups, half, ff))),
        ((groups, half, ff), BF, full((groups, half, ff))),
        ((tok, ff), BF, full((tok, ff))),
        ((8, ff), F32, full((8, ff))),
    ]
    return kernel_call(body, (groups,), in_specs, outs, [pltpu.VMEM((rows, width), BF)], 6.8)(
        sc, *flat(cots), lens, slope, w_down, in_mlp
    )


def attention(sc, in_attn, branch, cosine, sine, lens, vec, own, mine, other, w_out, groups, slots):
    tok, width = in_attn.shape
    rows = tok // groups
    wide = width // groups
    half = wide // 2
    scale = HD ** (-0.5)

    def body(s_ref, *refs):
        a_ref, branch_ref, cos_ref, sin_ref, lens_ref, vec_ref = refs[:6]
        own_ref = refs[6]
        mine_refs = refs[7 : 6 + groups]
        other_refs = refs[6 + groups : 5 + 2 * groups]
        wo_ref, heads_ref, proj_ref, bias_ref, w_ref = refs[5 + 2 * groups :]
        me, core = s_ref[0], s_ref[1]
        block = pl.program_id(0)

        @pl.when(block == 0)
        def _():
            w_ref[part(me * wide, wide), :] = own_ref[...]
            for step in range(1, groups):
                at = (me ^ step) * wide
                w_ref[part(at + core * half, half), :] = mine_refs[step - 1][...]
                w_ref[part(at + (1 - core) * half, half), :] = other_refs[step - 1][...]
            bias_ref[...] = jnp.zeros_like(bias_ref)

        bias = [vec_ref[6 + p : 7 + p, part(me * wide, wide)] for p in range(3)]
        projected = dot(a_ref[...], w_ref[...])
        d_heads = dot_rt(branch_ref[...], wo_ref[...]).astype(BF)
        _, ends = ends_of(lens_ref, block, slots)
        key_index = index_of((rows, 1), 0)
        query_index = index_of((1, rows), 1)
        allowed = (segments(key_index, ends) == segments(query_index, ends)) & (key_index <= query_index)
        lane = lax.broadcasted_iota(jnp.int32, (rows, LANES), 1)
        cosine, sine = cos_ref[...], sin_ref[...]
        low = jnp.where(lane % HD < ROT // 2, sine, 0.0)
        high = jnp.where(lane % HD >= ROT // 2, sine, 0.0)

        def turn(values, sign):
            ahead = pltpu.roll(values, LANES - ROT // 2, 1)
            behind = pltpu.roll(values, ROT // 2, 1)
            return values * cosine + sign * (behind * high - ahead * low)

        first_half = lane < HD
        for pair in range(wide // LANES):
            lo, hi = pair * LANES, (pair + 1) * LANES
            query = turn(projected[:, lo:hi] + bias[0][:, lo:hi], 1.0).astype(BF)
            key = turn(projected[:, wide + lo : wide + hi] + bias[1][:, lo:hi], 1.0).astype(BF)
            value = (projected[:, 2 * wide + lo : 2 * wide + hi] + bias[2][:, lo:hi]).astype(BF)
            d_out = d_heads[:, lo:hi]
            key_t, value_t = key.T, value.T
            heads_t, query_t, d_keys, d_values = [], [], [], []
            for head in range(2):
                mask = first_half if head == 0 else ~first_half
                only_key = jnp.where(mask, key, jnp.zeros_like(key))
                only_value = jnp.where(mask, value, jnp.zeros_like(value))
                scores = jnp.where(allowed, dot_rt(only_key, query) * scale, -1e30)
                top = jnp.max(scores, axis=0, keepdims=True)
                weights = jnp.exp(scores - top)
                probs = weights * (1.0 / jnp.sum(weights, axis=0, keepdims=True))
                probs_b = probs.astype(BF)
                d_probs = dot_rt(only_value, d_out)
                delta = jnp.sum(probs * d_probs, axis=0, keepdims=True)
                d_scores = (probs * (d_probs - delta)).astype(BF)
                heads_t.append(dot(value_t[head * HD : (head + 1) * HD], probs_b))
                query_t.append(dot(key_t[head * HD : (head + 1) * HD], d_scores))
                d_keys.append(dot(d_scores, query))
                d_values.append(dot(probs_b, d_out))
            heads_ref[:, lo:hi] = jnp.concatenate(heads_t, axis=0).T.astype(BF)
            d_query = turn(jnp.concatenate(query_t, axis=0).T * scale, -1.0)
            d_key = turn(jnp.where(first_half, d_keys[0], d_keys[1]) * scale, -1.0)
            d_value = jnp.where(first_half, d_values[0], d_values[1])
            for p, item in enumerate((d_query, d_key, d_value)):
                proj_ref[:, p * wide + lo : p * wide + hi] = item.astype(BF)
                bias_ref[0:1, p * wide + lo : p * wide + hi] += jnp.sum(item, axis=0, keepdims=True)

    in_specs = (
        [by_row((rows, width)), by_row((rows, width)), by_row((rows, LANES)), by_row((rows, LANES))]
        + [full(lens.shape), full(vec.shape)]
        + [full((half, 3 * wide))] * (1 + 2 * (groups - 1))
        + [full(w_out.shape)]
    )
    outs = [
        ((tok, wide), BF, by_row((rows, wide))),
        ((tok, 3 * wide), BF, by_row((rows, 3 * wide))),
        ((8, 3 * wide), F32, full((8, 3 * wide))),
        ((width, 3 * wide), BF, full((width, 3 * wide))),
    ]
    return kernel_call(body, (groups,), in_specs, outs, (), 0.0)(
        sc, in_attn, branch, cosine, sine, lens, vec, own, *mine, *other, w_out
    )


def back_to_tokens(sc, xs, heads, mlp, d_proj, d_up, stats, vec, w_out, w_qkv, w_up, bias_up, bias_qkv, bias_out):
    groups, n_x = len(xs), len(flat(xs))
    rows, width = xs[0][0].shape
    wide = width // groups
    ff = d_up.shape[1]

    def body(s_ref, *refs):
        x_refs, refs = refs[:n_x], refs[n_x:]
        (
            heads_ref, mlp_ref, proj_ref, d_up_ref, stats_ref, vec_ref, wo_ref, wq_ref, wu_ref,
            up_ref, qkv_ref, out_ref,
        ) = refs[:12]
        own_ref = refs[12]
        piece_refs = refs[13 : 12 + groups]
        grad_ref, x_scr = refs[12 + groups :]
        me = s_ref[0]
        block = pl.program_id(0)
        load_block(block, xs, x_refs, x_scr)

        @pl.when(block == 0)
        def _():
            grad_ref[...] = jnp.zeros_like(grad_ref)
            grad_ref[4:6, :] = out_ref[0:2, :]
            for p in range(3):
                grad_ref[6 + p : 7 + p, part(me * wide, wide)] = qkv_ref[0:1, p * wide : (p + 1) * wide]
            first = me * ff
            grad_ref[pl.ds(9 + first // width, 1), part(lax.rem(me, width // ff) * ff, ff, LANES)] = up_ref[0:1, :]

        normed = (x_scr[...].astype(F32) - stats_ref[:, 0:1]) * stats_ref[:, 1:2]
        branch_out = dot(heads_ref[...], wo_ref[...]) + mlp_ref[...].astype(F32)
        total = None
        for row, left, right in ((0, proj_ref, wq_ref), (2, d_up_ref, wu_ref)):
            d_in = dot_rt(left[...], right[...])
            grad_ref[row : row + 1, :] += jnp.sum(d_in * normed, axis=0, keepdims=True)
            grad_ref[row + 1 : row + 2, :] += jnp.sum(d_in, axis=0, keepdims=True)
            term = d_in * vec_ref[row : row + 1, :]
            total = term if total is None else total + term

        @pl.when(block == 0)
        def _():
            own_ref[:, :width] = branch_out.astype(BF)
            own_ref[:, width:] = total.astype(BF)

        for step in range(1, groups):

            @pl.when(block == step)
            def _(step=step):
                piece_refs[step - 1][:, :width] = branch_out.astype(BF)
                piece_refs[step - 1][:, width:] = total.astype(BF)

    constant = [vec, w_out, w_qkv, w_up, bias_up, bias_qkv, bias_out]
    in_specs = (
        [full(item.shape) for item in flat(xs)]
        + [by_row((rows, item.shape[1])) for item in (heads, mlp, d_proj, d_up, stats)]
        + [full(item.shape) for item in constant]
    )
    outs = [((rows, 2 * width), BF, full((rows, 2 * width)))]
    outs += [((rows, 2 * width), BF, full((rows, 2 * width)))] * (groups - 1)
    outs += [((EXTRA, width), F32, full((EXTRA, width)))]
    got = kernel_call(
        body,
        (groups,),
        in_specs,
        outs,
        [pltpu.VMEM((rows, width), BF)],
        0.0,
    )(sc, *flat(xs), heads, mlp, d_proj, d_up, stats, *constant)
    return got[0], got[1:groups], got[groups]


def grads_of_attention(sc, in_attn, d_proj, heads, branch, scale, groups):
    tok, width = in_attn.shape
    wide = heads.shape[1]
    half = wide // 2

    def body(s_ref, a_ref, proj_ref, heads_ref, branch_ref, out_away, out_keep, qkv_away, qkv_keep):
        me, core = s_ref[0], s_ref[1]

        def piece(i, carry):
            grad = (dot_lt(a_ref[:, part((me ^ i) * wide, wide)], proj_ref[...]) * scale).astype(BF)
            qkv_keep[i], qkv_away[i] = halves(grad, core)
            return carry

        lax.fori_loop(0, groups, piece, 0)
        grad = (dot_lt(heads_ref[...], branch_ref[...]) * scale).astype(BF)
        out_keep[...], out_away[...] = halves(grad, core)

    ops = (in_attn, d_proj, heads, branch)
    out = ((half, width), BF, full(None))
    qkv = ((groups, half, 3 * wide), BF, full(None))
    return kernel_call(body, (1,), [full(None)] * len(ops), [out, out, qkv, qkv], (), 0.0)(sc, *ops)


def merge(sc, qkv_keep, qkv_got):
    groups, half, columns = qkv_keep.shape

    def body(s_ref, keep_ref, got_ref, stay_ref, away_ref):
        for i in range(groups):
            ref, at = (away_ref if i % 2 else stay_ref), i // 2 * half
            ref[at : at + half, :] = keep_ref[i] + got_ref[i]

    shape = jax.ShapeDtypeStruct((groups // 2 * half, columns), BF)
    return on_vmem(body, [shape, shape], sc, [qkv_keep, qkv_got])


def join(sc, qkv_rows, out_keep, out_got, vec_sum):
    groups = len(qkv_rows)
    half, width = out_keep.shape
    wide = 2 * half
    share = width // groups

    def body(s_ref, *refs):
        rows, (keep_ref, got_ref, vec_ref, out) = refs[:groups], refs[groups:]
        out[groups * half :, :] = jnp.zeros((EXTRA, 3 * wide + share), BF)
        for i in range(groups):
            at = slice(i * half, (i + 1) * half)
            columns = slice(i * share, (i + 1) * share)
            out[at, : 3 * wide] = rows[i][...]
            out[at, 3 * wide :] = keep_ref[:, columns] + got_ref[:, columns]
        out[groups * half :, :wide] = vec_ref[:, part(s_ref[0] * wide, wide)].astype(BF)

    shape = jax.ShapeDtypeStruct((groups * half + EXTRA, 3 * wide + share), BF)
    return on_vmem(body, [shape], sc, [*qkv_rows, out_keep, out_got, vec_sum])[0]


def sum_along(value, axis):
    size = lax.axis_size(axis)
    bit = 1
    while bit < size:
        value = value + lax.ppermute(value, axis, [(i, i ^ bit) for i in range(size)])
        bit *= 2
    return value


def finish(sc, own, got, left, right, tokens, cotangent, lens, stats, vec, slots):
    rows, width = tokens.shape

    def body(s_ref, own_ref, *refs):
        count = len(got) + 2 * len(left)
        got_refs, left_refs, right_refs = refs[: len(got)], refs[len(got) : len(got) + len(left)], refs[len(got) + len(left) : count]
        tok_ref, cot_ref, lens_ref, stats_ref, vec_ref, out_ref, grad_ref = refs[count:]
        branch = own_ref[:, :width].astype(F32)
        scaled = own_ref[:, width:].astype(F32)
        for ref in got_refs:
            branch = branch + ref[:, :width].astype(F32)
            scaled = scaled + ref[:, width:].astype(F32)
        for ref in left_refs:
            branch = branch + ref[...].astype(F32)
        for ref in right_refs:
            scaled = scaled + ref[...].astype(F32)
        size = branch.shape[0]
        _, ends = ends_of(lens_ref, 0, slots)
        index = index_of((size, 1), 0) + (pl.program_id(0) * size).astype(F32)
        valid = jnp.where(index < jnp.broadcast_to(ends[-1], (size, 1)), 1.0, 0.0)
        x = tok_ref[...].astype(F32)
        out_ref[...] = (x + valid * (branch + vec_ref[4:5, :] + vec_ref[5:6, :])).astype(BF)
        inv = stats_ref[:, 1:2]
        normed = (x - stats_ref[:, 0:1]) * inv
        d_tokens = inv * (
            scaled
            - jnp.mean(scaled, axis=1, keepdims=True)
            - normed * jnp.mean(scaled * normed, axis=1, keepdims=True)
        )
        grad_ref[...] = (cot_ref[...].astype(F32) + d_tokens).astype(BF)

    size = rows // 2
    in_specs = [by_row((size, 2 * width))] * (1 + len(got)) + [by_row((size, width))] * (2 * len(left) + 2)
    in_specs += [full(lens.shape), by_row((size, LANES)), full(vec.shape)]
    out = ((rows, width), BF, by_row((size, width)))
    return kernel_call(body, (2,), in_specs, [out, out], (), 2.4)(
        sc, own, *got, *left, *right, tokens, cotangent, lens, stats, vec
    )


def assemble(shapes, arrays, plan):
    def body(*refs):
        ins, outs = refs[: len(arrays)], refs[len(arrays) :]
        me, core = lax.axis_index("shard"), lax.rem(lax.axis_index("dp"), 2)
        for target, row, column, size, which, index in plan(me, core):
            outs[target][part(row, size[0]), part(column, size[1])] = ins[which][index]

    vmem = pl.BlockSpec(memory_space=pltpu.VMEM)
    return pl.pallas_call(
        body,
        out_shape=[jax.ShapeDtypeStruct(shape, arrays[0].dtype) for shape in shapes],
        in_specs=[vmem] * len(arrays),
        out_specs=[vmem] * len(shapes),
        compiler_params=pltpu.CompilerParams(vmem_limit_bytes=8 * MIB),
        cost_estimate=pl.CostEstimate(flops=0, bytes_accessed=int(3.2e6), transcendentals=0),
    )(*arrays)


def adam_blocks(sc, grads, masters, grid, block, where, fill, time):
    shape = masters[0].shape

    def body(s_ref, *refs):
        grad_refs = refs[: len(grads)]
        w_ref, m_ref, v_ref, g_out, w_out, m_out, v_out = refs[len(grads) :]
        fill(s_ref, grad_refs, g_out)
        w_out[...], m_out[...], v_out[...] = adam_terms(
            w_ref[...], m_ref[...], v_ref[...], g_out[...], DECAY_RATE, LEARN_RATE
        )

    spec = pl.BlockSpec(block, where)
    return kernel_call(
        body, grid, [full(None)] * len(grads) + [spec] * 3, [(shape, F32, spec)] * 4, (), time, 30
    )(sc, *grads, *masters)


def choose(condition, yes, no, out):
    @pl.when(condition)
    def _():
        out[...] = yes().astype(F32)

    @pl.when(jnp.logical_not(condition))
    def _():
        out[...] = no().astype(F32)


def adam(masters, grad, decay=DECAY_RATE, rate=LEARN_RATE):
    weight, first, second = masters
    grad = grad.astype(F32)
    return (grad,) + adam_terms(weight, first, second, grad, decay, rate)


def local(
    tokens, cotangent, lengths,
    w_qkv, w_out, w_up, w_down, vectors,
    m_qkv, m_out, m_up, m_down, m_vectors,
    v_qkv, v_out, v_up, v_down, v_vectors,
):
    groups = lax.axis_size("shard")
    me = lax.axis_index("shard")
    core = lax.axis_index("dp") % 2
    rows, width = tokens.shape
    hidden = w_up.shape[1]
    wide = width // groups
    half = wide // 2
    ff = hidden // groups
    n_vec = vectors.shape[0]
    slots = lengths.shape[1]
    others = range(1, groups)
    quarter = wide // 4
    places = lax.axis_size("dp") // 2
    place = lax.axis_index("dp") // 2
    outer = (place == 0) | (place == places - 1)
    sc = jnp.stack([me, core, outer, place % 2]).astype(jnp.int32)
    scale = float(rows * groups * lax.axis_size("dp")) ** (-0.5)

    size = ff // 2
    fence = lax.optimization_barrier

    up_parts, qkv_parts, down_w, out_w = pack(groups, sc, w_up, w_qkv, w_down, w_out, vectors, lengths)
    near = [shard_swap(tokens, step) for step in (1, 2)]
    up_mine = [shard_swap(item, step) for item, step in zip(up_parts[1:], others, strict=True)]
    near, up_mine[0], qkv_parts = fence((near, up_mine[0], qkv_parts))
    xs = gather_rest(tokens, near)
    cot_near = [shard_swap(after(cotangent, xs[3]), step) for step in (1, 2)]
    up_stack = jnp.concatenate([item[:quarter] for item in up_mine])
    up_side = place_send(up_stack, [(i, i ^ 1) for i in range(places)])
    up_other = [up_side, core_swap(up_stack), core_swap(up_side)]
    in_attn, in_mlp, act, slope, stats, up_w, vec, lens = forward_up(
        sc, xs, up_parts[0], up_mine, up_other, vectors, lengths
    )
    cot_near, act = fence((cot_near, act))
    cots = gather_rest(cotangent, cot_near)
    qkv_mine = [shard_swap(item, step) for item, step in zip(after(qkv_parts[1:], cot_near), others, strict=True)]
    cots, act = fence((cots, act))

    branch, bias_out, up_away, up_keep, d_up, bias_up = backward_up(
        sc, cots, lens, slots, slope, down_w, in_mlp, scale
    )
    up_away, up_keep, qkv_mine, branch = fence((up_away, up_keep, qkv_mine, branch))
    up_got = core_swap(up_away)
    qkv_other = [core_swap(item) for item in qkv_mine]
    down_away, down_keep = grad_of_down(sc, branch, act, scale)
    down_away, down_keep, up_got, qkv_other = fence((down_away, down_keep, up_got, qkv_other))
    down_got = core_swap(down_away)
    cosine, sine = tables(sc, after(lens, down_away), groups, rows, slots)
    down = down_keep + down_got
    down, branch_a, up_got, cosine = fence((down, branch, up_got, cosine))

    down, _, _ = dp_round(sc, down, None, None)
    up_sums = [up_keep[i] + up_got[i] for i in range(groups)]
    up_sums, branch_a = fence((up_sums, branch_a))
    up_rows = [up_sums[0]] + [shard_swap(up_sums[step], step) for step in others]
    heads, d_proj, bias_qkv, qkv_w = attention(
        sc, in_attn, branch_a, cosine, sine, lens, vec, qkv_parts[0], qkv_mine, qkv_other, out_w, groups, slots
    )
    out_away, out_keep, qkv_away, qkv_keep = grads_of_attention(sc, in_attn, d_proj, heads, branch, scale, groups)
    up_rows, out_away, qkv_away = fence((up_rows, out_away, qkv_away))
    qkv_got = core_swap(qkv_away)
    out_got = core_swap(out_away)
    mlp = feed_out(sc, after(act, out_away), down_w, groups)
    down, up_rows, qkv_got, out_got, d_proj, mlp = fence((down, up_rows, qkv_got, out_got, d_proj, mlp))
    up = jnp.concatenate(up_rows + [jnp.zeros((EXTRA, ff), BF)])
    stay, away = merge(sc, qkv_keep, qkv_got)
    up, down, stay, away, d_proj = fence((up, down, stay, away, d_proj))

    qkv_rows = exchange(stay, away)
    own, pieces, vec_grad = back_to_tokens(
        sc, xs, heads, mlp, d_proj, d_up, stats, vec, out_w, qkv_w, up_w, bias_up, bias_qkv, bias_out
    )
    vec_sum = sum_along(vec_grad * scale, "shard")
    rest = join(sc, qkv_rows, out_keep, out_got, vec_sum)
    up, down, _ = dp_round(sc, up, down, None, rest)
    down, up, rest, pieces = fence((down, up, rest, pieces))

    rest, up, down = dp_round(sc, rest, up, down, rows=size)
    got = [shard_swap(item, step) for item, step in zip(pieces[:2], (1, 2), strict=True)]
    down, up, rest, got, pieces = fence((down, up, rest, got, pieces))

    down_other = core_swap(down)
    _, rest, up = dp_round(sc, None, rest, up)
    left = [shard_swap(item[:, :width], step) for item, step in zip(pieces[2:], others[2:], strict=True)]

    def fill_down(s_ref, refs, out):
        step = pl.program_id(0)
        at = part((step % 2) * (size // 2), size // 2)
        choose(step // 2 == s_ref[1], lambda: refs[0][at, :], lambda: refs[1][at, :], out)

    new_down = adam_blocks(
        sc, [down, down_other], (w_down, m_down, v_down),
        (4,), (size // 2, width), lambda i, s: (i, 0), fill_down, 0.0,
    )
    up, rest, new_down, left, pieces = fence((up, rest, new_down, left, pieces))
    right = [shard_swap(item[:, width:], step) for item, step in zip(pieces[2:], others[2:], strict=True)]

    up_other = core_swap(up)
    _, _, rest = dp_round(sc, None, None, rest)

    def fill_up(s_ref, refs, out):
        at = part((s_ref[0] ^ pl.program_id(1)) * half, half)
        choose(pl.program_id(0) == s_ref[1], lambda: refs[0][at, :], lambda: refs[1][at, :], out)

    new_up = adam_blocks(
        sc, [up, up_other], (w_up, m_up, v_up),
        (2, groups), (half, ff), lambda i, j, s: (i, j), fill_up, 0.0,
    )
    output, input_grad = finish(
        sc, own, got, left, after(right, new_up), tokens, cotangent, lens, stats, vec, slots
    )
    rest, new_up, output, input_grad = fence((rest, new_up, output, input_grad))
    rest_other = core_swap(rest)

    def rest_plan(me, core):
        plan = []
        for side in range(2):
            row = (core ^ side) * half
            for step in range(groups):
                at = slice(step * half, (step + 1) * half)
                for p in range(3):
                    columns = slice(p * wide, (p + 1) * wide)
                    plan.append((0, row, p * width + (me ^ step) * wide, (half, wide), side, (at, columns)))
                columns = slice(3 * wide, 4 * wide)
                plan.append((1, row, step * wide, (half, wide), side, (at, columns)))
        return plan

    qkv_grad, out_grad = assemble([(wide, 3 * width), (wide, width)], [rest, rest_other], rest_plan)
    vec_rows = slice(groups * half, groups * half + n_vec)
    vec_total = rest[vec_rows, :wide].astype(F32) + rest_other[vec_rows, :wide].astype(F32)

    news = (
        adam((w_qkv, m_qkv, v_qkv), qkv_grad),
        adam((w_out, m_out, v_out), out_grad),
        new_up,
        new_down,
        adam((vectors, m_vectors, v_vectors), vec_total, 0.0, VECTOR_RATE),
    )
    return (output, input_grad) + tuple(item[kind] for kind in range(4) for item in news)


def solution(mesh):
    by_token = P(("shard", "dp"), None)
    params = (P("shard", None),) * 4 + (P(None, "shard"),)
    return jax.shard_map(
        local,
        mesh=mesh,
        in_specs=(by_token,) * 3 + params * 3,
        out_specs=(by_token,) * 2 + params * 4,
        check_vma=False,
    )
```

```python
import functools
import math

import jax
import jax.numpy as jnp
from jax import lax
from jax.experimental import pallas as pl
from jax.experimental.pallas import tpu as pltpu
from jax.sharding import PartitionSpec as P

H = 16
HD = 64
ROT = 16
ADAM_STEP = 4


EPS_NORM = 1e-05
BETA_ONE = 0.9
BETA_TWO = 0.95
ADAM_EPS = 1e-08
LEARN_RATE = 0.01
VECTOR_RATE = 0.1
DECAY_RATE = 0.1
SQRT_HALF = 0.7071067811865476
INV_ROOT_TWO_PI = 0.3989422804014327

BF = jnp.bfloat16
F32 = jnp.float32
EXTRA = 16
LANES = 128
MIB = 2**20


def dot(left, right):
    return jnp.dot(left, right, preferred_element_type=F32)


def dot_lt(left, right):
    return lax.dot_general(left, right, (((0,), (0,)), ((), ())), preferred_element_type=F32)


def dot_rt(left, right):
    return lax.dot_general(left, right, (((1,), (1,)), ((), ())), preferred_element_type=F32)


def part(start, size, multiple=None):
    return pl.ds(pl.multiple_of(start, multiple or size), size)


def shard_swap(value, step):
    size = lax.axis_size("shard")
    return lax.ppermute(value, "shard", [(i, i ^ step) for i in range(size)])


def exchange(stay, away):
    size = lax.axis_size("shard")
    rows = stay.shape[0] // (size // 2)
    got = shard_swap(away, 1)
    pieces = [(got if step % 2 else stay)[step // 2 * rows : (step // 2 + 1) * rows] for step in range(size)]
    bit = 2
    while bit < size:
        sent = [step for step in range(size) if step & bit]
        got = shard_swap(jnp.concatenate([pieces[step] for step in sent]), bit)
        for i, step in enumerate(sent):
            pieces[step] = got[i * rows : (i + 1) * rows]
        bit *= 2
    return pieces


def core_swap(value):
    size = lax.axis_size("dp")
    return lax.ppermute(value, "dp", [(i, i ^ 1) for i in range(size)])


def chain_stages():
    places = lax.axis_size("dp") // 2
    half = places // 2
    if places == 1:
        return []
    stages = []
    for step in range(half - 1):
        stages.append(([(step, step + 1), (places - 1 - step, places - 2 - step)], None))
    stages.append(([(half - 1, half), (half, half - 1)], None))
    for step in reversed(range(half - 1)):
        stages.append(
            ([(step + 1, step), (places - 2 - step, places - 1 - step)], (step, places - 1 - step))
        )
    return stages


def place_send(value, pairs):
    return lax.ppermute(
        value, "dp", [(2 * a + core, 2 * b + core) for a, b in pairs for core in range(2)]
    )


def after(value, *earlier):
    return lax.optimization_barrier((value, earlier))[0]


def combine(items):
    def body(flag_ref, *refs):
        count = len(items)
        for i, (_, _, taker) in enumerate(items):
            value, got, out = refs[2 * i], refs[2 * i + 1], refs[2 * count + i]
            if taker is None:
                out[...] = value[...] + got[...]
            else:
                out[...] = jnp.where(flag_ref[i] > 0, got[...], value[...])

    flags = [jnp.int32(0) if taker is None else taker.astype(jnp.int32) for _, _, taker in items]
    vmem = pl.BlockSpec(memory_space=pltpu.VMEM)
    return pl.pallas_call(
        body,
        out_shape=[jax.ShapeDtypeStruct(value.shape, value.dtype) for value, _, _ in items],
        in_specs=[pl.BlockSpec(memory_space=pltpu.SMEM)] + [vmem] * (2 * len(items)),
        out_specs=[vmem] * len(items),
        compiler_params=pltpu.CompilerParams(vmem_limit_bytes=12 * MIB),
        cost_estimate=pl.CostEstimate(flops=0, bytes_accessed=int(3.2e6), transcendentals=0),
    )(jnp.stack(flags), *[item for value, got, _ in items for item in (value, got)])


def advance(*moves):
    values = [value for value, _ in moves]
    depth = max(len(stages) for _, stages in moves)
    for step in range(depth):
        active = [i for i, (_, stages) in enumerate(moves) if step < len(stages)]
        items = []
        for i in active:
            pairs, takers = moves[i][1][step]
            flag = None
            if takers is not None:
                place = lax.axis_index("dp") // 2
                flag = functools.reduce(jnp.logical_or, [place == taker for taker in takers])
            items.append((values[i], place_send(values[i], pairs), flag))
        for i, item in zip(active, combine(items), strict=True):
            values[i] = item
    return values


def chain_parts():
    stages = chain_stages()
    half = (len(stages) + 1) // 2
    if not stages:
        return [], [], []
    return stages[: half - 1], stages[half - 1 : half], stages[half:]


def dp_round(sc, fresh, inner, total, upcoming=None, rows=None):
    parts = chain_parts()
    if lax.axis_size("dp") // 2 != 4:
        moves = [(value, stages) for value, stages in zip((fresh, inner, total), parts, strict=True) if value is not None]
        moved = iter(advance(*moves))
        return [None if value is None else next(moved) for value in (fresh, inner, total)]
    if fresh is None:
        sent, pairs = total, [(1, 0), (2, 3)]
    elif total is None:
        sent, pairs = fresh, [(0, 1), (3, 2)]
    else:
        sent, pairs = total, [(0, 1), (1, 0), (2, 3), (3, 2)]
    edge = place_send(sent, pairs)
    centre = None if inner is None else place_send(inner, [(1, 2), (2, 1)])
    arrays, shapes, steps = [], [], []

    def plan(kind, items, shape):
        steps.append((kind, len(arrays), len(shapes)))
        arrays.extend(items)
        shapes.append(shape)

    if fresh is not None:
        plan("sum", [fresh, edge], fresh)
    if inner is not None and upcoming is None:
        plan("sum", [inner, centre], inner)
    if inner is not None and upcoming is not None:
        plan("next", [inner, centre, upcoming], max(inner, upcoming, key=lambda item: item.shape[0]))
    if total is not None:
        shape = total if rows is None else jax.ShapeDtypeStruct((rows, total.shape[1]), total.dtype)
        plan("last", [total, edge], shape)

    def body(s_ref, *refs):
        outs = refs[len(arrays) :]
        for kind, at, place in steps:
            value, got, out = refs[at], refs[at + 1], outs[place]
            size = min(value.shape[0], out.shape[0])
            if kind == "sum":
                out[...] = value[...] + got[:size, :]
                continue

            @pl.when(s_ref[2] == 0)
            def _(kind=kind, value=value, got=got, out=out, size=size):
                out[:size, :] = value[:size, :] + got[:size, :] if kind == "next" else value[:size, :]

            @pl.when(s_ref[2] > 0)
            def _(kind=kind, got=got, out=out, at=at, size=size):
                if kind == "next":
                    out[: refs[at + 2].shape[0], :] = refs[at + 2][...]
                else:
                    out[...] = got[:size, :]

    moved = iter(on_vmem(body, shapes, sc, arrays))
    return [None if value is None else next(moved) for value in (fresh, inner, total)]


def on_vmem(body, shapes, sc, arrays, limit=8):
    vmem = pl.BlockSpec(memory_space=pltpu.VMEM)
    return pl.pallas_call(
        body,
        out_shape=[jax.ShapeDtypeStruct(item.shape, item.dtype) for item in shapes],
        in_specs=[pl.BlockSpec(memory_space=pltpu.SMEM)] + [vmem] * len(arrays),
        out_specs=[vmem] * len(shapes),
        compiler_params=pltpu.CompilerParams(vmem_limit_bytes=limit * MIB),
        cost_estimate=pl.CostEstimate(flops=0, bytes_accessed=int(3.2e6), transcendentals=0),
    )(sc, *arrays)


def gather_rest(block, near):
    groups = lax.axis_size("shard")
    rows = block.shape[0]
    got = [[block], [near[0]], [near[1]]]
    got.append([shard_swap(near[0][: rows // 2], 2), shard_swap(near[1][rows // 2 :], 1)])
    for step in range(4, groups):
        got.append([shard_swap(block, step)])
    return got


def whole():
    return pl.BlockSpec(memory_space=pltpu.VMEM)


def full(shape):
    return pl.BlockSpec(memory_space=pltpu.VMEM)


def by_row(shape):
    return pl.BlockSpec(shape, lambda i, *_: (i,) + (0,) * (len(shape) - 1))


def kernel_call(body, grid, in_specs, outs, scratch=(), time=1.0, limit=12):
    return pl.pallas_call(
        body,
        out_shape=[jax.ShapeDtypeStruct(shape, dtype) for shape, dtype, _ in outs],
        grid_spec=pltpu.PrefetchScalarGridSpec(
            num_scalar_prefetch=1,
            grid=grid,
            in_specs=in_specs,
            out_specs=[spec for _, _, spec in outs],
            scratch_shapes=list(scratch),
        ),
        compiler_params=pltpu.CompilerParams(vmem_limit_bytes=limit * MIB),
        cost_estimate=pl.CostEstimate(flops=0, bytes_accessed=int(3.2e6 * time), transcendentals=0),
    )


def flat(blocks):
    return [piece for block in blocks for piece in block]


def load_block(block, blocks, refs, scratch):
    at = 0
    for step, pieces in enumerate(blocks):
        mine = refs[at : at + len(pieces)]
        at += len(pieces)

        @pl.when(block == step)
        def _(mine=mine):
            row = 0
            for ref in mine:
                scratch[row : row + ref.shape[0], :] = ref[...]
                row += ref.shape[0]


def halves(value, core):
    size = value.shape[0] // 2
    first, second = value[:size], value[size:]
    return jnp.where(core == 0, first, second), jnp.where(core == 0, second, first)


def ends_of(lens_ref, block, slots):
    lengths = [lens_ref[block, 0:1, k : k + 1] for k in range(slots)]
    ends = []
    for item in lengths:
        ends.append(item if not ends else ends[-1] + item)
    return lengths, ends


def segments(index, ends):
    total = jnp.zeros(index.shape, F32)
    for end in ends:
        total = total + jnp.where(jnp.broadcast_to(end, index.shape) <= index, 1.0, 0.0)
    return total


def index_of(shape, axis):
    return lax.broadcasted_iota(jnp.int32, shape, axis).astype(F32)


def gelu_parts(values):
    gate = 0.5 * (1.0 + lax.erf(values * SQRT_HALF))
    slope = gate + values * jnp.exp(-0.5 * values * values) * INV_ROOT_TWO_PI
    return values * gate, slope


def adam_terms(weight, first, second, grad, decay, rate):
    corr_one = 1.0 - math.exp(ADAM_STEP * math.log(BETA_ONE))
    corr_two = 1.0 - math.exp(ADAM_STEP * math.log(BETA_TWO))
    first_new = BETA_ONE * first + (1.0 - BETA_ONE) * grad
    second_new = BETA_TWO * second + (1.0 - BETA_TWO) * grad * grad
    step_size = (first_new * (1.0 / corr_one)) / (jnp.sqrt(second_new * (1.0 / corr_two)) + ADAM_EPS)
    return weight - rate * (step_size + decay * weight), first_new, second_new


def pack(groups, sc, w_up, w_qkv, w_down, w_out, vectors, lengths):
    wide, hidden = w_up.shape
    half, quarter, ff = wide // 2, wide // 4, hidden // groups
    n_vec, slots = vectors.shape[0], lengths.shape[1]

    def body(s_ref, up_hbm, qkv_hbm, down_hbm, out_hbm, vec_ref, len_ref, *refs):
        out, (down_out, out_out) = refs[: 2 * groups], refs[2 * groups : 2 * groups + 2]
        up_scr, qkv_scr, down_scr, out_scr, sems, more = refs[2 * groups + 2 :]
        me, core = s_ref[0], s_ref[1]
        rest = [
            pltpu.make_async_copy(down_hbm, down_scr, more.at[0]),
            pltpu.make_async_copy(out_hbm, out_scr, more.at[1]),
        ]
        copies = []
        for step in range(groups):
            size = wide if step == 0 else quarter
            rows = pl.ds(0, wide) if step == 0 else part((2 * s_ref[3] + core) * quarter, quarter)
            owner = me ^ step
            at = pl.ds(0 if step == 0 else wide + (step - 1) * quarter, size)
            mine = [pltpu.make_async_copy(up_hbm.at[rows, part(owner * ff, ff)], up_scr.at[at], sems.at[step, 0])]
            size = wide if step == 0 else half
            rows = pl.ds(0, wide) if step == 0 else part(core * half, half)
            at = pl.ds(0 if step == 0 else wide + (step - 1) * half, size)
            for p in range(3):
                mine.append(
                    pltpu.make_async_copy(
                        qkv_hbm.at[rows, part(p * groups * wide + owner * wide, wide)],
                        qkv_scr.at[at, pl.ds(p * wide, wide)],
                        sems.at[step, 1 + p],
                    )
                )
            copies.append(mine)
        order = list(range(1, groups)) + [0]
        for step in order:
            for copy in copies[step]:
                copy.start()
        for copy in rest:
            copy.start()
        for step in order:
            for copy in copies[step]:
                copy.wait()
            up_out, qkv_out = out[2 * step], out[2 * step + 1]
            if step == 0:
                up_out[...] = up_scr[:wide].astype(BF)
                qkv_out[...] = qkv_scr[:wide].astype(BF)
                continue
            at = wide + (step - 1) * quarter
            up_out[:quarter, :] = up_scr[at : at + quarter].astype(BF)
            up_out[quarter:, :] = jnp.zeros((EXTRA, ff), BF)
            up_out[quarter : quarter + n_vec, :wide] = vec_ref[...].astype(BF)
            up_out[quarter + n_vec : quarter + n_vec + 1, :slots] = len_ref[...].astype(F32).astype(BF)
            at = wide + (step - 1) * half
            qkv_out[...] = qkv_scr[at : at + half].astype(BF)
        for copy in rest:
            copy.wait()
        down_out[...] = down_scr[...].astype(BF)
        out_out[...] = out_scr[...].astype(BF)

    in_specs = [pl.BlockSpec(memory_space=pltpu.HBM)] * 4 + [full(vectors.shape), full(lengths.shape)]
    outs = []
    for step in range(groups):
        size = wide if step == 0 else half
        outs.append(((wide if step == 0 else quarter + EXTRA, ff), BF, full(None)))
        outs.append(((size, 3 * wide), BF, full(None)))
    outs += [(w_down.shape, BF, full(None)), (w_out.shape, BF, full(None))]
    rows = wide + (groups - 1) * half
    scratch = [pltpu.VMEM((wide + (groups - 1) * quarter, ff), F32), pltpu.VMEM((rows, 3 * wide), F32)]
    scratch += [pltpu.VMEM(w_down.shape, F32), pltpu.VMEM(w_out.shape, F32)]
    scratch += [pltpu.SemaphoreType.DMA((groups, 4)), pltpu.SemaphoreType.DMA((2,))]
    got = kernel_call(body, (1,), in_specs, outs, scratch, 7.0, 60)(sc, w_up, w_qkv, w_down, w_out, vectors, lengths)
    return got[0 : 2 * groups : 2], got[1 : 2 * groups : 2], got[2 * groups], got[2 * groups + 1]


def tables(sc, lens, groups, rows, slots):
    def body(s_ref, lens_ref, cos_ref, sin_ref):
        lane = lax.broadcasted_iota(jnp.int32, (8, LANES), 1) % HD
        pair = (lane % (ROT // 2)).astype(F32)
        freq = jnp.where(lane < ROT, jnp.exp(-pair * (2.0 * math.log(10000.0) / ROT)), 0.0)[0:1, :]
        index = index_of((rows, LANES), 0)
        angle = index * freq
        cos_index, sin_index = jnp.cos(angle), jnp.sin(angle)
        for block in range(groups):
            lengths, ends = ends_of(lens_ref, block, slots)
            cos_start = jnp.ones((rows, LANES), F32)
            sin_start = jnp.zeros((rows, LANES), F32)
            for length, end in zip(lengths, ends, strict=True):
                turn = jnp.broadcast_to(end, (8, LANES)) * jnp.broadcast_to(freq, (8, LANES))
                inside = jnp.broadcast_to(end, index.shape) <= index
                cos_start = jnp.where(inside, jnp.cos(turn)[0:1, :], cos_start)
                sin_start = jnp.where(inside, jnp.sin(turn)[0:1, :], sin_start)
            at = slice(block * rows, (block + 1) * rows)
            cos_ref[at, :] = cos_index * cos_start + sin_index * sin_start
            sin_ref[at, :] = sin_index * cos_start - cos_index * sin_start

    out = ((groups * rows, LANES), F32, full(None))
    return kernel_call(body, (1,), [full(lens.shape)], [out, out], (), 1.5)(sc, lens)


def forward_up(sc, xs, own, mine, other, vectors, lengths):
    groups, n_x = len(xs), len(flat(xs))
    rows, width = xs[0][0].shape
    wide, ff = own.shape
    quarter = wide // 4
    n_vec, slots = vectors.shape[0], lengths.shape[1]
    tok = groups * rows

    def body(s_ref, *refs):
        x_refs, refs = refs[:n_x], refs[n_x:]
        own_ref = refs[0]
        mine_refs = refs[1:groups]
        other_refs = refs[groups : groups + 3]
        vec_in, len_in = refs[groups + 3 : groups + 5]
        attn_ref, mlp_ref, act_ref, slope_ref, stats_ref, w_ref, vec_ref, lens_ref, x_scr = refs[groups + 5 :]
        me, core, side = s_ref[0], s_ref[1], s_ref[3]
        block = pl.program_id(0)

        @pl.when(block == 0)
        def _():
            w_ref[part(me * wide, wide), :] = own_ref[...]
            vec_ref[...] = jnp.zeros_like(vec_ref)
            lens_ref[...] = jnp.zeros_like(lens_ref)
            vec_ref[0:n_vec, part(me * wide, wide)] = vec_in[...].astype(BF).astype(F32)
            lens_ref[0, 0:1, 0:slots] = len_in[...].astype(F32)
            for step in range(1, groups):
                at = (me ^ step) * wide
                w_ref[part(at + (2 * side + core) * quarter, quarter), :] = mine_refs[step - 1][:quarter, :]
                for ref, which in zip(
                    other_refs, (2 * (1 - side) + core, 2 * side + 1 - core, 2 * (1 - side) + 1 - core), strict=True
                ):
                    w_ref[part(at + which * quarter, quarter), :] = ref[(step - 1) * quarter : step * quarter, :]
                vec_ref[0:n_vec, part(at, wide)] = mine_refs[step - 1][quarter : quarter + n_vec, :wide].astype(F32)
                lens_ref[step, 0:1, 0:slots] = mine_refs[step - 1][
                    quarter + n_vec : quarter + n_vec + 1, :slots
                ].astype(F32)

        load_block(block, xs, x_refs, x_scr)
        x = x_scr[...].astype(F32)
        mean = jnp.mean(x, axis=1, keepdims=True)
        centred = x - mean
        inv = lax.rsqrt(jnp.mean(centred * centred, axis=1, keepdims=True) + EPS_NORM)
        normed = centred * inv
        lane = lax.broadcasted_iota(jnp.int32, (rows, LANES), 1)
        stats_ref[...] = jnp.where(lane == 0, mean, inv)
        attn_ref[...] = (normed * vec_ref[0:1, :] + vec_ref[1:2, :]).astype(BF)
        in_mlp = (normed * vec_ref[2:3, :] + vec_ref[3:4, :]).astype(BF)
        mlp_ref[...] = in_mlp
        first = me * ff
        bias = vec_ref[pl.ds(9 + first // width, 1), part(lax.rem(me, width // ff) * ff, ff, LANES)]
        act, slope = gelu_parts(dot(in_mlp, w_ref[...]) + bias)
        act_ref[...] = act.astype(BF)
        slope_ref[...] = slope

    in_specs = (
        [full(item.shape) for item in flat(xs)]
        + [full(own.shape)]
        + [full(None)] * (groups + 2)
        + [full(vectors.shape), full(lengths.shape)]
    )
    outs = [
        ((tok, width), BF, by_row((rows, width))),
        ((tok, width), BF, by_row((rows, width))),
        ((tok, ff), BF, by_row((rows, ff))),
        ((tok, ff), F32, by_row((rows, ff))),
        ((tok, LANES), F32, by_row((rows, LANES))),
        ((width, ff), BF, full((width, ff))),
        ((EXTRA, width), F32, full((EXTRA, width))),
        ((groups, 8, LANES), F32, full((groups, 8, LANES))),
    ]
    return kernel_call(
        body, (groups,), in_specs, outs, [pltpu.VMEM((rows, width), BF)], 6.5, 20
    )(sc, *flat(xs), own, *mine, *other, vectors, lengths)


def grad_of_down(sc, branch, act, scale):
    tok, width = branch.shape
    size = act.shape[1] // 2

    def body(s_ref, branch_ref, act_ref, away_ref, keep_ref):
        core = s_ref[1]
        for ref, which in ((away_ref, 1 - core), (keep_ref, core)):
            ref[...] = (dot_lt(act_ref[:, part(which * size, size)], branch_ref[...]) * scale).astype(BF)

    outs = [((size, width), BF, full(None))] * 2
    return kernel_call(body, (1,), [full(branch.shape), full(act.shape)], outs, (), 3.0)(sc, branch, act)


def feed_out(sc, act, w_down, groups):
    tok, ff = act.shape
    rows = tok // groups

    def body(s_ref, act_ref, wd_ref, out_ref):
        out_ref[...] = dot(act_ref[...], wd_ref[...]).astype(BF)

    width = w_down.shape[1]
    outs = [((tok, width), BF, by_row((rows, width)))]
    return kernel_call(body, (groups,), [by_row((rows, ff)), full(None)], outs, (), 3.0)(sc, act, w_down)[0]


def backward_up(sc, cots, lens, slots, slope, w_down, in_mlp, scale):
    groups, n_c = len(cots), len(flat(cots))
    rows, width = cots[0][0].shape
    tok = groups * rows
    ff = slope.shape[1]
    half = width // groups // 2

    def body(s_ref, *refs):
        cot_refs, refs = refs[:n_c], refs[n_c:]
        lens_ref, slope_ref, wd_ref, mlp_ref, branch_ref, sum_ref, away_ref, keep_ref, up_ref, bias_ref, scratch = refs
        me, core = s_ref[0], s_ref[1]
        block = pl.program_id(0)

        @pl.when(block == 0)
        def _():
            bias_ref[...] = jnp.zeros_like(bias_ref)

        load_block(block, cots, cot_refs, scratch)
        total = jnp.zeros((1, 1), F32)
        for slot in range(slots):
            total = total + lens_ref[block, 0:1, slot : slot + 1]
        valid = jnp.where(index_of((rows, 1), 0) < jnp.broadcast_to(total, (rows, 1)), 1.0, 0.0)
        branch_f = scratch[...].astype(F32) * valid
        branch = branch_f.astype(BF)
        branch_ref[...] = branch

        @pl.when(block == 0)
        def _():
            sum_ref[...] = jnp.broadcast_to(jnp.sum(branch_f, axis=0, keepdims=True), sum_ref.shape)

        d_up = dot_rt(branch, wd_ref[...]) * slope_ref[...]
        bias_ref[0:1, :] += jnp.sum(d_up, axis=0, keepdims=True)
        up_ref[part(block * rows, rows), :] = d_up.astype(BF)

        @pl.when(block == groups - 1)
        def _():
            def pair(i, carry):
                grad = (dot_lt(mlp_ref[:, part(i * (4 * half), 4 * half)], up_ref[...]) * scale).astype(BF)
                for j in range(2):
                    step = me ^ (2 * i + j)
                    keep_ref[step], away_ref[step] = halves(grad[j * 2 * half : (j + 1) * 2 * half], core)
                return carry

            lax.fori_loop(0, groups // 2, pair, 0)

    in_specs = [full(None)] * (n_c + 1) + [by_row((rows, ff)), full(w_down.shape), full(in_mlp.shape)]
    outs = [
        ((tok, width), BF, by_row((rows, width))),
        ((8, width), F32, full(None)),
        ((groups, half, ff), BF, full((groups, half, ff))),
        ((groups, half, ff), BF, full((groups, half, ff))),
        ((tok, ff), BF, full((tok, ff))),
        ((8, ff), F32, full((8, ff))),
    ]
    return kernel_call(body, (groups,), in_specs, outs, [pltpu.VMEM((rows, width), BF)], 6.8)(
        sc, *flat(cots), lens, slope, w_down, in_mlp
    )


def attention(sc, in_attn, branch, cosine, sine, lens, vec, own, mine, other, w_out, groups, slots):
    tok, width = in_attn.shape
    rows = tok // groups
    wide = width // groups
    half = wide // 2
    scale = HD ** (-0.5)

    def body(s_ref, *refs):
        a_ref, branch_ref, cos_ref, sin_ref, lens_ref, vec_ref = refs[:6]
        own_ref = refs[6]
        mine_refs = refs[7 : 6 + groups]
        other_refs = refs[6 + groups : 5 + 2 * groups]
        wo_ref, heads_ref, proj_ref, bias_ref, w_ref = refs[5 + 2 * groups :]
        me, core = s_ref[0], s_ref[1]
        block = pl.program_id(0)

        @pl.when(block == 0)
        def _():
            w_ref[part(me * wide, wide), :] = own_ref[...]
            for step in range(1, groups):
                at = (me ^ step) * wide
                w_ref[part(at + core * half, half), :] = mine_refs[step - 1][...]
                w_ref[part(at + (1 - core) * half, half), :] = other_refs[step - 1][...]
            bias_ref[...] = jnp.zeros_like(bias_ref)

        bias = [vec_ref[6 + p : 7 + p, part(me * wide, wide)] for p in range(3)]
        projected = dot(a_ref[...], w_ref[...])
        d_heads = dot_rt(branch_ref[...], wo_ref[...]).astype(BF)
        _, ends = ends_of(lens_ref, block, slots)
        key_index = index_of((rows, 1), 0)
        query_index = index_of((1, rows), 1)
        allowed = (segments(key_index, ends) == segments(query_index, ends)) & (key_index <= query_index)
        lane = lax.broadcasted_iota(jnp.int32, (rows, LANES), 1)
        cosine, sine = cos_ref[...], sin_ref[...]
        low = jnp.where(lane % HD < ROT // 2, sine, 0.0)
        high = jnp.where(lane % HD >= ROT // 2, sine, 0.0)

        def turn(values, sign):
            ahead = pltpu.roll(values, LANES - ROT // 2, 1)
            behind = pltpu.roll(values, ROT // 2, 1)
            return values * cosine + sign * (behind * high - ahead * low)

        first_half = lane < HD
        for pair in range(wide // LANES):
            lo, hi = pair * LANES, (pair + 1) * LANES
            query = turn(projected[:, lo:hi] + bias[0][:, lo:hi], 1.0).astype(BF)
            key = turn(projected[:, wide + lo : wide + hi] + bias[1][:, lo:hi], 1.0).astype(BF)
            value = (projected[:, 2 * wide + lo : 2 * wide + hi] + bias[2][:, lo:hi]).astype(BF)
            d_out = d_heads[:, lo:hi]
            key_t, value_t = key.T, value.T
            heads_t, query_t, d_keys, d_values = [], [], [], []
            for head in range(2):
                mask = first_half if head == 0 else ~first_half
                only_key = jnp.where(mask, key, jnp.zeros_like(key))
                only_value = jnp.where(mask, value, jnp.zeros_like(value))
                scores = jnp.where(allowed, dot_rt(only_key, query) * scale, -1e30)
                top = jnp.max(scores, axis=0, keepdims=True)
                weights = jnp.exp(scores - top)
                probs = weights * (1.0 / jnp.sum(weights, axis=0, keepdims=True))
                probs_b = probs.astype(BF)
                d_probs = dot_rt(only_value, d_out)
                delta = jnp.sum(probs * d_probs, axis=0, keepdims=True)
                d_scores = (probs * (d_probs - delta)).astype(BF)
                heads_t.append(dot(value_t[head * HD : (head + 1) * HD], probs_b))
                query_t.append(dot(key_t[head * HD : (head + 1) * HD], d_scores))
                d_keys.append(dot(d_scores, query))
                d_values.append(dot(probs_b, d_out))
            heads_ref[:, lo:hi] = jnp.concatenate(heads_t, axis=0).T.astype(BF)
            d_query = turn(jnp.concatenate(query_t, axis=0).T * scale, -1.0)
            d_key = turn(jnp.where(first_half, d_keys[0], d_keys[1]) * scale, -1.0)
            d_value = jnp.where(first_half, d_values[0], d_values[1])
            for p, item in enumerate((d_query, d_key, d_value)):
                proj_ref[:, p * wide + lo : p * wide + hi] = item.astype(BF)
                bias_ref[0:1, p * wide + lo : p * wide + hi] += jnp.sum(item, axis=0, keepdims=True)

    in_specs = (
        [by_row((rows, width)), by_row((rows, width)), by_row((rows, LANES)), by_row((rows, LANES))]
        + [full(lens.shape), full(vec.shape)]
        + [full((half, 3 * wide))] * (1 + 2 * (groups - 1))
        + [full(w_out.shape)]
    )
    outs = [
        ((tok, wide), BF, by_row((rows, wide))),
        ((tok, 3 * wide), BF, by_row((rows, 3 * wide))),
        ((8, 3 * wide), F32, full((8, 3 * wide))),
        ((width, 3 * wide), BF, full((width, 3 * wide))),
    ]
    return kernel_call(body, (groups,), in_specs, outs, (), 0.0)(
        sc, in_attn, branch, cosine, sine, lens, vec, own, *mine, *other, w_out
    )


def back_to_tokens(sc, xs, heads, mlp, d_proj, d_up, stats, vec, w_out, w_qkv, w_up, bias_up, bias_qkv, bias_out):
    groups, n_x = len(xs), len(flat(xs))
    rows, width = xs[0][0].shape
    wide = width // groups
    ff = d_up.shape[1]

    def body(s_ref, *refs):
        x_refs, refs = refs[:n_x], refs[n_x:]
        (
            heads_ref, mlp_ref, proj_ref, d_up_ref, stats_ref, vec_ref, wo_ref, wq_ref, wu_ref,
            up_ref, qkv_ref, out_ref,
        ) = refs[:12]
        own_ref = refs[12]
        piece_refs = refs[13 : 12 + groups]
        grad_ref, x_scr = refs[12 + groups :]
        me = s_ref[0]
        block = pl.program_id(0)
        load_block(block, xs, x_refs, x_scr)

        @pl.when(block == 0)
        def _():
            grad_ref[...] = jnp.zeros_like(grad_ref)
            grad_ref[4:6, :] = out_ref[0:2, :]
            for p in range(3):
                grad_ref[6 + p : 7 + p, part(me * wide, wide)] = qkv_ref[0:1, p * wide : (p + 1) * wide]
            first = me * ff
            grad_ref[pl.ds(9 + first // width, 1), part(lax.rem(me, width // ff) * ff, ff, LANES)] = up_ref[0:1, :]

        normed = (x_scr[...].astype(F32) - stats_ref[:, 0:1]) * stats_ref[:, 1:2]
        branch_out = dot(heads_ref[...], wo_ref[...]) + mlp_ref[...].astype(F32)
        total = None
        for row, left, right in ((0, proj_ref, wq_ref), (2, d_up_ref, wu_ref)):
            d_in = dot_rt(left[...], right[...])
            grad_ref[row : row + 1, :] += jnp.sum(d_in * normed, axis=0, keepdims=True)
            grad_ref[row + 1 : row + 2, :] += jnp.sum(d_in, axis=0, keepdims=True)
            term = d_in * vec_ref[row : row + 1, :]
            total = term if total is None else total + term

        @pl.when(block == 0)
        def _():
            own_ref[:, :width] = branch_out.astype(BF)
            own_ref[:, width:] = total.astype(BF)

        for step in range(1, groups):

            @pl.when(block == step)
            def _(step=step):
                piece_refs[step - 1][:, :width] = branch_out.astype(BF)
                piece_refs[step - 1][:, width:] = total.astype(BF)

    constant = [vec, w_out, w_qkv, w_up, bias_up, bias_qkv, bias_out]
    in_specs = (
        [full(item.shape) for item in flat(xs)]
        + [by_row((rows, item.shape[1])) for item in (heads, mlp, d_proj, d_up, stats)]
        + [full(item.shape) for item in constant]
    )
    outs = [((rows, 2 * width), BF, full((rows, 2 * width)))]
    outs += [((rows, 2 * width), BF, full((rows, 2 * width)))] * (groups - 1)
    outs += [((EXTRA, width), F32, full((EXTRA, width)))]
    got = kernel_call(
        body,
        (groups,),
        in_specs,
        outs,
        [pltpu.VMEM((rows, width), BF)],
        0.0,
    )(sc, *flat(xs), heads, mlp, d_proj, d_up, stats, *constant)
    return got[0], got[1:groups], got[groups]


def grads_of_attention(sc, in_attn, d_proj, heads, branch, scale, groups):
    tok, width = in_attn.shape
    wide = heads.shape[1]
    half = wide // 2

    def body(s_ref, a_ref, proj_ref, heads_ref, branch_ref, out_away, out_keep, qkv_away, qkv_keep):
        me, core = s_ref[0], s_ref[1]

        def pair(i, carry):
            grad = (dot_lt(a_ref[:, part(i * (2 * wide), 2 * wide)], proj_ref[...]) * scale).astype(BF)
            for j in range(2):
                step = me ^ (2 * i + j)
                qkv_keep[step], qkv_away[step] = halves(grad[j * wide : (j + 1) * wide], core)
            return carry

        lax.fori_loop(0, groups // 2, pair, 0)
        grad = (dot_lt(heads_ref[...], branch_ref[...]) * scale).astype(BF)
        out_keep[...], out_away[...] = halves(grad, core)

    ops = (in_attn, d_proj, heads, branch)
    out = ((half, width), BF, full(None))
    qkv = ((groups, half, 3 * wide), BF, full(None))
    return kernel_call(body, (1,), [full(None)] * len(ops), [out, out, qkv, qkv], (), 0.0)(sc, *ops)


def merge(sc, qkv_keep, qkv_got):
    groups, half, columns = qkv_keep.shape

    def body(s_ref, keep_ref, got_ref, stay_ref, away_ref):
        for i in range(groups):
            ref, at = (away_ref if i % 2 else stay_ref), i // 2 * half
            ref[at : at + half, :] = keep_ref[i] + got_ref[i]

    shape = jax.ShapeDtypeStruct((groups // 2 * half, columns), BF)
    return on_vmem(body, [shape, shape], sc, [qkv_keep, qkv_got])


def join(sc, qkv_rows, out_keep, out_got, vec_sum):
    groups = len(qkv_rows)
    half, width = out_keep.shape
    wide = 2 * half
    share = width // groups

    def body(s_ref, *refs):
        rows, (keep_ref, got_ref, vec_ref, out) = refs[:groups], refs[groups:]
        out[groups * half :, :] = jnp.zeros((EXTRA, 3 * wide + share), BF)
        for i in range(groups):
            at = slice(i * half, (i + 1) * half)
            columns = slice(i * share, (i + 1) * share)
            out[at, : 3 * wide] = rows[i][...]
            out[at, 3 * wide :] = keep_ref[:, columns] + got_ref[:, columns]
        out[groups * half :, :wide] = vec_ref[:, part(s_ref[0] * wide, wide)].astype(BF)

    shape = jax.ShapeDtypeStruct((groups * half + EXTRA, 3 * wide + share), BF)
    return on_vmem(body, [shape], sc, [*qkv_rows, out_keep, out_got, vec_sum])[0]


def sum_along(value, axis):
    size = lax.axis_size(axis)
    bit = 1
    while bit < size:
        value = value + lax.ppermute(value, axis, [(i, i ^ bit) for i in range(size)])
        bit *= 2
    return value


def finish(sc, own, got, left, right, tokens, cotangent, lens, stats, vec, slots):
    rows, width = tokens.shape

    def body(s_ref, own_ref, *refs):
        count = len(got) + 2 * len(left)
        got_refs, left_refs, right_refs = refs[: len(got)], refs[len(got) : len(got) + len(left)], refs[len(got) + len(left) : count]
        tok_ref, cot_ref, lens_ref, stats_ref, vec_ref, out_ref, grad_ref = refs[count:]
        branch = own_ref[:, :width].astype(F32)
        scaled = own_ref[:, width:].astype(F32)
        for ref in got_refs:
            branch = branch + ref[:, :width].astype(F32)
            scaled = scaled + ref[:, width:].astype(F32)
        for ref in left_refs:
            branch = branch + ref[...].astype(F32)
        for ref in right_refs:
            scaled = scaled + ref[...].astype(F32)
        size = branch.shape[0]
        _, ends = ends_of(lens_ref, 0, slots)
        index = index_of((size, 1), 0) + (pl.program_id(0) * size).astype(F32)
        valid = jnp.where(index < jnp.broadcast_to(ends[-1], (size, 1)), 1.0, 0.0)
        x = tok_ref[...].astype(F32)
        out_ref[...] = (x + valid * (branch + vec_ref[4:5, :] + vec_ref[5:6, :])).astype(BF)
        inv = stats_ref[:, 1:2]
        normed = (x - stats_ref[:, 0:1]) * inv
        d_tokens = inv * (
            scaled
            - jnp.mean(scaled, axis=1, keepdims=True)
            - normed * jnp.mean(scaled * normed, axis=1, keepdims=True)
        )
        grad_ref[...] = (cot_ref[...].astype(F32) + d_tokens).astype(BF)

    size = rows // 2
    in_specs = [by_row((size, 2 * width))] * (1 + len(got)) + [by_row((size, width))] * (2 * len(left) + 2)
    in_specs += [full(lens.shape), by_row((size, LANES)), full(vec.shape)]
    out = ((rows, width), BF, by_row((size, width)))
    return kernel_call(body, (2,), in_specs, [out, out], (), 2.4)(
        sc, own, *got, *left, *right, tokens, cotangent, lens, stats, vec
    )


def assemble(shapes, arrays, plan):
    def body(*refs):
        ins, outs = refs[: len(arrays)], refs[len(arrays) :]
        me, core = lax.axis_index("shard"), lax.rem(lax.axis_index("dp"), 2)
        for target, row, column, size, which, index in plan(me, core):
            outs[target][part(row, size[0]), part(column, size[1])] = ins[which][index]

    vmem = pl.BlockSpec(memory_space=pltpu.VMEM)
    return pl.pallas_call(
        body,
        out_shape=[jax.ShapeDtypeStruct(shape, arrays[0].dtype) for shape in shapes],
        in_specs=[vmem] * len(arrays),
        out_specs=[vmem] * len(shapes),
        compiler_params=pltpu.CompilerParams(vmem_limit_bytes=8 * MIB),
        cost_estimate=pl.CostEstimate(flops=0, bytes_accessed=int(3.2e6), transcendentals=0),
    )(*arrays)


def adam_blocks(sc, grads, masters, grid, block, where, fill, time):
    shape = masters[0].shape

    def body(s_ref, *refs):
        grad_refs = refs[: len(grads)]
        w_ref, m_ref, v_ref, g_out, w_out, m_out, v_out = refs[len(grads) :]
        fill(s_ref, grad_refs, g_out)
        w_out[...], m_out[...], v_out[...] = adam_terms(
            w_ref[...], m_ref[...], v_ref[...], g_out[...], DECAY_RATE, LEARN_RATE
        )

    spec = pl.BlockSpec(block, where)
    return kernel_call(
        body, grid, [full(None)] * len(grads) + [spec] * 3, [(shape, F32, spec)] * 4, (), time, 30
    )(sc, *grads, *masters)


def choose(condition, yes, no, out):
    @pl.when(condition)
    def _():
        out[...] = yes().astype(F32)

    @pl.when(jnp.logical_not(condition))
    def _():
        out[...] = no().astype(F32)


def adam(masters, grad, decay=DECAY_RATE, rate=LEARN_RATE):
    weight, first, second = masters
    grad = grad.astype(F32)
    return (grad,) + adam_terms(weight, first, second, grad, decay, rate)


def local(
    tokens, cotangent, lengths,
    w_qkv, w_out, w_up, w_down, vectors,
    m_qkv, m_out, m_up, m_down, m_vectors,
    v_qkv, v_out, v_up, v_down, v_vectors,
):
    groups = lax.axis_size("shard")
    me = lax.axis_index("shard")
    core = lax.axis_index("dp") % 2
    rows, width = tokens.shape
    hidden = w_up.shape[1]
    wide = width // groups
    half = wide // 2
    ff = hidden // groups
    n_vec = vectors.shape[0]
    slots = lengths.shape[1]
    others = range(1, groups)
    quarter = wide // 4
    places = lax.axis_size("dp") // 2
    place = lax.axis_index("dp") // 2
    outer = (place == 0) | (place == places - 1)
    sc = jnp.stack([me, core, outer, place % 2]).astype(jnp.int32)
    scale = float(rows * groups * lax.axis_size("dp")) ** (-0.5)

    size = ff // 2
    fence = lax.optimization_barrier

    up_parts, qkv_parts, down_w, out_w = pack(groups, sc, w_up, w_qkv, w_down, w_out, vectors, lengths)
    near = [shard_swap(tokens, step) for step in (1, 2)]
    up_mine = [shard_swap(item, step) for item, step in zip(up_parts[1:], others, strict=True)]
    near, up_mine[0], qkv_parts = fence((near, up_mine[0], qkv_parts))
    xs = gather_rest(tokens, near)
    cot_near = [shard_swap(after(cotangent, xs[3]), step) for step in (1, 2)]
    up_stack = jnp.concatenate([item[:quarter] for item in up_mine])
    up_side = place_send(up_stack, [(i, i ^ 1) for i in range(places)])
    up_other = [up_side, core_swap(up_stack), core_swap(up_side)]
    in_attn, in_mlp, act, slope, stats, up_w, vec, lens = forward_up(
        sc, xs, up_parts[0], up_mine, up_other, vectors, lengths
    )
    cot_near, act = fence((cot_near, act))
    cots = gather_rest(cotangent, cot_near)
    qkv_mine = [shard_swap(item, step) for item, step in zip(after(qkv_parts[1:], cot_near), others, strict=True)]
    cots, act = fence((cots, act))

    branch, bias_out, up_away, up_keep, d_up, bias_up = backward_up(
        sc, cots, lens, slots, slope, down_w, in_mlp, scale
    )
    up_away, up_keep, qkv_mine, branch = fence((up_away, up_keep, qkv_mine, branch))
    up_got = core_swap(up_away)
    qkv_other = [core_swap(item) for item in qkv_mine]
    down_away, down_keep = grad_of_down(sc, branch, act, scale)
    down_away, down_keep, up_got, qkv_other = fence((down_away, down_keep, up_got, qkv_other))
    down_got = core_swap(down_away)
    cosine, sine = tables(sc, after(lens, down_away), groups, rows, slots)
    down = down_keep + down_got
    down, branch_a, up_got, cosine = fence((down, branch, up_got, cosine))

    down, _, _ = dp_round(sc, down, None, None)
    up_sums = [up_keep[i] + up_got[i] for i in range(groups)]
    up_sums, branch_a = fence((up_sums, branch_a))
    up_rows = [up_sums[0]] + [shard_swap(up_sums[step], step) for step in others]
    heads, d_proj, bias_qkv, qkv_w = attention(
        sc, in_attn, branch_a, cosine, sine, lens, vec, qkv_parts[0], qkv_mine, qkv_other, out_w, groups, slots
    )
    out_away, out_keep, qkv_away, qkv_keep = grads_of_attention(sc, in_attn, d_proj, heads, branch, scale, groups)
    up_rows, out_away, qkv_away = fence((up_rows, out_away, qkv_away))
    qkv_got = core_swap(qkv_away)
    out_got = core_swap(out_away)
    mlp = feed_out(sc, after(act, out_away), down_w, groups)
    down, up_rows, qkv_got, out_got, d_proj, mlp = fence((down, up_rows, qkv_got, out_got, d_proj, mlp))
    up = jnp.concatenate(up_rows + [jnp.zeros((EXTRA, ff), BF)])
    stay, away = merge(sc, qkv_keep, qkv_got)
    up, down, stay, away, d_proj = fence((up, down, stay, away, d_proj))

    qkv_rows = exchange(stay, away)
    own, pieces, vec_grad = back_to_tokens(
        sc, xs, heads, mlp, d_proj, d_up, stats, vec, out_w, qkv_w, up_w, bias_up, bias_qkv, bias_out
    )
    vec_sum = sum_along(vec_grad * scale, "shard")
    rest = join(sc, qkv_rows, out_keep, out_got, vec_sum)
    up, down, _ = dp_round(sc, up, down, None, rest)
    down, up, rest, pieces = fence((down, up, rest, pieces))

    rest, up, down = dp_round(sc, rest, up, down, rows=size)
    got = [shard_swap(item, step) for item, step in zip(pieces[:2], (1, 2), strict=True)]
    down, up, rest, got, pieces = fence((down, up, rest, got, pieces))

    down_other = core_swap(down)
    _, rest, up = dp_round(sc, None, rest, up)
    left = [shard_swap(item[:, :width], step) for item, step in zip(pieces[2:], others[2:], strict=True)]

    def fill_down(s_ref, refs, out):
        step = pl.program_id(0)
        at = part((step % 2) * (size // 2), size // 2)
        choose(step // 2 == s_ref[1], lambda: refs[0][at, :], lambda: refs[1][at, :], out)

    new_down = adam_blocks(
        sc, [down, down_other], (w_down, m_down, v_down),
        (4,), (size // 2, width), lambda i, s: (i, 0), fill_down, 0.0,
    )
    up, rest, new_down, left, pieces = fence((up, rest, new_down, left, pieces))
    right = [shard_swap(item[:, width:], step) for item, step in zip(pieces[2:], others[2:], strict=True)]

    up_other = core_swap(up)
    _, _, rest = dp_round(sc, None, None, rest)

    def fill_up(s_ref, refs, out):
        at = part((s_ref[0] ^ pl.program_id(1)) * half, half)
        choose(pl.program_id(0) == s_ref[1], lambda: refs[0][at, :], lambda: refs[1][at, :], out)

    new_up = adam_blocks(
        sc, [up, up_other], (w_up, m_up, v_up),
        (2, groups), (half, ff), lambda i, j, s: (i, j), fill_up, 0.0,
    )
    output, input_grad = finish(
        sc, own, got, left, after(right, new_up), tokens, cotangent, lens, stats, vec, slots
    )
    rest, new_up, output, input_grad = fence((rest, new_up, output, input_grad))
    rest_other = core_swap(rest)

    def rest_plan(me, core):
        plan = []
        for side in range(2):
            row = (core ^ side) * half
            for step in range(groups):
                at = slice(step * half, (step + 1) * half)
                for p in range(3):
                    columns = slice(p * wide, (p + 1) * wide)
                    plan.append((0, row, p * width + (me ^ step) * wide, (half, wide), side, (at, columns)))
                columns = slice(3 * wide, 4 * wide)
                plan.append((1, row, step * wide, (half, wide), side, (at, columns)))
        return plan

    qkv_grad, out_grad = assemble([(wide, 3 * width), (wide, width)], [rest, rest_other], rest_plan)
    vec_rows = slice(groups * half, groups * half + n_vec)
    vec_total = rest[vec_rows, :wide].astype(F32) + rest_other[vec_rows, :wide].astype(F32)

    news = (
        adam((w_qkv, m_qkv, v_qkv), qkv_grad),
        adam((w_out, m_out, v_out), out_grad),
        new_up,
        new_down,
        adam((vectors, m_vectors, v_vectors), vec_total, 0.0, VECTOR_RATE),
    )
    return (output, input_grad) + tuple(item[kind] for kind in range(4) for item in news)


def solution(mesh):
    by_token = P(("shard", "dp"), None)
    params = (P("shard", None),) * 4 + (P(None, "shard"),)
    return jax.shard_map(
        local,
        mesh=mesh,
        in_specs=(by_token,) * 3 + params * 3,
        out_specs=(by_token,) * 2 + params * 4,
        check_vma=False,
    )
```
